32 devices in a mesh: rows: 16 (over z, y, core), cols: 2 (over x).
Axes of the slice: x: 2, y: 2, z: 4, core: 2. Of those that a mesh axis runs over, the one named last changes fastest.
Arguments:
- features: bfloat16 [16, 256, 256], P('rows', 'cols'), may hold values from -48 to 48
- projection: bfloat16 [256, 512], replicated, may hold values from -1 to 1
- first_kernel: bfloat16 [3, 3, 256, 128], replicated, may hold values from -0.125 to 0.125
- second_kernel: bfloat16 [3, 3, 128, 128], replicated, may hold values from -0.1875 to 0.1875
- cotangent: bfloat16 [16, 256, 128], P('rows', 'cols'), may hold values from -6 to 6
Outputs:
- output_map: bfloat16 [16, 256, 128], P('rows', 'cols')
- input_grad: bfloat16 [16, 256, 256], P('rows', 'cols')
- projection_grad: float32 [256, 512], replicated
- first_grad: float32 [3, 3, 256, 128], replicated
- second_grad: float32 [3, 3, 128, 128], replicated
The draws below stay inside these ranges and needn't reach their ends.
All inputs are finite; a program needn't handle non-finite values.
Results may differ from the reference program's by a relative error of at most 0.033.
Values may be sent and summed in bfloat16 or wider, within the bound.
No kernel may reach another device: no remote copies, remote signals or barrier semaphores. Data moves between devices by JAX's collectives and lax.ppermute only.
A program may use at most 64 MiB of HBM per device.

```python
import math
import jax
import jax.numpy as jnp
from jax import lax

CH = 256
QK = 128
VAL = 256
HEADS = 8
CONV = 128
HEIGHT = 16
WIDTH = 256


def draw_features(key, part):
    keys_all = jax.random.split(key, 1)
    result = jnp.clip(jax.random.normal(keys_all[0], (HEIGHT, WIDTH, CH), jnp.float32), -4.5, 4.5)
    return result.astype(jnp.bfloat16)


def draw_projection(key, part):
    keys_all = jax.random.split(key, 3)
    base = jnp.clip(jax.random.normal(keys_all[0], (CH, QK), jnp.float32), -4.5, 4.5)
    other = jnp.clip(jax.random.normal(keys_all[1], (CH, QK), jnp.float32), -4.5, 4.5)
    values_part = jnp.clip(jax.random.normal(keys_all[2], (CH, VAL), jnp.float32), -4.5, 4.5)
    result = jnp.concatenate([base, 0.6 * base + 0.8 * other, values_part], axis=1) / math.sqrt(CH)
    return result.astype(jnp.bfloat16)


def steps_of(key, dims, shards, low, top_value):
    loudness = 1.0
    for axis_at, blocks in shards:
        draws = jax.random.uniform(jax.random.fold_in(jax.random.fold_in(key, 6), axis_at), (blocks,), jnp.float32, low / len(shards), top_value / len(shards))
        loudness = loudness * jnp.repeat(jnp.exp(draws), dims[axis_at] // blocks).reshape((-1,) + (1,) * (len(dims) - 1 - axis_at))
    return loudness


def normal_values(rng, extent, spread, reach, cuts=(), held_as=jnp.bfloat16):
    values = jax.random.normal(rng, extent, jnp.float32) * spread
    if len(cuts) > 0:
        values = steps_of(rng, extent, cuts, -0.22, 0.18) * values
    return jnp.clip(values, min=-reach, max=reach).astype(held_as)


def setup_inputs(seed: int = 0) -> dict:
    seeds = jax.random.split(jax.random.key(seed), 6)
    features = draw_features(jax.random.fold_in(seeds[5], 71), 0)
    projection = draw_projection(jax.random.fold_in(seeds[5], 71), 0)
    first_kernel = normal_values(seeds[2], (3, 3, VAL, CONV), (9 * VAL) ** -0.5, 0.125)
    second_kernel = normal_values(seeds[3], (3, 3, CONV, CONV), (9 * CONV) ** -0.5, 0.1875)
    cotangent = normal_values(seeds[4], (HEIGHT, WIDTH, CONV), 1.0, 6.0, ((0, 16), (1, 2)))
    return dict(features=features, projection=projection, first_kernel=first_kernel, second_kernel=second_kernel, cotangent=cotangent)


def rounded(values):
    return lax.optimization_barrier(values.astype(jnp.bfloat16))

def as_wide(values):
    return values.astype(jnp.float32)

def pad_image(field):
    return jnp.pad(field, ((1, 1), (1, 1), (0, 0)))

def conv_apply(padded, kernel):
    rows_out = padded.shape[0] - 2
    cols_out = padded.shape[1] - 2
    result = jnp.zeros((rows_out, cols_out, kernel.shape[3]), jnp.float32)
    for tap_row in range(3):
        for tap_col in range(3):
            window = padded[tap_row:tap_row + rows_out, tap_col:tap_col + cols_out]
            result = result + jnp.einsum('rwc,cd->rwd', as_wide(window), as_wide(kernel[tap_row, tap_col]))
    return result

def conv_transpose(padded, kernel):
    rows_out = padded.shape[0] - 2
    cols_out = padded.shape[1] - 2
    result = jnp.zeros((rows_out, cols_out, kernel.shape[2]), jnp.float32)
    for tap_row in range(3):
        for tap_col in range(3):
            window = padded[2 - tap_row:2 - tap_row + rows_out, 2 - tap_col:2 - tap_col + cols_out]
            result = result + jnp.einsum('rwd,cd->rwc', as_wide(window), as_wide(kernel[tap_row, tap_col]))
    return result

def kernel_grad(padded, upstream):
    rows_out = upstream.shape[0]
    cols_out = upstream.shape[1]
    taps = []
    for tap_row in range(3):
        for tap_col in range(3):
            window = padded[tap_row:tap_row + rows_out, tap_col:tap_col + cols_out]
            taps.append(jnp.einsum('rwc,rwd->cd', as_wide(window), as_wide(upstream)))
    return jnp.stack(taps).reshape(3, 3, padded.shape[2], upstream.shape[2])

def silu_slope(pre_act):
    sigma = jax.nn.sigmoid(pre_act)
    return sigma * (1.0 + pre_act * (1.0 - sigma))

def row_forward(query_rows, key_rows, value_rows, scaling):
    query_count = query_rows.shape[0]
    block_rows = min(512, query_count)
    head_count = query_rows.shape[1]
    grouped = query_rows.reshape(query_count // block_rows, block_rows, head_count, query_rows.shape[2])

    def one_block(query_block):
        scores = scaling * jnp.einsum('qhd,khd->hqk', as_wide(query_block), as_wide(key_rows))
        maxima = lax.optimization_barrier(jnp.max(scores, axis=-1))
        exponent = jnp.exp(scores - maxima[:, :, None])
        totals = lax.optimization_barrier(jnp.sum(exponent, axis=-1))
        weighted = jnp.einsum('hqk,khd->qhd', as_wide(rounded(exponent)), as_wide(value_rows))
        return rounded(weighted / jnp.transpose(totals)[:, :, None])
    return lax.map(one_block, grouped).reshape(query_count, head_count, value_rows.shape[2])

def row_backward(query_rows, key_rows, value_rows, upstream_rows, attended_rows, scaling):
    query_count = query_rows.shape[0]
    block_rows = min(512, query_count)
    head_count = query_rows.shape[1]
    blocks_total = query_count // block_rows
    grouped_query = query_rows.reshape(blocks_total, block_rows, head_count, query_rows.shape[2])
    grouped_up = upstream_rows.reshape(blocks_total, block_rows, head_count, value_rows.shape[2])
    grouped_att = attended_rows.reshape(blocks_total, block_rows, head_count, value_rows.shape[2])

    def one_block(running, block_items):
        query_block, up_block, att_block = block_items
        scores = scaling * jnp.einsum('qhd,khd->hqk', as_wide(query_block), as_wide(key_rows))
        maxima = lax.optimization_barrier(jnp.max(scores, axis=-1))
        totals = lax.optimization_barrier(jnp.sum(jnp.exp(scores - maxima[:, :, None]), axis=-1))
        log_total = maxima + jnp.log(totals)
        soft = jnp.exp(scores - log_total[:, :, None])
        inner = jnp.transpose(lax.optimization_barrier(jnp.sum(as_wide(up_block) * as_wide(att_block), axis=-1)))
        slopes = jnp.einsum('qhd,khd->hqk', as_wide(up_block), as_wide(value_rows))
        dscore = as_wide(rounded(soft * (slopes - inner[:, :, None])))
        grad_query = scaling * jnp.einsum('hqk,khd->qhd', dscore, as_wide(key_rows))
        grad_key = running[0] + scaling * jnp.einsum('hqk,qhd->khd', dscore, as_wide(query_block))
        grad_value = running[1] + jnp.einsum('hqk,qhd->khd', as_wide(rounded(soft)), as_wide(up_block))
        return ((grad_key, grad_value), grad_query)
    zeros_pair = (jnp.zeros(key_rows.shape, jnp.float32), jnp.zeros(value_rows.shape, jnp.float32))
    sums_pair, grad_query = lax.scan(one_block, zeros_pair, (grouped_query, grouped_up, grouped_att))
    return (grad_query.reshape(query_count, head_count, query_rows.shape[2]), sums_pair[0], sums_pair[1])

def reference(features, projection, first_kernel, second_kernel, cotangent):
    head_qk = QK // HEADS
    head_val = VAL // HEADS
    scaling = head_qk ** (-0.5)
    flattened = features.reshape(HEIGHT * WIDTH, CH)
    packed = rounded(jnp.dot(flattened, projection, preferred_element_type=jnp.float32))
    query_all = packed[:, :QK].reshape(HEIGHT, WIDTH, HEADS, head_qk)
    key_all = packed[:, QK:2 * QK].reshape(HEIGHT, WIDTH, HEADS, head_qk)
    value_all = packed[:, 2 * QK:].reshape(HEIGHT, WIDTH, HEADS, head_val)

    def forward_row(row_items):
        return row_forward(row_items[0], row_items[1], row_items[2], scaling)
    attended4 = lax.map(forward_row, (query_all, key_all, value_all))
    attended = attended4.reshape(HEIGHT, WIDTH, VAL)
    attended_pad = pad_image(attended)
    pre_act = conv_apply(attended_pad, first_kernel)
    hidden = rounded(jax.nn.silu(pre_act))
    hidden_pad = pad_image(hidden)
    output_map = conv_apply(hidden_pad, second_kernel).astype(jnp.bfloat16)
    second_sum = kernel_grad(hidden_pad, cotangent)
    slope_pre = rounded(conv_transpose(pad_image(cotangent), second_kernel) * silu_slope(pre_act))
    first_sum = kernel_grad(attended_pad, slope_pre)
    upstream = rounded(conv_transpose(pad_image(slope_pre), first_kernel))
    upstream4 = upstream.reshape(HEIGHT, WIDTH, HEADS, head_val)

    def backward_row(row_items):
        return row_backward(row_items[0], row_items[1], row_items[2], row_items[3], row_items[4], scaling)
    grad_query, grad_key, grad_value = lax.map(backward_row, (query_all, key_all, value_all, upstream4, attended4))
    grad_packed = rounded(jnp.concatenate([grad_query.reshape(HEIGHT * WIDTH, QK), grad_key.reshape(HEIGHT * WIDTH, QK), grad_value.reshape(HEIGHT * WIDTH, VAL)], axis=-1))
    input_grad = jnp.dot(grad_packed, projection.T, preferred_element_type=jnp.float32).astype(jnp.bfloat16)
    projection_sum = jnp.dot(flattened.T, grad_packed, preferred_element_type=jnp.float32)
    factor = 1.0 / math.sqrt(HEIGHT * WIDTH)
    return (output_map, input_grad.reshape(HEIGHT, WIDTH, CH), projection_sum * factor, first_sum * factor, second_sum * factor)
```

```python
import functools
import math

import jax
import jax.numpy as jnp
from jax import lax
from jax.experimental import pallas as pl
from jax.experimental.pallas import tpu as pltpu
from jax.sharding import PartitionSpec as P

QK = 128
VAL = 256
HEADS = 8
CONV = 128
HEAD_QK = QK // HEADS
HEAD_VAL = VAL // HEADS
PACKED = 2 * QK + VAL
BLOCK = 256
BF = jnp.bfloat16
F32 = jnp.float32
SCALING = HEAD_QK ** (-0.5)

PARTS = 8
FIRST_ROWS = 9 * VAL // PARTS
SECOND_ROWS = 9 * CONV // PARTS


def mm(a, b):
    return lax.dot_general(a, b, (((1,), (0,)), ((), ())), preferred_element_type=F32)


def mm_t(a, b):
    return lax.dot_general(a, b, (((1,), (1,)), ((), ())), preferred_element_type=F32)


def one_hot(shape, wanted):
    rows = lax.broadcasted_iota(jnp.int32, shape, 0)
    columns = lax.broadcasted_iota(jnp.int32, shape, 1)
    return jnp.where(columns == wanted(rows), 1.0, 0.0).astype(BF)


def identity(size):
    return one_hot((size, size), lambda rows: rows)


def head_of(values, head, width):
    lanes = lax.broadcasted_iota(jnp.int32, values.shape, 1)
    return jnp.where(lanes // width == head, values, jnp.zeros_like(values))


def moved(values, step):
    count = values.shape[0]
    turned = pltpu.roll(values, (-step) % count, 0)
    at = lax.broadcasted_iota(jnp.int32, values.shape, 0)
    return jnp.where(at == (count - 1 if step > 0 else 0), 0.0, turned)


def for_blocks(count, run):
    if count == 1:
        run(0)
    else:
        lax.fori_loop(0, count, lambda i, carry: (run(i), carry)[1], 0)


def block_at(index):
    return pl.ds(index if isinstance(index, int) else pl.multiple_of(index * BLOCK, BLOCK), BLOCK)


def forward_kernel(whole, *refs):
    pieces = refs[: 1 if whole else 2]
    projection, comb, local, lse, values_t = refs[len(pieces) :]
    across = comb.shape[0]
    for which, piece in enumerate(pieces):
        width = piece.shape[0]
        if whole:
            at = pl.ds(0, width)
        else:
            place = lax.rem(lax.axis_index("cols") + which, 2)
            at = pl.ds(pl.multiple_of(place * width, width), width)
        local[at, PACKED:] = piece[:, :VAL]
        comb[at, VAL:] = piece[:, VAL:]
    packed = mm(local[:, PACKED:], projection[...]).astype(BF)
    local[:, :PACKED] = packed
    keys = packed[:, QK : 2 * QK]
    values_t[...] = mm_t(identity(VAL), packed[:, 2 * QK :]).astype(BF)

    def block(index):
        at = block_at(index)
        queries = local[at, :QK]
        rows = []
        for head in range(HEADS):
            scores = SCALING * mm_t(head_of(keys, head, HEAD_QK), queries)
            maxima = jnp.max(scores, axis=0, keepdims=True)
            exponent = jnp.exp(scores - maxima)
            totals = jnp.sum(exponent, axis=0, keepdims=True)
            weighted = mm(values_t[head * HEAD_VAL : (head + 1) * HEAD_VAL, :], exponent.astype(BF))
            rows.append((weighted / totals).astype(BF))
            lse[head : head + 1, at] = maxima + jnp.log(totals)
        comb[at, :VAL] = mm_t(identity(BLOCK), jnp.concatenate(rows, axis=0)).astype(BF)

    for_blocks(across // BLOCK, block)


def backward_kernel(
    near2,
    near1,
    own,
    mate,
    mate1,
    local,
    lse,
    projection,
    first_kernel,
    second_kernel,
    output_map,
    input_grad,
    keep,
    send,
    proj_own,
    proj_mate,
    wide,
    upstream_ref,
    grad_t,
):
    across = own.shape[0]
    part_width = output_map.shape[0]
    row = lax.axis_index("rows")
    col = lax.axis_index("cols")
    core = lax.rem(row, 2)
    chip_bit = lax.rem(row // 2, 2)
    col_bit = lax.rem(col, 2)
    quarter = 2 * core + col_bit
    other_quarter = 2 * (1 - core) + col_bit
    inside = jnp.where(core == 0, row > 0, row < lax.axis_size("rows") - 1)
    slots = (near2, near1, own, mate, mate1)
    taps = [tap + core * (2 - 2 * tap) for tap in range(3)]

    def attended(slot):
        return slots[slot][:, :VAL]

    def cotangent(slot):
        return slots[slot][:, VAL:]

    def side(total, width, sign):
        left = moved(total[:, :width], -sign)
        right = moved(total[:, 2 * width :], sign)
        return left + total[:, width : 2 * width] + right

    def spread(values):
        return jnp.concatenate(
            [moved(values, 1).astype(BF), values.astype(BF), moved(values, -1).astype(BF)], axis=1
        )

    def beside(weights, tap):
        return jnp.concatenate([weights[taps[tap], b] for b in range(3)], axis=1)

    def stacked(weights, tap):
        return jnp.concatenate([weights[taps[tap], b] for b in range(3)], axis=0)

    hidden = {}
    slope = {}
    for slot in (1, 2, 3):
        pre = side(sum(mm(attended(slot + a - 1), beside(first_kernel, a)) for a in range(3)), CONV, 1)
        back = side(sum(mm_t(cotangent(slot + 1 - a), stacked(second_kernel, a)) for a in range(3)), CONV, -1)
        sigma = 1.0 / (1.0 + jnp.exp(-pre))
        hidden_wide = pre * sigma
        slope_wide = back * (sigma * (1.0 + pre * (1.0 - sigma)))
        if slot == 1:
            hidden_wide = jnp.where(inside, hidden_wide, 0.0)
            slope_wide = jnp.where(inside, slope_wide, 0.0)
        hidden[slot] = hidden_wide.astype(BF)
        slope[slot] = slope_wide

    wide[...] = side(sum(mm(hidden[1 + a], beside(second_kernel, a)) for a in range(3)), CONV, 1)
    mine = pl.ds(pl.multiple_of(col * part_width, part_width), part_width)
    output_map[...] = wide[mine, :].astype(BF)

    upstream_ref[...] = side(
        sum(mm_t(slope[3 - a].astype(BF), stacked(first_kernel, a)) for a in range(3)), VAL, -1
    ).astype(BF)

    def chosen(total, which):
        size = total // 4
        half = size // 2

        def wanted(rows):
            swapped = jnp.where(rows < half, rows + half, rows - half)
            return which * size + jnp.where(chip_bit == 0, rows, swapped)

        return one_hot((size, total), wanted)

    pick = chosen(VAL, quarter)
    attended_t = {slot: mm_t(pick, attended(slot)).astype(BF) for slot in (1, 2, 3, 4)}
    spread_slope = {slot: spread(slope[slot]) for slot in (2, 3)}
    step = VAL // PARTS
    for a in range(3):
        total = sum(mm(attended_t[slot + a - 1], spread_slope[slot]) for slot in (2, 3)).astype(BF)
        for b in range(3):
            at = pl.ds(pl.multiple_of((taps[a] * 3 + b) * step, step), step)
            keep[at, :] = total[:step, b * CONV : (b + 1) * CONV]
            send[at, :] = total[step:, b * CONV : (b + 1) * CONV]
    pick = chosen(CONV, quarter)
    hidden_t = {slot: mm_t(pick, hidden[slot]).astype(BF) for slot in (2, 3)}
    spread_cot = {slot: spread(cotangent(slot).astype(F32)) for slot in (1, 2, 3, 4)}
    step = CONV // PARTS
    for a in range(3):
        total = sum(mm(hidden_t[slot], spread_cot[slot + 1 - a]) for slot in (2, 3)).astype(BF)
        for b in range(3):
            at = pl.ds(pl.multiple_of(FIRST_ROWS + (taps[a] * 3 + b) * step, step), step)
            keep[at, :] = total[:step, b * CONV : (b + 1) * CONV]
            send[at, :] = total[step:, b * CONV : (b + 1) * CONV]

    keys = local[:, QK : 2 * QK]
    values = local[:, 2 * QK : PACKED]
    keys_t = mm_t(identity(QK), keys).astype(BF)
    blocks = across // BLOCK
    if blocks > 1:
        grad_t[...] = jnp.zeros_like(grad_t)

    def add_rows(start, count, terms):
        if blocks > 1:
            grad_t[start : start + count, :] += terms
        else:
            grad_t[start : start + count, :] = terms

    def block(index):
        at = block_at(index)
        queries = local[at, :QK]
        upstream = upstream_ref[at, :]
        queries_t = mm_t(identity(QK), queries).astype(BF)
        upstream_t = mm_t(identity(VAL), upstream)
        products = upstream_t * mm_t(identity(VAL), own[at, :VAL])
        upstream_t = upstream_t.astype(BF)
        for head in range(HEADS):
            qk_rows = slice(head * HEAD_QK, (head + 1) * HEAD_QK)
            val_rows = slice(head * HEAD_VAL, (head + 1) * HEAD_VAL)
            scores = SCALING * mm_t(head_of(keys, head, HEAD_QK), queries)
            soft = jnp.exp(scores - lse[head : head + 1, at])
            inner = jnp.sum(products[val_rows, :], axis=0, keepdims=True)
            slopes = mm_t(head_of(values, head, HEAD_VAL), upstream)
            dscore = (soft * (slopes - inner)).astype(BF)
            grad_t[qk_rows, at] = SCALING * mm(keys_t[qk_rows, :], dscore)
            add_rows(QK + head * HEAD_QK, HEAD_QK, SCALING * mm_t(queries_t[qk_rows, :], dscore))
            add_rows(2 * QK + head * HEAD_VAL, HEAD_VAL, mm_t(upstream_t[val_rows, :], soft.astype(BF)))

    for_blocks(blocks, block)

    grad = grad_t[...].astype(BF)
    own_pixels = one_hot((part_width, across), lambda rows: rows + col * part_width)
    grad_own = mm_t(own_pixels, grad).astype(BF)
    input_grad[...] = mm_t(grad_own, projection[...]).astype(BF)
    features = local[:, PACKED:]
    step = VAL // PARTS
    for target, which in ((proj_own, quarter), (proj_mate, other_quarter)):
        features_t = mm_t(chosen(VAL, which), features).astype(BF)
        total = mm_t(features_t, grad).astype(BF)
        for j in range(PACKED // CONV):
            target[0, j * step : (j + 1) * step, :] = total[:step, j * CONV : (j + 1) * CONV]
            target[1, j * step : (j + 1) * step, :] = total[step:, j * CONV : (j + 1) * CONV]


def unpack_kernel(factor, *refs):
    pieces = refs[:8]
    projection_grad, first_grad, second_grad = refs[8:]
    row = lax.axis_index("rows")
    core = lax.rem(row, 2)
    chip_bit = lax.rem(row // 2, 2)
    col_bit = lax.rem(lax.axis_index("cols"), 2)
    for which, piece in enumerate(pieces):
        core_flip, col_flip, chip_flip = which // 4, which // 2 % 2, which % 2
        part = (
            4 * lax.rem(core + core_flip, 2) + 2 * lax.rem(col_bit + col_flip, 2) + lax.rem(chip_bit + chip_flip, 2)
        )
        step = VAL // PARTS
        at = pl.ds(pl.multiple_of(part * step, step), step)
        for tap in range(9):
            first_grad[tap // 3, tap % 3, at, :] = piece[tap * step : (tap + 1) * step, :].astype(F32) * factor
        start = FIRST_ROWS + SECOND_ROWS
        for j in range(PACKED // CONV):
            projection_grad[at, j * CONV : (j + 1) * CONV] = (
                piece[start + j * step : start + (j + 1) * step, :].astype(F32) * factor
            )
        step = CONV // PARTS
        at = pl.ds(pl.multiple_of(part * step, step), step)
        for tap in range(9):
            begin = FIRST_ROWS + tap * step
            second_grad[tap // 3, tap % 3, at, :] = piece[begin : begin + step, :].astype(F32) * factor


def shape(*dims, dtype=BF):
    return jax.ShapeDtypeStruct(dims, dtype)


PARAMS = dict(compiler_params=pltpu.CompilerParams(vmem_limit_bytes=52 * 1024 * 1024))
VMEM = pl.BlockSpec(memory_space=pltpu.VMEM)


def body(features, projection, first_kernel, second_kernel, cotangent):
    height, part_width, channels = features.shape
    rows_size = lax.axis_size("rows")
    cols_size = lax.axis_size("cols")
    across = part_width * cols_size
    flat = PACKED // CONV * (VAL // PARTS)

    def rows_flip(values, bit):
        return lax.ppermute(values, "rows", [(i, i ^ bit) for i in range(rows_size)])

    def cols_flip(values):
        return lax.ppermute(values, "cols", [(i, i ^ 1) for i in range(cols_size)])

    both = jnp.concatenate([features[0], cotangent[0]], axis=-1)
    if cols_size == 2:
        pieces = (both, cols_flip(both))
    else:
        pieces = (lax.all_gather(both, "cols", axis=0, tiled=True),)
    own, local, lse = pl.pallas_call(
        functools.partial(forward_kernel, cols_size != 2),
        out_shape=(
            shape(across, VAL + CONV),
            shape(across, PACKED + channels),
            shape(HEADS, across, dtype=F32),
        ),
        in_specs=[VMEM] * (len(pieces) + 1),
        out_specs=[VMEM] * 3,
        scratch_shapes=[pltpu.VMEM((VAL, across), BF)],
        name="attention_forward",
        **PARAMS,
    )(*pieces, projection)

    far = [(i, i + 2) for i in range(0, rows_size - 2, 2)] + [(i, i - 2) for i in range(3, rows_size, 2)]
    near = [(i, i + 1) for i in range(1, rows_size - 1, 2)] + [(i + 1, i) for i in range(1, rows_size - 1, 2)]
    near1 = lax.ppermute(own, "rows", near)
    near2 = lax.ppermute(own, "rows", far)
    mate = rows_flip(own, 1)
    mate1 = rows_flip(near1, 1)

    output_map, input_grad, keep, send, proj_own, proj_mate = pl.pallas_call(
        backward_kernel,
        out_shape=(
            shape(part_width, CONV),
            shape(part_width, channels),
            shape(FIRST_ROWS + SECOND_ROWS, CONV),
            shape(FIRST_ROWS + SECOND_ROWS, CONV),
            shape(2, flat, CONV),
            shape(2, flat, CONV),
        ),
        in_specs=[VMEM] * 10,
        out_specs=[VMEM] * 6,
        scratch_shapes=[
            pltpu.VMEM((across, CONV), F32),
            pltpu.VMEM((across, VAL), BF),
            pltpu.VMEM((PACKED, across), F32),
        ],
        name="block_backward",
        **PARAMS,
    )(near2, near1, own, mate, mate1, local, lse, projection, first_kernel, second_kernel)

    proj_sum = (proj_own.astype(F32) + rows_flip(proj_mate, 1).astype(F32)).astype(BF)
    arrived = rows_flip(jnp.concatenate([send, proj_sum[1]], axis=0), 2)
    total = jnp.concatenate([keep, proj_sum[0]], axis=0)
    total = (total.astype(F32) + arrived.astype(F32)).astype(BF)
    bit = 4
    while bit < rows_size:
        total = (total.astype(F32) + rows_flip(total, bit).astype(F32)).astype(BF)
        bit *= 2
    chip = rows_flip(total, 2)
    side = cols_flip(total)
    corner = lax.ppermute(
        total,
        ("rows", "cols"),
        [(i * cols_size + j, (i ^ 2) * cols_size + (j ^ 1)) for i in range(rows_size) for j in range(cols_size)],
    )
    four = (total, chip, side, corner)
    eight = four + tuple(rows_flip(piece, 1) for piece in four)
    factor = 1.0 / math.sqrt(height * across * rows_size)
    projection_grad, first_grad, second_grad = pl.pallas_call(
        functools.partial(unpack_kernel, factor),
        out_shape=(
            shape(channels, PACKED, dtype=F32),
            shape(3, 3, VAL, CONV, dtype=F32),
            shape(3, 3, CONV, CONV, dtype=F32),
        ),
        in_specs=[VMEM] * 8,
        out_specs=[VMEM] * 3,
        name="unpack_sums",
        **PARAMS,
    )(*eight)
    return (output_map[None], input_grad[None], projection_grad, first_grad, second_grad)


def solution(mesh):
    placed = (P("rows", "cols", None), P(), P(), P(), P("rows", "cols", None))
    return jax.shard_map(
        body,
        mesh=mesh,
        in_specs=placed,
        out_specs=(P("rows", "cols", None), P("rows", "cols", None), P(), P(), P()),
        check_vma=False,
    )
```

```python
import functools
import math

import jax
import jax.numpy as jnp
from jax import lax
from jax.experimental import pallas as pl
from jax.experimental.pallas import tpu as pltpu
from jax.sharding import PartitionSpec as P

QK = 128
VAL = 256
HEADS = 8
CONV = 128
HEAD_QK = QK // HEADS
HEAD_VAL = VAL // HEADS
PACKED = 2 * QK + VAL
BLOCK = 256
BF = jnp.bfloat16
F32 = jnp.float32
SCALING = HEAD_QK ** (-0.5)

PARTS = 8
FIRST_ROWS = 9 * VAL // PARTS
SECOND_ROWS = 9 * CONV // PARTS


def mm(a, b):
    return lax.dot_general(a, b, (((1,), (0,)), ((), ())), preferred_element_type=F32)


def mm_t(a, b):
    return lax.dot_general(a, b, (((1,), (1,)), ((), ())), preferred_element_type=F32)


def one_hot(shape, wanted):
    rows = lax.broadcasted_iota(jnp.int32, shape, 0)
    columns = lax.broadcasted_iota(jnp.int32, shape, 1)
    return jnp.where(columns == wanted(rows), 1.0, 0.0).astype(BF)


def identity(size):
    return one_hot((size, size), lambda rows: rows)


def head_of(values, head, width):
    lanes = lax.broadcasted_iota(jnp.int32, values.shape, 1)
    return jnp.where(lanes // width == head, values, jnp.zeros_like(values))


def moved(values, step):
    count = values.shape[0]
    turned = pltpu.roll(values, (-step) % count, 0)
    at = lax.broadcasted_iota(jnp.int32, values.shape, 0)
    return jnp.where(at == (count - 1 if step > 0 else 0), 0.0, turned)


def for_blocks(count, run):
    if count == 1:
        run(0)
    else:
        lax.fori_loop(0, count, lambda i, carry: (run(i), carry)[1], 0)


def block_at(index):
    return pl.ds(index if isinstance(index, int) else pl.multiple_of(index * BLOCK, BLOCK), BLOCK)


def fetch_kernel(*refs):
    count = (len(refs) - 1) // 2
    copies = [pltpu.make_async_copy(refs[i], refs[count + i], refs[-1].at[i]) for i in range(count)]
    for copy in copies:
        copy.start()
    for copy in copies:
        copy.wait()


def forward_kernel(whole, *refs):
    count = 1 if whole else 2
    features = refs[:count]
    cotangent = refs[count : 2 * count]
    projection, comb, local, lse, values_t = refs[2 * count :]
    across = comb.shape[0]
    for which in range(count):
        width = features[which].shape[0]
        if whole:
            at = pl.ds(0, width)
        else:
            place = lax.rem(lax.axis_index("cols") + which, 2)
            at = pl.ds(pl.multiple_of(place * width, width), width)
        local[at, PACKED:] = features[which][...]
        comb[at, VAL:] = cotangent[which][...]
    packed = mm(local[:, PACKED:], projection[...]).astype(BF)
    local[:, :PACKED] = packed
    keys = packed[:, QK : 2 * QK]
    values_t[...] = mm_t(identity(VAL), packed[:, 2 * QK :]).astype(BF)

    def block(index):
        at = block_at(index)
        queries = local[at, :QK]
        rows = []
        for head in range(HEADS):
            scores = SCALING * mm_t(head_of(keys, head, HEAD_QK), queries)
            maxima = jnp.max(scores, axis=0, keepdims=True)
            exponent = jnp.exp(scores - maxima)
            totals = jnp.sum(exponent, axis=0, keepdims=True)
            weighted = mm(values_t[head * HEAD_VAL : (head + 1) * HEAD_VAL, :], exponent.astype(BF))
            rows.append((weighted / totals).astype(BF))
            lse[head : head + 1, at] = maxima + jnp.log(totals)
        comb[at, :VAL] = mm_t(identity(BLOCK), jnp.concatenate(rows, axis=0)).astype(BF)

    for_blocks(across // BLOCK, block)


def backward_kernel(
    near2,
    near1,
    own,
    mate,
    mate1,
    local,
    lse,
    projection,
    first_kernel,
    second_kernel,
    output_map,
    input_grad,
    keep,
    send,
    proj_own,
    proj_mate,
    wide,
    upstream_ref,
    grad_t,
):
    across = own.shape[0]
    part_width = output_map.shape[0]
    row = lax.axis_index("rows")
    col = lax.axis_index("cols")
    core = lax.rem(row, 2)
    chip_bit = lax.rem(row // 2, 2)
    col_bit = lax.rem(col, 2)
    quarter = 2 * core + col_bit
    other_quarter = 2 * (1 - core) + col_bit
    inside = jnp.where(core == 0, row > 0, row < lax.axis_size("rows") - 1)
    slots = (near2, near1, own, mate, mate1)
    taps = [tap + core * (2 - 2 * tap) for tap in range(3)]

    def attended(slot):
        return slots[slot][:, :VAL]

    def cotangent(slot):
        return slots[slot][:, VAL:]

    def side(total, width, sign):
        left = moved(total[:, :width], -sign)
        right = moved(total[:, 2 * width :], sign)
        return left + total[:, width : 2 * width] + right

    def spread(values):
        return jnp.concatenate(
            [moved(values, 1).astype(BF), values.astype(BF), moved(values, -1).astype(BF)], axis=1
        )

    def beside(weights, tap):
        return jnp.concatenate([weights[taps[tap], b] for b in range(3)], axis=1)

    def stacked(weights, tap):
        return jnp.concatenate([weights[taps[tap], b] for b in range(3)], axis=0)

    hidden = {}
    slope = {}
    for slot in (1, 2, 3):
        pre = side(sum(mm(attended(slot + a - 1), beside(first_kernel, a)) for a in range(3)), CONV, 1)
        back = side(sum(mm_t(cotangent(slot + 1 - a), stacked(second_kernel, a)) for a in range(3)), CONV, -1)
        sigma = 1.0 / (1.0 + jnp.exp(-pre))
        hidden_wide = pre * sigma
        slope_wide = back * (sigma * (1.0 + pre * (1.0 - sigma)))
        if slot == 1:
            hidden_wide = jnp.where(inside, hidden_wide, 0.0)
            slope_wide = jnp.where(inside, slope_wide, 0.0)
        hidden[slot] = hidden_wide.astype(BF)
        slope[slot] = slope_wide

    wide[...] = side(sum(mm(hidden[1 + a], beside(second_kernel, a)) for a in range(3)), CONV, 1)
    mine = pl.ds(pl.multiple_of(col * part_width, part_width), part_width)
    output_map[...] = wide[mine, :].astype(BF)

    upstream_ref[...] = side(
        sum(mm_t(slope[3 - a].astype(BF), stacked(first_kernel, a)) for a in range(3)), VAL, -1
    ).astype(BF)

    def chosen(total, which):
        size = total // 4
        half = size // 2

        def wanted(rows):
            swapped = jnp.where(rows < half, rows + half, rows - half)
            return which * size + jnp.where(chip_bit == 0, rows, swapped)

        return one_hot((size, total), wanted)

    pick = chosen(VAL, quarter)
    attended_t = {slot: mm_t(pick, attended(slot)).astype(BF) for slot in (1, 2, 3, 4)}
    spread_slope = {slot: spread(slope[slot]) for slot in (2, 3)}
    step = VAL // PARTS
    for a in range(3):
        total = sum(mm(attended_t[slot + a - 1], spread_slope[slot]) for slot in (2, 3)).astype(BF)
        for b in range(3):
            at = pl.ds(pl.multiple_of((taps[a] * 3 + b) * step, step), step)
            keep[at, :] = total[:step, b * CONV : (b + 1) * CONV]
            send[at, :] = total[step:, b * CONV : (b + 1) * CONV]
    pick = chosen(CONV, quarter)
    hidden_t = {slot: mm_t(pick, hidden[slot]).astype(BF) for slot in (2, 3)}
    spread_cot = {slot: spread(cotangent(slot).astype(F32)) for slot in (1, 2, 3, 4)}
    step = CONV // PARTS
    for a in range(3):
        total = sum(mm(hidden_t[slot], spread_cot[slot + 1 - a]) for slot in (2, 3)).astype(BF)
        for b in range(3):
            at = pl.ds(pl.multiple_of(FIRST_ROWS + (taps[a] * 3 + b) * step, step), step)
            keep[at, :] = total[:step, b * CONV : (b + 1) * CONV]
            send[at, :] = total[step:, b * CONV : (b + 1) * CONV]

    keys = local[:, QK : 2 * QK]
    values = local[:, 2 * QK : PACKED]
    keys_t = mm_t(identity(QK), keys).astype(BF)
    blocks = across // BLOCK
    if blocks > 1:
        grad_t[...] = jnp.zeros_like(grad_t)

    def add_rows(start, count, terms):
        if blocks > 1:
            grad_t[start : start + count, :] += terms
        else:
            grad_t[start : start + count, :] = terms

    def block(index):
        at = block_at(index)
        queries = local[at, :QK]
        upstream = upstream_ref[at, :]
        queries_t = mm_t(identity(QK), queries).astype(BF)
        upstream_t = mm_t(identity(VAL), upstream)
        products = upstream_t * mm_t(identity(VAL), own[at, :VAL])
        upstream_t = upstream_t.astype(BF)
        for head in range(HEADS):
            qk_rows = slice(head * HEAD_QK, (head + 1) * HEAD_QK)
            val_rows = slice(head * HEAD_VAL, (head + 1) * HEAD_VAL)
            scores = SCALING * mm_t(head_of(keys, head, HEAD_QK), queries)
            soft = jnp.exp(scores - lse[head : head + 1, at])
            inner = jnp.sum(products[val_rows, :], axis=0, keepdims=True)
            slopes = mm_t(head_of(values, head, HEAD_VAL), upstream)
            dscore = (soft * (slopes - inner)).astype(BF)
            grad_t[qk_rows, at] = SCALING * mm(keys_t[qk_rows, :], dscore)
            add_rows(QK + head * HEAD_QK, HEAD_QK, SCALING * mm_t(queries_t[qk_rows, :], dscore))
            add_rows(2 * QK + head * HEAD_VAL, HEAD_VAL, mm_t(upstream_t[val_rows, :], soft.astype(BF)))

    for_blocks(blocks, block)

    grad = grad_t[...].astype(BF)
    own_pixels = one_hot((part_width, across), lambda rows: rows + col * part_width)
    grad_own = mm_t(own_pixels, grad).astype(BF)
    input_grad[...] = mm_t(grad_own, projection[...]).astype(BF)
    features = local[:, PACKED:]
    step = VAL // PARTS
    for target, which in ((proj_own, quarter), (proj_mate, other_quarter)):
        features_t = mm_t(chosen(VAL, which), features).astype(BF)
        total = mm_t(features_t, grad).astype(BF)
        for j in range(PACKED // CONV):
            target[0, j * step : (j + 1) * step, :] = total[:step, j * CONV : (j + 1) * CONV]
            target[1, j * step : (j + 1) * step, :] = total[step:, j * CONV : (j + 1) * CONV]


def unpack_kernel(factor, *refs):
    pieces = refs[:8]
    projection_grad, first_grad, second_grad = refs[8:]
    row = lax.axis_index("rows")
    core = lax.rem(row, 2)
    chip_bit = lax.rem(row // 2, 2)
    col_bit = lax.rem(lax.axis_index("cols"), 2)
    for which, piece in enumerate(pieces):
        core_flip, col_flip, chip_flip = which // 4, which // 2 % 2, which % 2
        part = (
            4 * lax.rem(core + core_flip, 2) + 2 * lax.rem(col_bit + col_flip, 2) + lax.rem(chip_bit + chip_flip, 2)
        )
        step = VAL // PARTS
        at = pl.ds(pl.multiple_of(part * step, step), step)
        for tap in range(9):
            first_grad[tap // 3, tap % 3, at, :] = piece[tap * step : (tap + 1) * step, :].astype(F32) * factor
        start = FIRST_ROWS + SECOND_ROWS
        for j in range(PACKED // CONV):
            projection_grad[at, j * CONV : (j + 1) * CONV] = (
                piece[start + j * step : start + (j + 1) * step, :].astype(F32) * factor
            )
        step = CONV // PARTS
        at = pl.ds(pl.multiple_of(part * step, step), step)
        for tap in range(9):
            begin = FIRST_ROWS + tap * step
            second_grad[tap // 3, tap % 3, at, :] = piece[begin : begin + step, :].astype(F32) * factor


def shape(*dims, dtype=BF):
    return jax.ShapeDtypeStruct(dims, dtype)


def granted(across):
    return dict(compiler_params=pltpu.CompilerParams(vmem_limit_bytes=across * 64 * 1024))


VMEM = pl.BlockSpec(memory_space=pltpu.VMEM)
HBM = pl.BlockSpec(memory_space=pltpu.HBM)


def body(features, projection, first_kernel, second_kernel, cotangent):
    height, part_width, channels = features.shape
    rows_size = lax.axis_size("rows")
    cols_size = lax.axis_size("cols")
    across = part_width * cols_size
    flat = PACKED // CONV * (VAL // PARTS)

    def rows_flip(values, bit):
        return lax.ppermute(values, "rows", [(i, i ^ bit) for i in range(rows_size)])

    def cols_flip(values):
        return lax.ppermute(values, "cols", [(i, i ^ 1) for i in range(cols_size)])

    params = granted(across)
    weights = (projection, first_kernel, second_kernel)
    projection, first_kernel, second_kernel = pl.pallas_call(
        fetch_kernel,
        out_shape=tuple(shape(*array.shape) for array in weights),
        in_specs=[HBM] * 3,
        out_specs=[VMEM] * 3,
        scratch_shapes=[pltpu.SemaphoreType.DMA((3,))],
        cost_estimate=pl.CostEstimate(flops=0, bytes_accessed=4 * 1024 * 1024, transcendentals=0),
        name="fetch_weights",
        **granted(32),
    )(*weights)
    if cols_size == 2:
        pieces = (features[0], cols_flip(features[0]), cotangent[0], cols_flip(cotangent[0]))
    else:
        pieces = tuple(lax.all_gather(array[0], "cols", axis=0, tiled=True) for array in (features, cotangent))
    own, local, lse = pl.pallas_call(
        functools.partial(forward_kernel, cols_size != 2),
        out_shape=(
            shape(across, VAL + CONV),
            shape(across, PACKED + channels),
            shape(HEADS, across, dtype=F32),
        ),
        in_specs=[VMEM] * (len(pieces) + 1),
        out_specs=[VMEM] * 3,
        scratch_shapes=[pltpu.VMEM((VAL, across), BF)],
        name="attention_forward",
        **params,
    )(*pieces, projection)

    far = [(i, i + 2) for i in range(0, rows_size - 2, 2)] + [(i, i - 2) for i in range(3, rows_size, 2)]
    near = [(i, i + 1) for i in range(1, rows_size - 1, 2)] + [(i + 1, i) for i in range(1, rows_size - 1, 2)]
    near1 = lax.ppermute(own, "rows", near)
    near2 = lax.ppermute(own, "rows", far)
    mate = rows_flip(own, 1)
    mate1 = rows_flip(near1, 1)

    output_map, input_grad, keep, send, proj_own, proj_mate = pl.pallas_call(
        backward_kernel,
        out_shape=(
            shape(part_width, CONV),
            shape(part_width, channels),
            shape(FIRST_ROWS + SECOND_ROWS, CONV),
            shape(FIRST_ROWS + SECOND_ROWS, CONV),
            shape(2, flat, CONV),
            shape(2, flat, CONV),
        ),
        in_specs=[VMEM] * 10,
        out_specs=[VMEM] * 6,
        scratch_shapes=[
            pltpu.VMEM((across, CONV), F32),
            pltpu.VMEM((across, VAL), BF),
            pltpu.VMEM((PACKED, across), F32),
        ],
        name="block_backward",
        **params,
    )(near2, near1, own, mate, mate1, local, lse, projection, first_kernel, second_kernel)

    proj_sum = (proj_own.astype(F32) + rows_flip(proj_mate, 1).astype(F32)).astype(BF)
    arrived = rows_flip(jnp.concatenate([send, proj_sum[1]], axis=0), 2)
    total = jnp.concatenate([keep, proj_sum[0]], axis=0)
    total = (total.astype(F32) + arrived.astype(F32)).astype(BF)
    bit = 4
    while bit < rows_size:
        total = (total.astype(F32) + rows_flip(total, bit).astype(F32)).astype(BF)
        bit *= 2
    chip = rows_flip(total, 2)
    side = cols_flip(total)
    corner = lax.ppermute(
        total,
        ("rows", "cols"),
        [(i * cols_size + j, (i ^ 2) * cols_size + (j ^ 1)) for i in range(rows_size) for j in range(cols_size)],
    )
    four = (total, chip, side, corner)
    eight = four + tuple(rows_flip(piece, 1) for piece in four)
    factor = 1.0 / math.sqrt(height * across * rows_size)
    projection_grad, first_grad, second_grad = pl.pallas_call(
        functools.partial(unpack_kernel, factor),
        out_shape=(
            shape(channels, PACKED, dtype=F32),
            shape(3, 3, VAL, CONV, dtype=F32),
            shape(3, 3, CONV, CONV, dtype=F32),
        ),
        in_specs=[VMEM] * 8,
        out_specs=[VMEM] * 3,
        name="unpack_sums",
        **params,
    )(*eight)
    return (output_map[None], input_grad[None], projection_grad, first_grad, second_grad)


def solution(mesh):
    placed = (P("rows", "cols", None), P(), P(), P(), P("rows", "cols", None))
    return jax.shard_map(
        body,
        mesh=mesh,
        in_specs=placed,
        out_specs=(P("rows", "cols", None), P("rows", "cols", None), P(), P(), P()),
        check_vma=False,
    )
```

```python
import functools
import math

import jax
import jax.numpy as jnp
from jax import lax
from jax.experimental import pallas as pl
from jax.experimental.pallas import tpu as pltpu
from jax.sharding import PartitionSpec as P

QK = 128
VAL = 256
HEADS = 8
CONV = 128
HEAD_QK = QK // HEADS
HEAD_VAL = VAL // HEADS
PACKED = 2 * QK + VAL
BLOCK = 256
BF = jnp.bfloat16
F32 = jnp.float32
SCALING = HEAD_QK ** (-0.5)
EXP2_SCALING = SCALING * math.log2(math.e)

PARTS = 8
FIRST_ROWS = 9 * VAL // PARTS
SECOND_ROWS = 9 * CONV // PARTS
CONV_ROWS = FIRST_ROWS + SECOND_ROWS
PROJ_ROWS = PACKED // CONV * (VAL // PARTS)


def mm(a, b):
    return lax.dot_general(a, b, (((1,), (0,)), ((), ())), preferred_element_type=F32)


def mm_t(a, b):
    return lax.dot_general(a, b, (((1,), (1,)), ((), ())), preferred_element_type=F32)


def one_hot(shape, wanted):
    rows = lax.broadcasted_iota(jnp.int32, shape, 0)
    columns = lax.broadcasted_iota(jnp.int32, shape, 1)
    return jnp.where(columns == wanted(rows), 1.0, 0.0).astype(BF)


def identity(size):
    return one_hot((size, size), lambda rows: rows)


def head_of(values, head, width):
    lanes = lax.broadcasted_iota(jnp.int32, values.shape, 1)
    return jnp.where(lanes // width == head, values, jnp.zeros_like(values))


def moved(values, step):
    count = values.shape[0]
    turned = pltpu.roll(values, (-step) % count, 0)
    at = lax.broadcasted_iota(jnp.int32, values.shape, 0)
    return jnp.where(at == (count - 1 if step > 0 else 0), 0.0, turned)


def for_blocks(count, run):
    if count == 1:
        run(0)
    else:
        lax.fori_loop(0, count, lambda i, carry: (run(i), carry)[1], 0)


def block_at(index):
    return pl.ds(index if isinstance(index, int) else pl.multiple_of(index * BLOCK, BLOCK), BLOCK)


def fetch_kernel(count, *refs):
    targets = refs[-1 - count : -1]
    copies = [pltpu.make_async_copy(refs[i], targets[i], refs[-1].at[i]) for i in range(count)]
    for copy in copies:
        copy.start()
    for copy in copies:
        copy.wait()


def fetch(arrays, after=()):
    return pl.pallas_call(
        functools.partial(fetch_kernel, len(arrays)),
        out_shape=tuple(shape(*array.shape) for array in arrays),
        in_specs=[HBM] * (len(arrays) + len(after)),
        out_specs=[VMEM] * len(arrays),
        scratch_shapes=[pltpu.SemaphoreType.DMA((len(arrays),))],
        cost_estimate=pl.CostEstimate(flops=0, bytes_accessed=4 * 1024 * 1024, transcendentals=0),
        name="fetch",
        **granted(32),
    )(*arrays, *after)


def forward_kernel(whole, *refs):
    count = 1 if whole else 2
    features = refs[:count]
    cotangent = refs[count : 2 * count]
    projection, comb, local, lse, values_t = refs[2 * count :]
    across = comb.shape[0]
    for which in range(count):
        width = features[which].shape[0]
        if whole:
            at = pl.ds(0, width)
        else:
            place = lax.rem(lax.axis_index("cols") + which, 2)
            at = pl.ds(pl.multiple_of(place * width, width), width)
        local[at, PACKED:] = features[which][...]
        comb[at, VAL:] = cotangent[which][...]
    packed = mm(local[:, PACKED:], projection[...]).astype(BF)
    local[:, :PACKED] = packed
    keys = packed[:, QK : 2 * QK]
    values_t[...] = mm_t(identity(VAL), packed[:, 2 * QK :]).astype(BF)

    def block(index):
        at = block_at(index)
        queries = local[at, :QK]
        rows = []
        all_scores = mm_t(jnp.concatenate([head_of(keys, h, HEAD_QK) for h in range(HEADS)], axis=0), queries)
        for head in range(HEADS):
            scores = all_scores[head * across : (head + 1) * across, :]
            maxima = jnp.max(scores, axis=0, keepdims=True)
            exponent = jnp.exp2((scores - maxima) * EXP2_SCALING)
            totals = jnp.sum(exponent, axis=0, keepdims=True)
            weighted = mm(values_t[head * HEAD_VAL : (head + 1) * HEAD_VAL, :], exponent.astype(BF))
            rows.append((weighted * (1.0 / totals)).astype(BF))
            lse[head : head + 1, at] = maxima * EXP2_SCALING + jnp.log2(totals)
        comb[at, :VAL] = mm_t(identity(BLOCK), jnp.concatenate(rows, axis=0)).astype(BF)

    for_blocks(across // BLOCK, block)


class Place:
    def __init__(self):
        row = lax.axis_index("rows")
        self.col = lax.axis_index("cols")
        self.core = lax.rem(row, 2)
        self.chip_bit = lax.rem(row // 2, 2)
        self.col_bit = lax.rem(self.col, 2)
        self.near_inside = jnp.where(self.core == 0, row > 0, row < lax.axis_size("rows") - 1)
        self.taps = [tap + self.core * (2 - 2 * tap) for tap in range(3)]

    def chosen(self, total, half):
        size = total // 4
        middle = size // 2

        def wanted(rows):
            swapped = jnp.where(rows < middle, rows + middle, rows - middle)
            return (2 * half + self.col_bit) * size + jnp.where(self.chip_bit == 0, rows, swapped)

        return one_hot((size, total), wanted)

    def beside(self, weights, tap):
        return jnp.concatenate([weights[self.taps[tap], b] for b in range(3)], axis=1)

    def stacked(self, weights, tap):
        return jnp.concatenate([weights[self.taps[tap], b] for b in range(3)], axis=0)


def side(total, width, sign):
    left = moved(total[:, :width], -sign)
    right = moved(total[:, 2 * width :], sign)
    return left + total[:, width : 2 * width] + right


def spread(values):
    return jnp.concatenate(
        [moved(values, 1).astype(BF), values.astype(BF), moved(values, -1).astype(BF)], axis=1
    )


def middle_kernel(far, near, own, mate, mate1, first_kernel, second_kernel, near_out, own_out, mate_out):
    place = Place()
    slots = (far, near, own, mate, mate1)
    first = [place.beside(first_kernel, a) for a in range(3)]
    second = [place.stacked(second_kernel, a) for a in range(3)]
    for slot, out in ((1, near_out), (2, own_out), (3, mate_out)):
        pre = side(sum(mm(slots[slot + a - 1][:, :VAL], first[a]) for a in range(3)), CONV, 1)
        back = side(sum(mm_t(slots[slot + 1 - a][:, VAL:], second[a]) for a in range(3)), CONV, -1)
        sigma = 1.0 / (1.0 + jnp.exp(-pre))
        hidden = pre * sigma
        slope = back * (sigma * (1.0 + pre * (1.0 - sigma)))
        if slot == 1:
            hidden = jnp.where(place.near_inside, hidden, 0.0)
            slope = jnp.where(place.near_inside, slope, 0.0)
        out[:, :CONV] = hidden.astype(BF)
        out[:, CONV:] = slope.astype(BF)


def conv_grads_kernel(near, own, mate, mate1, own_mid, mate_mid, keep, send):
    place = Place()
    slots = (near, own, mate, mate1)
    mids = {1: own_mid, 2: mate_mid}

    def store(total, start, step, a):
        for b in range(3):
            at = pl.ds(pl.multiple_of(start + (place.taps[a] * 3 + b) * step, step), step)
            keep[at, :] = total[:step, b * CONV : (b + 1) * CONV]
            send[at, :] = total[step:, b * CONV : (b + 1) * CONV]

    pick = place.chosen(VAL, place.core)
    attended_t = [mm_t(pick, slot[:, :VAL]).astype(BF) for slot in slots]
    slope = {slot: spread(mid[:, CONV:].astype(F32)) for slot, mid in mids.items()}
    for a in range(3):
        total = sum(mm(attended_t[slot + a - 1], slope[slot]) for slot in mids).astype(BF)
        store(total, 0, VAL // PARTS, a)
    pick = place.chosen(CONV, place.core)
    hidden_t = {slot: mm_t(pick, mid[:, :CONV]).astype(BF) for slot, mid in mids.items()}
    cotangent = [spread(slot[:, VAL:].astype(F32)) for slot in slots]
    for a in range(3):
        total = sum(mm(hidden_t[slot], cotangent[slot + 1 - a]) for slot in mids).astype(BF)
        store(total, FIRST_ROWS, CONV // PARTS, a)


def attention_backward_kernel(
    near_mid, own_mid, mate_mid, own, local, lse, first_kernel, grad_own, proj_own, proj_mate, upstream_ref, grad_t
):
    place = Place()
    across = own.shape[0]
    part_width = grad_own.shape[0]
    mids = (near_mid, own_mid, mate_mid)
    upstream_ref[...] = side(
        sum(mm_t(mids[2 - a][:, CONV:], place.stacked(first_kernel, a)) for a in range(3)), VAL, -1
    ).astype(BF)
    keys = local[:, QK : 2 * QK]
    values = local[:, 2 * QK : PACKED]
    keys_t = mm_t(identity(QK), keys).astype(BF)
    blocks = across // BLOCK
    if blocks > 1:
        grad_t[...] = jnp.zeros_like(grad_t)

    def add_rows(start, count, terms):
        if blocks > 1:
            grad_t[start : start + count, :] += terms
        else:
            grad_t[start : start + count, :] = terms

    def block(index):
        at = block_at(index)
        queries = local[at, :QK]
        upstream = upstream_ref[at, :]
        queries_t = mm_t(identity(QK), queries).astype(BF)
        upstream_t = mm_t(identity(VAL), upstream)
        products = upstream_t * mm_t(identity(VAL), own[at, :VAL])
        upstream_t = upstream_t.astype(BF)
        all_scores = mm_t(jnp.concatenate([head_of(keys, h, HEAD_QK) for h in range(HEADS)], axis=0), queries)
        all_slopes = mm_t(jnp.concatenate([head_of(values, h, HEAD_VAL) for h in range(HEADS)], axis=0), upstream)
        for head in range(HEADS):
            qk_rows = slice(head * HEAD_QK, (head + 1) * HEAD_QK)
            val_rows = slice(head * HEAD_VAL, (head + 1) * HEAD_VAL)
            scores = all_scores[head * across : (head + 1) * across, :]
            soft = jnp.exp2(scores * EXP2_SCALING - lse[head : head + 1, at])
            inner = jnp.sum(products[val_rows, :], axis=0, keepdims=True)
            slopes = all_slopes[head * across : (head + 1) * across, :]
            dscore = (soft * (slopes - inner)).astype(BF)
            grad_t[qk_rows, at] = SCALING * mm(keys_t[qk_rows, :], dscore)
            add_rows(QK + head * HEAD_QK, HEAD_QK, SCALING * mm_t(queries_t[qk_rows, :], dscore))
            add_rows(2 * QK + head * HEAD_VAL, HEAD_VAL, mm_t(upstream_t[val_rows, :], soft.astype(BF)))

    for_blocks(blocks, block)

    grad = grad_t[...].astype(BF)
    features = local[:, PACKED:]
    step = VAL // PARTS
    for target, half in ((proj_own, place.core), (proj_mate, 1 - place.core)):
        total = mm_t(mm_t(place.chosen(VAL, half), features).astype(BF), grad).astype(BF)
        for j in range(PACKED // CONV):
            target[0, j * step : (j + 1) * step, :] = total[:step, j * CONV : (j + 1) * CONV]
            target[1, j * step : (j + 1) * step, :] = total[step:, j * CONV : (j + 1) * CONV]
    own_pixels = one_hot((part_width, across), lambda rows: rows + place.col * part_width)
    grad_own[...] = mm_t(own_pixels, grad).astype(BF)


def backward_kernel(
    far,
    near,
    own,
    mate,
    mate1,
    local,
    lse,
    first_kernel,
    second_kernel,
    near_mid,
    own_mid,
    mate_mid,
    grad_own,
    keep,
    send,
    proj_own,
    proj_mate,
    upstream,
    grad_t,
):
    middle_kernel(far, near, own, mate, mate1, first_kernel, second_kernel, near_mid, own_mid, mate_mid)
    conv_grads_kernel(near, own, mate, mate1, own_mid, mate_mid, keep, send)
    attention_backward_kernel(
        near_mid, own_mid, mate_mid, own, local, lse, first_kernel, grad_own, proj_own, proj_mate, upstream, grad_t
    )


def outputs_kernel(near_mid, own_mid, mate_mid, grad_own, projection, second_kernel, output_map, input_grad, rows):
    place = Place()
    part_width = output_map.shape[0]
    mids = (near_mid, own_mid, mate_mid)
    rows[...] = side(sum(mm(mids[a][:, :CONV], place.beside(second_kernel, a)) for a in range(3)), CONV, 1)
    output_map[...] = rows[pl.ds(pl.multiple_of(place.col * part_width, part_width), part_width), :].astype(BF)
    input_grad[...] = mm_t(grad_own[...], projection[...]).astype(BF)


def unpack_kernel(factor, *refs):
    pieces = refs[:8]
    projection_grad, first_grad, second_grad = refs[8:]
    row = lax.axis_index("rows")
    core = lax.rem(row, 2)
    chip_bit = lax.rem(row // 2, 2)
    col_bit = lax.rem(lax.axis_index("cols"), 2)
    for which, piece in enumerate(pieces):
        core_flip, col_flip, chip_flip = which // 4, which // 2 % 2, which % 2
        part = (
            4 * lax.rem(core + core_flip, 2) + 2 * lax.rem(col_bit + col_flip, 2) + lax.rem(chip_bit + chip_flip, 2)
        )
        step = VAL // PARTS
        at = pl.ds(pl.multiple_of(part * step, step), step)
        for tap in range(9):
            first_grad[tap // 3, tap % 3, at, :] = piece[tap * step : (tap + 1) * step, :].astype(F32) * factor
        start = FIRST_ROWS + SECOND_ROWS
        for j in range(PACKED // CONV):
            projection_grad[at, j * CONV : (j + 1) * CONV] = (
                piece[start + j * step : start + (j + 1) * step, :].astype(F32) * factor
            )
        step = CONV // PARTS
        at = pl.ds(pl.multiple_of(part * step, step), step)
        for tap in range(9):
            begin = FIRST_ROWS + tap * step
            second_grad[tap // 3, tap % 3, at, :] = piece[begin : begin + step, :].astype(F32) * factor


def shape(*dims, dtype=BF):
    return jax.ShapeDtypeStruct(dims, dtype)


def granted(across):
    return dict(compiler_params=pltpu.CompilerParams(vmem_limit_bytes=across * 64 * 1024))


VMEM = pl.BlockSpec(memory_space=pltpu.VMEM)
HBM = pl.BlockSpec(memory_space=pltpu.HBM)


def body(features, projection, first_kernel, second_kernel, cotangent):
    height, part_width, channels = features.shape
    rows_size = lax.axis_size("rows")
    cols_size = lax.axis_size("cols")
    across = part_width * cols_size

    def rows_flip(values, bit):
        return lax.ppermute(values, "rows", [(i, i ^ bit) for i in range(rows_size)])

    def cols_flip(values):
        return lax.ppermute(values, "cols", [(i, i ^ 1) for i in range(cols_size)])

    def wide(values):
        return values.astype(F32)

    def added(one, two):
        return (one + two).astype(BF)

    def call(kernel, out_shape, operands, scratch=(), name=None):
        return pl.pallas_call(
            kernel,
            out_shape=out_shape,
            in_specs=[VMEM] * len(operands),
            out_specs=[VMEM] * len(out_shape),
            scratch_shapes=scratch,
            cost_estimate=pl.CostEstimate(flops=10**9, bytes_accessed=4 * 1024 * 1024, transcendentals=0),
            name=name,
            **granted(across),
        )(*operands)

    given = (features, cotangent)
    projection, features, cotangent = fetch((projection, features[0], cotangent[0]))
    if cols_size == 2:
        pieces = (features, cols_flip(given[0][0]), cotangent, cols_flip(given[1][0]))
    else:
        pieces = tuple(lax.all_gather(array[0], "cols", axis=0, tiled=True) for array in given)
    own, local, lse = call(
        functools.partial(forward_kernel, cols_size != 2),
        (
            shape(across, VAL + CONV),
            shape(across, PACKED + channels),
            shape(HEADS, across, dtype=F32),
        ),
        (*pieces, projection),
        (pltpu.VMEM((VAL, across), BF),),
        name="attention_forward",
    )

    first_kernel, second_kernel = fetch((first_kernel, second_kernel), (lse,))
    near = [(i, i + 1) for i in range(1, rows_size - 1, 2)] + [(i + 1, i) for i in range(1, rows_size - 1, 2)]
    far = [(i, i + 2) for i in range(0, rows_size - 2, 2)] + [(i, i - 2) for i in range(3, rows_size, 2)]
    near1 = lax.ppermute(own, "rows", near)
    near2 = lax.ppermute(own, "rows", far)
    mate = rows_flip(own, 1)
    mate1 = rows_flip(near1, 1)
    near_mid, own_mid, mate_mid, grad_own, keep, send, proj_own, proj_mate = call(
        backward_kernel,
        (
            shape(across, 2 * CONV),
            shape(across, 2 * CONV),
            shape(across, 2 * CONV),
            shape(part_width, PACKED),
            shape(FIRST_ROWS + SECOND_ROWS, CONV),
            shape(FIRST_ROWS + SECOND_ROWS, CONV),
            shape(2, PROJ_ROWS, CONV),
            shape(2, PROJ_ROWS, CONV),
        ),
        (near2, near1, own, mate, mate1, local, lse, first_kernel, second_kernel),
        (pltpu.VMEM((across, VAL), BF), pltpu.VMEM((PACKED, across), F32)),
        name="block_backward",
    )
    output_map, input_grad = call(
        outputs_kernel,
        (shape(part_width, CONV), shape(part_width, channels)),
        (near_mid, own_mid, mate_mid, grad_own, projection, second_kernel),
        (pltpu.VMEM((across, CONV), F32),),
        name="outputs",
    )
    proj_sum = added(wide(proj_own), wide(rows_flip(proj_mate, 1)))
    sent = jnp.concatenate([send, proj_sum[1]], axis=0)
    kept = jnp.concatenate([keep, proj_sum[0]], axis=0)
    if rows_size > 4:
        total = added(wide(kept) + wide(rows_flip(kept, 4)), wide(rows_flip(sent, 2)) + wide(rows_flip(sent, 6)))
    else:
        total = added(wide(kept), wide(rows_flip(sent, 2)))
    bit = 8
    while bit < rows_size:
        total = added(wide(total), wide(rows_flip(total, bit)))
        bit *= 2
    chip = rows_flip(total, 2)
    side = cols_flip(total)
    corner = lax.ppermute(
        total,
        ("rows", "cols"),
        [(i * cols_size + j, (i ^ 2) * cols_size + (j ^ 1)) for i in range(rows_size) for j in range(cols_size)],
    )
    four = (total, chip, side, corner)
    eight = four + tuple(rows_flip(piece, 1) for piece in four)
    factor = 1.0 / math.sqrt(height * across * rows_size)
    projection_grad, first_grad, second_grad = call(
        functools.partial(unpack_kernel, factor),
        (
            shape(channels, PACKED, dtype=F32),
            shape(3, 3, VAL, CONV, dtype=F32),
            shape(3, 3, CONV, CONV, dtype=F32),
        ),
        eight,
        name="unpack_sums",
    )
    return (output_map[None], input_grad[None], projection_grad, first_grad, second_grad)


def solution(mesh):
    placed = (P("rows", "cols", None), P(), P(), P(), P("rows", "cols", None))
    return jax.shard_map(
        body,
        mesh=mesh,
        in_specs=placed,
        out_specs=(P("rows", "cols", None), P("rows", "cols", None), P(), P(), P()),
        check_vma=False,
    )
```

```python
import functools
import math

import jax
import jax.numpy as jnp
from jax import lax
from jax.experimental import pallas as pl
from jax.experimental.pallas import tpu as pltpu
from jax.sharding import PartitionSpec as P

QK = 128
VAL = 256
HEADS = 8
CONV = 128
HEAD_QK = QK // HEADS
HEAD_VAL = VAL // HEADS
PACKED = 2 * QK + VAL
BLOCK = 256
BF = jnp.bfloat16
F32 = jnp.float32
SCALING = HEAD_QK ** (-0.5)
EXP2_SCALING = SCALING * math.log2(math.e)

PARTS = 8
FIRST_ROWS = 9 * VAL // PARTS
SECOND_ROWS = 9 * CONV // PARTS
CONV_ROWS = FIRST_ROWS + SECOND_ROWS
PROJ_ROWS = PACKED // CONV * (VAL // PARTS)


def mm(a, b):
    return lax.dot_general(a, b, (((1,), (0,)), ((), ())), preferred_element_type=F32)


def mm_t(a, b):
    return lax.dot_general(a, b, (((1,), (1,)), ((), ())), preferred_element_type=F32)


def one_hot(shape, wanted):
    rows = lax.broadcasted_iota(jnp.int32, shape, 0)
    columns = lax.broadcasted_iota(jnp.int32, shape, 1)
    return jnp.where(columns == wanted(rows), 1.0, 0.0).astype(BF)


def identity(size):
    return one_hot((size, size), lambda rows: rows)


def head_of(values, head, width):
    lanes = lax.broadcasted_iota(jnp.int32, values.shape, 1)
    return jnp.where(lanes // width == head, values, jnp.zeros_like(values))


def moved(values, step):
    count = values.shape[0]
    turned = pltpu.roll(values, (-step) % count, 0)
    at = lax.broadcasted_iota(jnp.int32, values.shape, 0)
    return jnp.where(at == (count - 1 if step > 0 else 0), 0.0, turned)


def for_blocks(count, run):
    if count == 1:
        run(0)
    else:
        lax.fori_loop(0, count, lambda i, carry: (run(i), carry)[1], 0)


def block_at(index):
    return pl.ds(index if isinstance(index, int) else pl.multiple_of(index * BLOCK, BLOCK), BLOCK)


def fetch_kernel(count, *refs):
    targets = refs[-1 - count : -1]
    copies = [pltpu.make_async_copy(refs[i], targets[i], refs[-1].at[i]) for i in range(count)]
    for copy in copies:
        copy.start()
    for copy in copies:
        copy.wait()


def fetch(arrays, after=()):
    return pl.pallas_call(
        functools.partial(fetch_kernel, len(arrays)),
        out_shape=tuple(shape(*array.shape) for array in arrays),
        in_specs=[HBM] * (len(arrays) + len(after)),
        out_specs=[VMEM] * len(arrays),
        scratch_shapes=[pltpu.SemaphoreType.DMA((len(arrays),))],
        cost_estimate=pl.CostEstimate(flops=0, bytes_accessed=4 * 1024 * 1024, transcendentals=0),
        name="fetch",
        **granted(32),
    )(*arrays, *after)


def forward_kernel(whole, *refs):
    count = 1 if whole else 2
    features = refs[:count]
    cotangent = refs[count : 2 * count]
    projection, comb, local, lse, values_t = refs[2 * count :]
    across = comb.shape[0]
    for which in range(count):
        width = features[which].shape[0]
        if whole:
            at = pl.ds(0, width)
        else:
            place = lax.rem(lax.axis_index("cols") + which, 2)
            at = pl.ds(pl.multiple_of(place * width, width), width)
        local[at, PACKED:] = features[which][...]
        comb[at, VAL:] = cotangent[which][...]
    packed = mm(local[:, PACKED:], projection[...]).astype(BF)
    local[:, :PACKED] = packed
    keys = packed[:, QK : 2 * QK]
    values_t[...] = mm_t(identity(VAL), packed[:, 2 * QK :]).astype(BF)

    def block(index):
        at = block_at(index)
        queries = local[at, :QK]
        rows = []
        all_scores = mm_t(jnp.concatenate([head_of(keys, h, HEAD_QK) for h in range(HEADS)], axis=0), queries)
        for head in range(HEADS):
            scores = all_scores[head * across : (head + 1) * across, :]
            maxima = jnp.max(scores, axis=0, keepdims=True)
            exponent = jnp.exp2((scores - maxima) * EXP2_SCALING)
            totals = jnp.sum(exponent, axis=0, keepdims=True)
            weighted = mm(values_t[head * HEAD_VAL : (head + 1) * HEAD_VAL, :], exponent.astype(BF))
            rows.append((weighted * (1.0 / totals)).astype(BF))
            lse[head : head + 1, at] = maxima * EXP2_SCALING + jnp.log2(totals)
        comb[at, :VAL] = mm_t(identity(BLOCK), jnp.concatenate(rows, axis=0)).astype(BF)

    for_blocks(across // BLOCK, block)


class Place:
    def __init__(self):
        row = lax.axis_index("rows")
        self.col = lax.axis_index("cols")
        self.core = lax.rem(row, 2)
        self.chip_bit = lax.rem(row // 2, 2)
        self.col_bit = lax.rem(self.col, 2)
        self.near_inside = jnp.where(self.core == 0, row > 0, row < lax.axis_size("rows") - 1)
        self.mate_inside = jnp.where(self.core == 0, row < lax.axis_size("rows") - 2, row > 1)
        self.taps = [tap + self.core * (2 - 2 * tap) for tap in range(3)]

    def chosen(self, total, half):
        size = total // 4
        middle = size // 2

        def wanted(rows):
            swapped = jnp.where(rows < middle, rows + middle, rows - middle)
            return (2 * half + self.col_bit) * size + jnp.where(self.chip_bit == 0, rows, swapped)

        return one_hot((size, total), wanted)

    def beside(self, weights, tap):
        return jnp.concatenate([weights[self.taps[tap], b] for b in range(3)], axis=1)

    def stacked(self, weights, tap):
        return jnp.concatenate([weights[self.taps[tap], b] for b in range(3)], axis=0)


def side(total, width, sign):
    left = moved(total[:, :width], -sign)
    right = moved(total[:, 2 * width :], sign)
    return left + total[:, width : 2 * width] + right


def spread(values):
    return jnp.concatenate(
        [moved(values, 1).astype(BF), values.astype(BF), moved(values, -1).astype(BF)], axis=1
    )


def prepare_kernel(own, local, lse, soft, keys_t, queries_t, attended_t, features_t):
    place = Place()
    across = own.shape[0]
    keys = local[:, QK : 2 * QK]
    keys_t[...] = mm_t(identity(QK), keys).astype(BF)
    pick = jnp.concatenate([place.chosen(VAL, place.core), place.chosen(VAL, 1 - place.core)], axis=0)
    features_t[...] = mm_t(pick, local[:, PACKED:]).astype(BF)

    def block(index):
        at = block_at(index)
        queries = local[at, :QK]
        queries_t[:, at] = mm_t(identity(QK), queries).astype(BF)
        attended_t[:, at] = mm_t(identity(VAL), own[at, :VAL]).astype(BF)
        scores = mm_t(jnp.concatenate([head_of(keys, h, HEAD_QK) for h in range(HEADS)], axis=0), queries)
        for head in range(HEADS):
            rows = slice(head * across, (head + 1) * across)
            soft[rows, at] = jnp.exp2(scores[rows, :] * EXP2_SCALING - lse[head : head + 1, at]).astype(BF)

    for_blocks(across // BLOCK, block)


def masked(inside, row):
    return jnp.where(inside, row, jnp.zeros_like(row))


def middle(place, slots, first_kernel, second_kernel, outs):
    first = [place.beside(first_kernel, a) for a in range(3)]
    second = [place.stacked(second_kernel, a) for a in range(3)]
    for slot, out in enumerate(outs, 1):
        pre = side(sum(mm(slots[slot + a - 1][:, :VAL], first[a]) for a in range(3)), CONV, 1)
        back = side(sum(mm_t(slots[slot + 1 - a][:, VAL:], second[a]) for a in range(3)), CONV, -1)
        sigma = 1.0 / (1.0 + jnp.exp(-pre))
        hidden = pre * sigma
        slope = back * (sigma * (1.0 + pre * (1.0 - sigma)))
        if slot == 1:
            hidden = masked(place.near_inside, hidden)
            slope = masked(place.near_inside, slope)
        out[:, :CONV] = hidden.astype(BF)
        out[:, CONV:] = slope.astype(BF)


def conv_grads_kernel(near, own, mate, mate1, own_mid, mate_mid, keep, send):
    place = Place()
    slots = (masked(place.near_inside, near[...]), own[...], mate[...], masked(place.mate_inside, mate1[...]))
    mids = {1: own_mid, 2: mate_mid}

    def store(total, start, step, a):
        for b in range(3):
            at = pl.ds(pl.multiple_of(start + (place.taps[a] * 3 + b) * step, step), step)
            keep[at, :] = total[:step, b * CONV : (b + 1) * CONV]
            send[at, :] = total[step:, b * CONV : (b + 1) * CONV]

    pick = place.chosen(VAL, place.core)
    attended_t = [mm_t(pick, slot[:, :VAL]).astype(BF) for slot in slots]
    slope = {slot: spread(mid[:, CONV:].astype(F32)) for slot, mid in mids.items()}
    for a in range(3):
        total = sum(mm(attended_t[slot + a - 1], slope[slot]) for slot in mids).astype(BF)
        store(total, 0, VAL // PARTS, a)
    pick = place.chosen(CONV, place.core)
    hidden_t = {slot: mm_t(pick, mid[:, :CONV]).astype(BF) for slot, mid in mids.items()}
    cotangent = [spread(slot[:, VAL:].astype(F32)) for slot in slots]
    for a in range(3):
        total = sum(mm(hidden_t[slot], cotangent[slot + 1 - a]) for slot in mids).astype(BF)
        store(total, FIRST_ROWS, CONV // PARTS, a)


def backward_kernel(
    far,
    near,
    own,
    mate,
    mate1,
    local,
    soft,
    keys_t,
    queries_t,
    attended_t,
    features_t,
    first_kernel,
    second_kernel,
    near_mid,
    own_mid,
    mate_mid,
    grad_own,
    proj_own,
    proj_mate,
    upstream_ref,
    grad_t,
):
    place = Place()
    across = own.shape[0]
    part_width = grad_own.shape[0]
    slots = (far[...], masked(place.near_inside, near[...]), own[...], mate[...], masked(place.mate_inside, mate1[...]))
    mids = (near_mid, own_mid, mate_mid)
    middle(place, slots, first_kernel, second_kernel, mids)
    upstream_ref[...] = side(
        sum(mm_t(mids[2 - a][:, CONV:], place.stacked(first_kernel, a)) for a in range(3)), VAL, -1
    ).astype(BF)
    values = local[:, 2 * QK : PACKED]
    blocks = across // BLOCK
    if blocks > 1:
        grad_t[...] = jnp.zeros_like(grad_t)

    def add_rows(start, count, terms):
        if blocks > 1:
            grad_t[start : start + count, :] += terms
        else:
            grad_t[start : start + count, :] = terms

    def block(index):
        at = block_at(index)
        upstream = upstream_ref[at, :]
        upstream_t = mm_t(identity(VAL), upstream)
        products = upstream_t * attended_t[:, at].astype(F32)
        upstream_t = upstream_t.astype(BF)
        slopes = mm_t(jnp.concatenate([head_of(values, h, HEAD_VAL) for h in range(HEADS)], axis=0), upstream)
        for head in range(HEADS):
            rows = slice(head * across, (head + 1) * across)
            qk_rows = slice(head * HEAD_QK, (head + 1) * HEAD_QK)
            val_rows = slice(head * HEAD_VAL, (head + 1) * HEAD_VAL)
            weights = soft[rows, at]
            inner = jnp.sum(products[val_rows, :], axis=0, keepdims=True)
            dscore = (weights.astype(F32) * (slopes[rows, :] - inner)).astype(BF)
            grad_t[qk_rows, at] = SCALING * mm(keys_t[qk_rows, :], dscore)
            add_rows(QK + head * HEAD_QK, HEAD_QK, SCALING * mm_t(queries_t[qk_rows, at], dscore))
            add_rows(2 * QK + head * HEAD_VAL, HEAD_VAL, mm_t(upstream_t[val_rows, :], weights))

    for_blocks(blocks, block)

    grad = grad_t[...].astype(BF)
    step = VAL // PARTS
    total = mm_t(features_t[...], grad).astype(BF)
    for which, target in enumerate((proj_own, proj_mate)):
        for j in range(PACKED // CONV):
            for part in range(2):
                begin = (2 * which + part) * step
                target[part, j * step : (j + 1) * step, :] = total[begin : begin + step, j * CONV : (j + 1) * CONV]
    own_pixels = one_hot((part_width, across), lambda rows: rows + place.col * part_width)
    grad_own[...] = mm_t(own_pixels, grad).astype(BF)


def outputs_kernel(near_mid, own_mid, mate_mid, grad_own, projection, second_kernel, output_map, input_grad, rows):
    place = Place()
    part_width = output_map.shape[0]
    mids = (near_mid, own_mid, mate_mid)
    rows[...] = side(sum(mm(mids[a][:, :CONV], place.beside(second_kernel, a)) for a in range(3)), CONV, 1)
    output_map[...] = rows[pl.ds(pl.multiple_of(place.col * part_width, part_width), part_width), :].astype(BF)
    input_grad[...] = mm_t(grad_own[...], projection[...]).astype(BF)


def unpack_kernel(factor, core_flip, *refs):
    pieces = refs[:4]
    outs = refs[-7:-4]
    blocks = refs[-4:-1]
    sem = refs[-1]
    projection_block, first_block, second_block = blocks
    row = lax.axis_index("rows")
    half = lax.rem(row + core_flip, 2)
    chip_bit = lax.rem(row // 2, 2)
    col_bit = lax.rem(lax.axis_index("cols"), 2)
    parts = [2 * lax.rem(col_bit + which // 2, 2) + lax.rem(chip_bit + which % 2, 2) for which in range(4)]
    copies = []

    def send(index, block, out):
        copies.append(pltpu.make_async_copy(block, out, sem.at[index]))
        copies[-1].start()

    def rows_of(which, step):
        return pl.ds(pl.multiple_of(parts[which] * step, step), step)

    def half_of(rows):
        return pl.ds(pl.multiple_of(half * rows, rows), rows)

    step = VAL // PARTS
    for a in range(3):
        for which, piece in enumerate(pieces):
            for b in range(3):
                begin = (3 * a + b) * step
                first_block[a, b, rows_of(which, step), :] = piece[begin : begin + step, :].astype(F32) * factor
        send(a, first_block.at[a], outs[1].at[a, :, half_of(VAL // 2), :])
    for which, piece in enumerate(pieces):
        for j in range(PACKED // CONV):
            begin = FIRST_ROWS + SECOND_ROWS + j * step
            projection_block[rows_of(which, step), j * CONV : (j + 1) * CONV] = (
                piece[begin : begin + step, :].astype(F32) * factor
            )
    send(3, projection_block, outs[0].at[half_of(VAL // 2), :])
    step = CONV // PARTS
    for which, piece in enumerate(pieces):
        for tap in range(9):
            begin = FIRST_ROWS + tap * step
            second_block[tap // 3, tap % 3, rows_of(which, step), :] = (
                piece[begin : begin + step, :].astype(F32) * factor
            )
    send(4, second_block, outs[2].at[:, :, half_of(CONV // 2), :])
    for copy in copies:
        copy.wait()


def unpack(factor, core_flip, pieces, into, **params):
    dims = ((2 * QK, PACKED), (3, 3, VAL, CONV), (3, 3, CONV, CONV))
    return pl.pallas_call(
        functools.partial(unpack_kernel, factor, core_flip),
        out_shape=tuple(shape(*size, dtype=F32) for size in dims),
        in_specs=[VMEM] * 4 + [HBM] * len(into),
        out_specs=[HBM] * 3,
        scratch_shapes=[pltpu.VMEM(size[:-2] + (size[-2] // 2, size[-1]), F32) for size in dims]
        + [pltpu.SemaphoreType.DMA((5,))],
        input_output_aliases={4 + i: i for i in range(len(into))},
        cost_estimate=pl.CostEstimate(flops=10**9, bytes_accessed=4 * 1024 * 1024, transcendentals=0),
        name="unpack_sums",
        **params,
    )(*pieces, *into)


def shape(*dims, dtype=BF):
    return jax.ShapeDtypeStruct(dims, dtype)


def granted(across):
    return dict(compiler_params=pltpu.CompilerParams(vmem_limit_bytes=across * 64 * 1024))


VMEM = pl.BlockSpec(memory_space=pltpu.VMEM)
HBM = pl.BlockSpec(memory_space=pltpu.HBM)


def body(features, projection, first_kernel, second_kernel, cotangent):
    height, part_width, channels = features.shape
    rows_size = lax.axis_size("rows")
    cols_size = lax.axis_size("cols")
    across = part_width * cols_size

    def rows_flip(values, bit):
        return lax.ppermute(values, "rows", [(i, i ^ bit) for i in range(rows_size)])

    def cols_flip(values):
        return lax.ppermute(values, "cols", [(i, i ^ 1) for i in range(cols_size)])

    def wide(values):
        return values.astype(F32)

    def added(one, two):
        return (one + two).astype(BF)

    def call(kernel, out_shape, operands, scratch=(), name=None):
        return pl.pallas_call(
            kernel,
            out_shape=out_shape,
            in_specs=[VMEM] * len(operands),
            out_specs=[VMEM] * len(out_shape),
            scratch_shapes=scratch,
            cost_estimate=pl.CostEstimate(flops=10**9, bytes_accessed=4 * 1024 * 1024, transcendentals=0),
            name=name,
            **granted(across),
        )(*operands)

    given = (features, cotangent)
    projection, features, cotangent = fetch((projection, features[0], cotangent[0]))
    if cols_size == 2:
        pieces = (features, cols_flip(given[0][0]), cotangent, cols_flip(given[1][0]))
    else:
        pieces = tuple(lax.all_gather(array[0], "cols", axis=0, tiled=True) for array in given)
    own, local, lse = call(
        functools.partial(forward_kernel, cols_size != 2),
        (
            shape(across, VAL + CONV),
            shape(across, PACKED + channels),
            shape(HEADS, across, dtype=F32),
        ),
        (*pieces, projection),
        (pltpu.VMEM((VAL, across), BF),),
        name="attention_forward",
    )

    first_kernel, second_kernel = fetch((first_kernel, second_kernel), (lse,))
    last = rows_size - 1
    out = [(i, i + 2) for i in range(0, last - 1, 2)] + [(i, i - 2) for i in range(3, rows_size, 2)]
    out += [(last - 1, last), (1, 0)]
    back = [(j, i) for i, j in out]
    mate1 = lax.ppermute(own, "rows", back)
    far = lax.ppermute(own, "rows", out)
    mate = rows_flip(own, 1)
    near = rows_flip(mate1, 1)
    soft, keys_t, queries_t, attended_t, features_t = call(
        prepare_kernel,
        (
            shape(HEADS * across, across),
            shape(QK, across),
            shape(QK, across),
            shape(VAL, across),
            shape(VAL // 2, across),
        ),
        (own, local, lse),
        name="prepare",
    )
    near_mid, own_mid, mate_mid, grad_own, proj_own, proj_mate = call(
        backward_kernel,
        (
            shape(across, 2 * CONV),
            shape(across, 2 * CONV),
            shape(across, 2 * CONV),
            shape(part_width, PACKED),
            shape(2, PROJ_ROWS, CONV),
            shape(2, PROJ_ROWS, CONV),
        ),
        (
            far,
            near,
            own,
            mate,
            mate1,
            local,
            soft,
            keys_t,
            queries_t,
            attended_t,
            features_t,
            first_kernel,
            second_kernel,
        ),
        (pltpu.VMEM((across, VAL), BF), pltpu.VMEM((PACKED, across), F32)),
        name="block_backward",
    )
    keep, send = call(
        conv_grads_kernel,
        (shape(FIRST_ROWS + SECOND_ROWS, CONV),) * 2,
        (near, own, mate, mate1, own_mid, mate_mid),
        name="conv_grads",
    )
    output_map, input_grad = call(
        outputs_kernel,
        (shape(part_width, CONV), shape(part_width, channels)),
        (near_mid, own_mid, mate_mid, grad_own, projection, second_kernel),
        (pltpu.VMEM((across, CONV), F32),),
        name="outputs",
    )
    proj_sum = added(wide(proj_own), wide(rows_flip(proj_mate, 1)))
    sent = jnp.concatenate([send, proj_sum[1]], axis=0)
    kept = jnp.concatenate([keep, proj_sum[0]], axis=0)
    if rows_size > 4:
        total = added(wide(kept) + wide(rows_flip(kept, 4)), wide(rows_flip(sent, 2)) + wide(rows_flip(sent, 6)))
    else:
        total = added(wide(kept), wide(rows_flip(sent, 2)))
    bit = 8
    while bit < rows_size:
        total = added(wide(total), wide(rows_flip(total, bit)))
        bit *= 2
    total, output_map, input_grad = lax.optimization_barrier((total, output_map, input_grad))
    chip = rows_flip(total, 2)
    side = cols_flip(total)
    corner = lax.ppermute(
        total,
        ("rows", "cols"),
        [(i * cols_size + j, (i ^ 2) * cols_size + (j ^ 1)) for i in range(rows_size) for j in range(cols_size)],
    )
    four = (total, chip, side, corner)
    factor = 1.0 / math.sqrt(height * across * rows_size)
    halves = unpack(factor, 0, four, (), **granted(across))
    projection_grad, first_grad, second_grad = unpack(
        factor, 1, [rows_flip(piece, 1) for piece in four], halves, **granted(across)
    )
    return (output_map[None], input_grad[None], projection_grad, first_grad, second_grad)


def solution(mesh):
    placed = (P("rows", "cols", None), P(), P(), P(), P("rows", "cols", None))
    return jax.shard_map(
        body,
        mesh=mesh,
        in_specs=placed,
        out_specs=(P("rows", "cols", None), P("rows", "cols", None), P(), P(), P()),
        check_vma=False,
    )
```

```python
import functools
import math

import jax
import jax.numpy as jnp
from jax import lax
from jax.experimental import pallas as pl
from jax.experimental.pallas import tpu as pltpu
from jax.sharding import PartitionSpec as P

QK = 128
VAL = 256
HEADS = 8
CONV = 128
HEAD_QK = QK // HEADS
HEAD_VAL = VAL // HEADS
PACKED = 2 * QK + VAL
BLOCK = 256
BF = jnp.bfloat16
F32 = jnp.float32
SCALING = HEAD_QK ** (-0.5)
EXP2_SCALING = SCALING * math.log2(math.e)

PARTS = 8
FIRST_ROWS = 9 * VAL // PARTS
SECOND_ROWS = 9 * CONV // PARTS
CONV_ROWS = FIRST_ROWS + SECOND_ROWS
PROJ_ROWS = PACKED // CONV * (VAL // PARTS)


def mm(a, b):
    return lax.dot_general(a, b, (((1,), (0,)), ((), ())), preferred_element_type=F32)


def mm_t(a, b):
    return lax.dot_general(a, b, (((1,), (1,)), ((), ())), preferred_element_type=F32)


def one_hot(shape, wanted):
    rows = lax.broadcasted_iota(jnp.int32, shape, 0)
    columns = lax.broadcasted_iota(jnp.int32, shape, 1)
    return jnp.where(columns == wanted(rows), 1.0, 0.0).astype(BF)


def identity(size):
    return one_hot((size, size), lambda rows: rows)


def head_of(values, head, width):
    lanes = lax.broadcasted_iota(jnp.int32, values.shape, 1)
    return jnp.where(lanes // width == head, values, jnp.zeros_like(values))


def moved(values, step):
    count = values.shape[0]
    turned = pltpu.roll(values, (-step) % count, 0)
    at = lax.broadcasted_iota(jnp.int32, values.shape, 0)
    return jnp.where(at == (count - 1 if step > 0 else 0), 0.0, turned)


def for_blocks(count, run):
    if count == 1:
        run(0)
    else:
        lax.fori_loop(0, count, lambda i, carry: (run(i), carry)[1], 0)


def block_at(index):
    return pl.ds(index if isinstance(index, int) else pl.multiple_of(index * BLOCK, BLOCK), BLOCK)


def fetch_kernel(count, *refs):
    targets = refs[-1 - count : -1]
    copies = [pltpu.make_async_copy(refs[i], targets[i], refs[-1].at[i]) for i in range(count)]
    for copy in copies:
        copy.start()
    for copy in copies:
        copy.wait()


def fetch(arrays, after=(), nbytes=4 * 1024 * 1024):
    return pl.pallas_call(
        functools.partial(fetch_kernel, len(arrays)),
        out_shape=tuple(shape(*array.shape) for array in arrays),
        in_specs=[HBM] * (len(arrays) + len(after)),
        out_specs=[VMEM] * len(arrays),
        scratch_shapes=[pltpu.SemaphoreType.DMA((len(arrays),))],
        cost_estimate=pl.CostEstimate(flops=0, bytes_accessed=nbytes, transcendentals=0),
        name="fetch",
        **granted(32),
    )(*arrays, *after)


def forward_kernel(whole, *refs):
    count = 1 if whole else 2
    features = refs[:count]
    cotangent = refs[count : 2 * count]
    projection, comb, local, lse, values_t = refs[2 * count :]
    across = comb.shape[0]
    for which in range(count):
        width = features[which].shape[0]
        if whole:
            at = pl.ds(0, width)
        else:
            place = lax.rem(lax.axis_index("cols") + which, 2)
            at = pl.ds(pl.multiple_of(place * width, width), width)
        local[at, PACKED:] = features[which][...]
        comb[at, VAL:] = cotangent[which][...]
    packed = mm(local[:, PACKED:], projection[...]).astype(BF)
    local[:, :PACKED] = packed
    keys = packed[:, QK : 2 * QK]
    values_t[...] = mm_t(identity(VAL), packed[:, 2 * QK :]).astype(BF)

    def block(index):
        at = block_at(index)
        queries = local[at, :QK]
        rows = []
        all_scores = mm_t(jnp.concatenate([head_of(keys, h, HEAD_QK) for h in range(HEADS)], axis=0), queries)
        for head in range(HEADS):
            scores = all_scores[head * across : (head + 1) * across, :]
            maxima = jnp.max(scores, axis=0, keepdims=True)
            exponent = jnp.exp2((scores - maxima) * EXP2_SCALING)
            totals = jnp.sum(exponent, axis=0, keepdims=True)
            weighted = mm(values_t[head * HEAD_VAL : (head + 1) * HEAD_VAL, :], exponent.astype(BF))
            rows.append((weighted * (1.0 / totals)).astype(BF))
            lse[head : head + 1, at] = maxima * EXP2_SCALING + jnp.log2(totals)
        comb[at, :VAL] = mm_t(identity(BLOCK), jnp.concatenate(rows, axis=0)).astype(BF)

    for_blocks(across // BLOCK, block)


class Place:
    def __init__(self):
        row = lax.axis_index("rows")
        self.col = lax.axis_index("cols")
        self.core = lax.rem(row, 2)
        self.chip_bit = lax.rem(row // 2, 2)
        self.col_bit = lax.rem(self.col, 2)
        self.near_inside = jnp.where(self.core == 0, row > 0, row < lax.axis_size("rows") - 1)
        self.mate_inside = jnp.where(self.core == 0, row < lax.axis_size("rows") - 2, row > 1)
        self.taps = [tap + self.core * (2 - 2 * tap) for tap in range(3)]

    def chosen(self, total, half):
        size = total // 4
        middle = size // 2

        def wanted(rows):
            swapped = jnp.where(rows < middle, rows + middle, rows - middle)
            return (2 * half + self.col_bit) * size + jnp.where(self.chip_bit == 0, rows, swapped)

        return one_hot((size, total), wanted)

    def beside(self, weights, tap):
        return jnp.concatenate([weights[self.taps[tap], b] for b in range(3)], axis=1)

    def stacked(self, weights, tap):
        return jnp.concatenate([weights[self.taps[tap], b] for b in range(3)], axis=0)


def side(total, width, sign):
    left = moved(total[:, :width], -sign)
    right = moved(total[:, 2 * width :], sign)
    return left + total[:, width : 2 * width] + right


def spread(values):
    return jnp.concatenate(
        [moved(values, 1).astype(BF), values.astype(BF), moved(values, -1).astype(BF)], axis=1
    )


def far_term_kernel(own, first_kernel, term):
    term[:, :CONV] = side(mm(own[:, :VAL], Place().beside(first_kernel, 0)), CONV, 1).astype(BF)
    term[:, CONV:] = own[:, VAL:]


def far_back_kernel(far, second_kernel, out):
    back = side(mm_t(far[:, CONV:], Place().stacked(second_kernel, 2)), CONV, -1)
    out[:, :CONV] = far[:, :CONV].astype(F32)
    out[:, CONV:] = back


def prepare_kernel(own, local, lse, soft, keys_t, queries_t, attended_t, features_t):
    place = Place()
    across = own.shape[0]
    keys = local[:, QK : 2 * QK]
    keys_t[...] = mm_t(identity(QK), keys).astype(BF)
    pick = jnp.concatenate([place.chosen(VAL, place.core), place.chosen(VAL, 1 - place.core)], axis=0)
    features_t[...] = mm_t(pick, local[:, PACKED:]).astype(BF)

    def block(index):
        at = block_at(index)
        queries = local[at, :QK]
        queries_t[:, at] = mm_t(identity(QK), queries).astype(BF)
        attended_t[:, at] = mm_t(identity(VAL), own[at, :VAL]).astype(BF)
        scores = mm_t(jnp.concatenate([head_of(keys, h, HEAD_QK) for h in range(HEADS)], axis=0), queries)
        for head in range(HEADS):
            rows = slice(head * across, (head + 1) * across)
            soft[rows, at] = jnp.exp2(scores[rows, :] * EXP2_SCALING - lse[head : head + 1, at]).astype(BF)

    for_blocks(across // BLOCK, block)


def masked(inside, row):
    return jnp.where(inside, row, jnp.zeros_like(row))


def middle(place, slots, first_kernel, second_kernel, outs):
    first = [place.beside(first_kernel, a) for a in range(3)]
    second = [place.stacked(second_kernel, a) for a in range(3)]
    for slot, out in enumerate(outs, 1):
        pre = side(sum(mm(slots[slot + a - 1][:, :VAL], first[a]) for a in range(3) if slot + a > 1), CONV, 1)
        if slot == 1:
            pre = pre + slots[0][:, :CONV]
        back = side(
            sum(mm_t(slots[slot + 1 - a][:, -CONV:], second[a]) for a in range(3) if slot + 1 - a > 0), CONV, -1
        )
        if slot == 1:
            back = back + slots[0][:, CONV:]
        sigma = 1.0 / (1.0 + jnp.exp(-pre))
        hidden = pre * sigma
        slope = back * (sigma * (1.0 + pre * (1.0 - sigma)))
        if slot == 1:
            hidden = masked(place.near_inside, hidden)
            slope = masked(place.near_inside, slope)
        out[:, :CONV] = hidden.astype(BF)
        out[:, CONV:] = slope.astype(BF)


def conv_grads_kernel(near, own, mate, mate1, own_mid, mate_mid, keep, send):
    place = Place()
    slots = (masked(place.near_inside, near[...]), own[...], mate[...], masked(place.mate_inside, mate1[...]))
    mids = {1: own_mid, 2: mate_mid}

    def store(total, start, step, a):
        for b in range(3):
            at = pl.ds(pl.multiple_of(start + (place.taps[a] * 3 + b) * step, step), step)
            keep[at, :] = total[:step, b * CONV : (b + 1) * CONV]
            send[at, :] = total[step:, b * CONV : (b + 1) * CONV]

    pick = place.chosen(VAL, place.core)
    attended_t = [mm_t(pick, slot[:, :VAL]).astype(BF) for slot in slots]
    slope = {slot: spread(mid[:, CONV:].astype(F32)) for slot, mid in mids.items()}
    for a in range(3):
        total = sum(mm(attended_t[slot + a - 1], slope[slot]) for slot in mids).astype(BF)
        store(total, 0, VAL // PARTS, a)
    pick = place.chosen(CONV, place.core)
    hidden_t = {slot: mm_t(pick, mid[:, :CONV]).astype(BF) for slot, mid in mids.items()}
    cotangent = [spread(slot[:, VAL:].astype(F32)) for slot in slots]
    for a in range(3):
        total = sum(mm(hidden_t[slot], cotangent[slot + 1 - a]) for slot in mids).astype(BF)
        store(total, FIRST_ROWS, CONV // PARTS, a)


def backward_kernel(
    far,
    near,
    own,
    mate,
    mate1,
    local,
    soft,
    keys_t,
    queries_t,
    attended_t,
    features_t,
    first_kernel,
    second_kernel,
    near_mid,
    own_mid,
    mate_mid,
    grad_own,
    proj_own,
    proj_mate,
    upstream_ref,
    grad_t,
):
    place = Place()
    across = own.shape[0]
    part_width = grad_own.shape[0]
    slots = (far[...], masked(place.near_inside, near[...]), own[...], mate[...], masked(place.mate_inside, mate1[...]))
    mids = (near_mid, own_mid, mate_mid)
    middle(place, slots, first_kernel, second_kernel, mids)
    upstream_ref[...] = side(
        sum(mm_t(mids[2 - a][:, CONV:], place.stacked(first_kernel, a)) for a in range(3)), VAL, -1
    ).astype(BF)
    values = local[:, 2 * QK : PACKED]
    blocks = across // BLOCK
    if blocks > 1:
        grad_t[...] = jnp.zeros_like(grad_t)

    def add_rows(start, count, terms):
        if blocks > 1:
            grad_t[start : start + count, :] += terms
        else:
            grad_t[start : start + count, :] = terms

    def block(index):
        at = block_at(index)
        upstream = upstream_ref[at, :]
        upstream_t = mm_t(identity(VAL), upstream)
        products = upstream_t * attended_t[:, at].astype(F32)
        upstream_t = upstream_t.astype(BF)
        slopes = mm_t(jnp.concatenate([head_of(values, h, HEAD_VAL) for h in range(HEADS)], axis=0), upstream)
        for head in range(HEADS):
            rows = slice(head * across, (head + 1) * across)
            qk_rows = slice(head * HEAD_QK, (head + 1) * HEAD_QK)
            val_rows = slice(head * HEAD_VAL, (head + 1) * HEAD_VAL)
            weights = soft[rows, at]
            inner = jnp.sum(products[val_rows, :], axis=0, keepdims=True)
            dscore = (weights.astype(F32) * (slopes[rows, :] - inner)).astype(BF)
            grad_t[qk_rows, at] = SCALING * mm(keys_t[qk_rows, :], dscore)
            add_rows(QK + head * HEAD_QK, HEAD_QK, SCALING * mm_t(queries_t[qk_rows, at], dscore))
            add_rows(2 * QK + head * HEAD_VAL, HEAD_VAL, mm_t(upstream_t[val_rows, :], weights))

    for_blocks(blocks, block)

    grad = grad_t[...].astype(BF)
    step = VAL // PARTS
    total = mm_t(features_t[...], grad).astype(BF)
    for which, target in enumerate((proj_own, proj_mate)):
        for j in range(PACKED // CONV):
            for part in range(2):
                begin = (2 * which + part) * step
                target[part, j * step : (j + 1) * step, :] = total[begin : begin + step, j * CONV : (j + 1) * CONV]
    own_pixels = one_hot((part_width, across), lambda rows: rows + place.col * part_width)
    grad_own[...] = mm_t(own_pixels, grad).astype(BF)


def outputs_kernel(near_mid, own_mid, mate_mid, grad_own, projection, second_kernel, output_map, input_grad, rows):
    place = Place()
    part_width = output_map.shape[0]
    mids = (near_mid, own_mid, mate_mid)
    rows[...] = side(sum(mm(mids[a][:, :CONV], place.beside(second_kernel, a)) for a in range(3)), CONV, 1)
    output_map[...] = rows[pl.ds(pl.multiple_of(place.col * part_width, part_width), part_width), :].astype(BF)
    input_grad[...] = mm_t(grad_own[...], projection[...]).astype(BF)


def unpack_kernel(factor, core_flip, *refs):
    pieces = refs[:4]
    outs = refs[-7:-4]
    blocks = refs[-4:-1]
    sem = refs[-1]
    projection_block, first_block, second_block = blocks
    row = lax.axis_index("rows")
    half = lax.rem(row + core_flip, 2)
    chip_bit = lax.rem(row // 2, 2)
    col_bit = lax.rem(lax.axis_index("cols"), 2)
    parts = [2 * lax.rem(col_bit + which // 2, 2) + lax.rem(chip_bit + which % 2, 2) for which in range(4)]
    copies = []

    def send(index, block, out):
        copies.append(pltpu.make_async_copy(block, out, sem.at[index]))
        copies[-1].start()

    def rows_of(which, step):
        return pl.ds(pl.multiple_of(parts[which] * step, step), step)

    def half_of(rows):
        return pl.ds(pl.multiple_of(half * rows, rows), rows)

    step = VAL // PARTS
    for a in range(3):
        for which, piece in enumerate(pieces):
            for b in range(3):
                begin = (3 * a + b) * step
                first_block[a, b, rows_of(which, step), :] = piece[begin : begin + step, :].astype(F32) * factor
        send(a, first_block.at[a], outs[1].at[a, :, half_of(VAL // 2), :])
    for which, piece in enumerate(pieces):
        for j in range(PACKED // CONV):
            begin = FIRST_ROWS + SECOND_ROWS + j * step
            projection_block[rows_of(which, step), j * CONV : (j + 1) * CONV] = (
                piece[begin : begin + step, :].astype(F32) * factor
            )
    send(3, projection_block, outs[0].at[half_of(VAL // 2), :])
    step = CONV // PARTS
    for which, piece in enumerate(pieces):
        for tap in range(9):
            begin = FIRST_ROWS + tap * step
            second_block[tap // 3, tap % 3, rows_of(which, step), :] = (
                piece[begin : begin + step, :].astype(F32) * factor
            )
    send(4, second_block, outs[2].at[:, :, half_of(CONV // 2), :])
    for copy in copies:
        copy.wait()


def unpack(factor, core_flip, pieces, into, **params):
    dims = ((2 * QK, PACKED), (3, 3, VAL, CONV), (3, 3, CONV, CONV))
    return pl.pallas_call(
        functools.partial(unpack_kernel, factor, core_flip),
        out_shape=tuple(shape(*size, dtype=F32) for size in dims),
        in_specs=[VMEM] * 4 + [HBM] * len(into),
        out_specs=[HBM] * 3,
        scratch_shapes=[pltpu.VMEM(size[:-2] + (size[-2] // 2, size[-1]), F32) for size in dims]
        + [pltpu.SemaphoreType.DMA((5,))],
        input_output_aliases={4 + i: i for i in range(len(into))},
        cost_estimate=pl.CostEstimate(flops=10**9, bytes_accessed=4 * 1024 * 1024, transcendentals=0),
        name="unpack_sums",
        **params,
    )(*pieces, *into)


def shape(*dims, dtype=BF):
    return jax.ShapeDtypeStruct(dims, dtype)


def granted(across):
    return dict(compiler_params=pltpu.CompilerParams(vmem_limit_bytes=across * 64 * 1024))


VMEM = pl.BlockSpec(memory_space=pltpu.VMEM)
HBM = pl.BlockSpec(memory_space=pltpu.HBM)


def body(features, projection, first_kernel, second_kernel, cotangent):
    height, part_width, channels = features.shape
    rows_size = lax.axis_size("rows")
    cols_size = lax.axis_size("cols")
    across = part_width * cols_size

    def rows_flip(values, bit):
        return lax.ppermute(values, "rows", [(i, i ^ bit) for i in range(rows_size)])

    def cols_flip(values):
        return lax.ppermute(values, "cols", [(i, i ^ 1) for i in range(cols_size)])

    def wide(values):
        return values.astype(F32)

    def added(one, two):
        return (one + two).astype(BF)

    def call(kernel, out_shape, operands, scratch=(), name=None, flops=10**9):
        return pl.pallas_call(
            kernel,
            out_shape=out_shape,
            in_specs=[VMEM] * len(operands),
            out_specs=[VMEM] * len(out_shape),
            scratch_shapes=scratch,
            cost_estimate=pl.CostEstimate(flops=flops, bytes_accessed=flops // 250, transcendentals=0),
            name=name,
            **granted(across),
        )(*operands)

    given = (features, cotangent)
    projection, features, cotangent = fetch((projection, features[0], cotangent[0]))
    if cols_size == 2:
        pieces = (features, cols_flip(given[0][0]), cotangent, cols_flip(given[1][0]))
    else:
        pieces = tuple(lax.all_gather(array[0], "cols", axis=0, tiled=True) for array in given)
    own, local, lse = call(
        functools.partial(forward_kernel, cols_size != 2),
        (
            shape(across, VAL + CONV),
            shape(across, PACKED + channels),
            shape(HEADS, across, dtype=F32),
        ),
        (*pieces, projection),
        (pltpu.VMEM((VAL, across), BF),),
        name="attention_forward",
    )

    given_first = first_kernel
    first_kernel, second_kernel = fetch((first_kernel, second_kernel), (lse,), 10**5)
    last = rows_size - 1
    out = [(i, i + 2) for i in range(0, last - 1, 2)] + [(i, i - 2) for i in range(3, rows_size, 2)]
    out += [(last - 1, last), (1, 0)]
    back = [(j, i) for i, j in out]
    (term,) = call(far_term_kernel, (shape(across, 2 * CONV),), (own, given_first), name="far_term")
    own, term = lax.optimization_barrier((own, term))
    mate1 = lax.ppermute(own, "rows", back)
    far = lax.ppermute(term, "rows", out)
    (far,) = call(
        far_back_kernel, (shape(across, 2 * CONV, dtype=F32),), (far, second_kernel), name="far_back", flops=4 * 10**9
    )
    mate = rows_flip(own, 1)
    near = rows_flip(mate1, 1)
    soft, keys_t, queries_t, attended_t, features_t = call(
        prepare_kernel,
        (
            shape(HEADS * across, across),
            shape(QK, across),
            shape(QK, across),
            shape(VAL, across),
            shape(VAL // 2, across),
        ),
        (own, local, lse),
        name="prepare",
        flops=10**7,
    )
    near_mid, own_mid, mate_mid, grad_own, proj_own, proj_mate = call(
        backward_kernel,
        (
            shape(across, 2 * CONV),
            shape(across, 2 * CONV),
            shape(across, 2 * CONV),
            shape(part_width, PACKED),
            shape(2, PROJ_ROWS, CONV),
            shape(2, PROJ_ROWS, CONV),
        ),
        (
            far,
            near,
            own,
            mate,
            mate1,
            local,
            soft,
            keys_t,
            queries_t,
            attended_t,
            features_t,
            first_kernel,
            second_kernel,
        ),
        (pltpu.VMEM((across, VAL), BF), pltpu.VMEM((PACKED, across), F32)),
        name="block_backward",
    )
    keep, send = call(
        conv_grads_kernel,
        (shape(FIRST_ROWS + SECOND_ROWS, CONV),) * 2,
        (near, own, mate, mate1, own_mid, mate_mid),
        name="conv_grads",
    )
    output_map, input_grad = call(
        outputs_kernel,
        (shape(part_width, CONV), shape(part_width, channels)),
        (near_mid, own_mid, mate_mid, grad_own, projection, second_kernel),
        (pltpu.VMEM((across, CONV), F32),),
        name="outputs",
    )
    proj_sum = added(wide(proj_own), wide(rows_flip(proj_mate, 1)))
    sent = jnp.concatenate([send, proj_sum[1]], axis=0)
    kept = jnp.concatenate([keep, proj_sum[0]], axis=0)
    if rows_size > 4:
        total = added(wide(kept) + wide(rows_flip(kept, 4)), wide(rows_flip(sent, 2)) + wide(rows_flip(sent, 6)))
    else:
        total = added(wide(kept), wide(rows_flip(sent, 2)))
    bit = 8
    while bit < rows_size:
        total = added(wide(total), wide(rows_flip(total, bit)))
        bit *= 2
    total, output_map, input_grad = lax.optimization_barrier((total, output_map, input_grad))
    chip = rows_flip(total, 2)
    side = cols_flip(total)
    corner = lax.ppermute(
        total,
        ("rows", "cols"),
        [(i * cols_size + j, (i ^ 2) * cols_size + (j ^ 1)) for i in range(rows_size) for j in range(cols_size)],
    )
    four = (total, chip, side, corner)
    factor = 1.0 / math.sqrt(height * across * rows_size)
    halves = unpack(factor, 0, four, (), **granted(across))
    projection_grad, first_grad, second_grad = unpack(
        factor, 1, [rows_flip(piece, 1) for piece in four], halves, **granted(across)
    )
    return (output_map[None], input_grad[None], projection_grad, first_grad, second_grad)


def solution(mesh):
    placed = (P("rows", "cols", None), P(), P(), P(), P("rows", "cols", None))
    return jax.shard_map(
        body,
        mesh=mesh,
        in_specs=placed,
        out_specs=(P("rows", "cols", None), P("rows", "cols", None), P(), P(), P()),
        check_vma=False,
    )
```

```python
import functools
import math

import jax
import jax.numpy as jnp
from jax import lax
from jax.experimental import pallas as pl
from jax.experimental.pallas import tpu as pltpu
from jax.sharding import PartitionSpec as P

QK = 128
VAL = 256
HEADS = 8
CONV = 128
HEAD_QK = QK // HEADS
HEAD_VAL = VAL // HEADS
PACKED = 2 * QK + VAL
BLOCK = 256
BF = jnp.bfloat16
F32 = jnp.float32
SCALING = HEAD_QK ** (-0.5)
EXP2_SCALING = SCALING * math.log2(math.e)

PARTS = 8
FIRST_ROWS = 9 * VAL // PARTS
SECOND_ROWS = 9 * CONV // PARTS
CONV_ROWS = FIRST_ROWS + SECOND_ROWS
PROJ_ROWS = PACKED // CONV * (VAL // PARTS)


def mm(a, b):
    return lax.dot_general(a, b, (((1,), (0,)), ((), ())), preferred_element_type=F32)


def mm_t(a, b):
    return lax.dot_general(a, b, (((1,), (1,)), ((), ())), preferred_element_type=F32)


def one_hot(shape, wanted):
    rows = lax.broadcasted_iota(jnp.int32, shape, 0)
    columns = lax.broadcasted_iota(jnp.int32, shape, 1)
    return jnp.where(columns == wanted(rows), 1.0, 0.0).astype(BF)


def identity(size):
    return one_hot((size, size), lambda rows: rows)


def head_of(values, head, width):
    lanes = lax.broadcasted_iota(jnp.int32, values.shape, 1)
    return jnp.where(lanes // width == head, values, jnp.zeros_like(values))


def moved(values, step):
    count = values.shape[0]
    turned = pltpu.roll(values, (-step) % count, 0)
    at = lax.broadcasted_iota(jnp.int32, values.shape, 0)
    return jnp.where(at == (count - 1 if step > 0 else 0), 0.0, turned)


def for_blocks(count, run):
    if count == 1:
        run(0)
    else:
        lax.fori_loop(0, count, lambda i, carry: (run(i), carry)[1], 0)


def block_at(index):
    return pl.ds(index if isinstance(index, int) else pl.multiple_of(index * BLOCK, BLOCK), BLOCK)


def fetch_kernel(count, *refs):
    targets = refs[-1 - count : -1]
    copies = [pltpu.make_async_copy(refs[i], targets[i], refs[-1].at[i]) for i in range(count)]
    for copy in copies:
        copy.start()
    for copy in copies:
        copy.wait()


def fetch(arrays, after=(), nbytes=4 * 1024 * 1024):
    return pl.pallas_call(
        functools.partial(fetch_kernel, len(arrays)),
        out_shape=tuple(shape(*array.shape) for array in arrays),
        in_specs=[HBM] * (len(arrays) + len(after)),
        out_specs=[VMEM] * len(arrays),
        scratch_shapes=[pltpu.SemaphoreType.DMA((len(arrays),))],
        cost_estimate=pl.CostEstimate(flops=0, bytes_accessed=nbytes, transcendentals=0),
        name="fetch",
        **granted(32),
    )(*arrays, *after)


def forward_kernel(whole, *refs):
    count = 1 if whole else 2
    features = refs[:count]
    cotangent = refs[count : 2 * count]
    projection, comb, local, lse, values_t = refs[2 * count :]
    across = comb.shape[0]
    for which in range(count):
        width = features[which].shape[0]
        if whole:
            at = pl.ds(0, width)
        else:
            place = lax.rem(lax.axis_index("cols") + which, 2)
            at = pl.ds(pl.multiple_of(place * width, width), width)
        local[at, PACKED:] = features[which][...]
        comb[at, VAL:] = cotangent[which][...]
    packed = mm(local[:, PACKED:], projection[...]).astype(BF)
    local[:, :PACKED] = packed
    keys = packed[:, QK : 2 * QK]
    values_t[...] = mm_t(identity(VAL), packed[:, 2 * QK :]).astype(BF)

    def block(index):
        at = block_at(index)
        queries = local[at, :QK]
        rows = []
        all_scores = mm_t(jnp.concatenate([head_of(keys, h, HEAD_QK) for h in range(HEADS)], axis=0), queries)
        for head in range(HEADS):
            scores = all_scores[head * across : (head + 1) * across, :]
            maxima = jnp.max(scores, axis=0, keepdims=True)
            exponent = jnp.exp2((scores - maxima) * EXP2_SCALING)
            totals = jnp.sum(exponent, axis=0, keepdims=True)
            weighted = mm(values_t[head * HEAD_VAL : (head + 1) * HEAD_VAL, :], exponent.astype(BF))
            rows.append((weighted * (1.0 / totals)).astype(BF))
            lse[head : head + 1, at] = maxima * EXP2_SCALING + jnp.log2(totals)
        comb[at, :VAL] = mm_t(identity(BLOCK), jnp.concatenate(rows, axis=0)).astype(BF)

    for_blocks(across // BLOCK, block)


class Place:
    def __init__(self):
        row = lax.axis_index("rows")
        self.col = lax.axis_index("cols")
        self.core = lax.rem(row, 2)
        self.chip_bit = lax.rem(row // 2, 2)
        self.col_bit = lax.rem(self.col, 2)
        self.near_inside = jnp.where(self.core == 0, row > 0, row < lax.axis_size("rows") - 1)
        self.mate_inside = jnp.where(self.core == 0, row < lax.axis_size("rows") - 2, row > 1)
        self.taps = [tap + self.core * (2 - 2 * tap) for tap in range(3)]

    def chosen(self, total, half):
        size = total // 4
        middle = size // 2

        def wanted(rows):
            swapped = jnp.where(rows < middle, rows + middle, rows - middle)
            return (2 * half + self.col_bit) * size + jnp.where(self.chip_bit == 0, rows, swapped)

        return one_hot((size, total), wanted)

    def beside(self, weights, tap):
        return jnp.concatenate([weights[self.taps[tap], b] for b in range(3)], axis=1)

    def stacked(self, weights, tap):
        return jnp.concatenate([weights[self.taps[tap], b] for b in range(3)], axis=0)


def side(total, width, sign):
    left = moved(total[:, :width], -sign)
    right = moved(total[:, 2 * width :], sign)
    return left + total[:, width : 2 * width] + right


def spread(values):
    return jnp.concatenate(
        [moved(values, 1).astype(BF), values.astype(BF), moved(values, -1).astype(BF)], axis=1
    )


def far_term_kernel(own, first_kernel, term):
    term[:, :CONV] = side(mm(own[:, :VAL], Place().beside(first_kernel, 0)), CONV, 1).astype(BF)
    term[:, CONV:] = own[:, VAL:]


def far_back_kernel(far, second_kernel, out):
    back = side(mm_t(far[:, CONV:], Place().stacked(second_kernel, 2)), CONV, -1)
    out[:, :CONV] = far[:, :CONV].astype(F32)
    out[:, CONV:] = back


def prepare_kernel(own, local, lse, soft, keys_t, queries_t, attended_t, features_t):
    place = Place()
    across = own.shape[0]
    keys = local[:, QK : 2 * QK]
    keys_t[...] = mm_t(identity(QK), keys).astype(BF)
    pick = jnp.concatenate([place.chosen(VAL, place.core), place.chosen(VAL, 1 - place.core)], axis=0)
    features_t[...] = mm_t(pick, local[:, PACKED:]).astype(BF)

    def block(index):
        at = block_at(index)
        queries = local[at, :QK]
        queries_t[:, at] = mm_t(identity(QK), queries).astype(BF)
        attended_t[:, at] = mm_t(identity(VAL), own[at, :VAL]).astype(BF)
        scores = mm_t(jnp.concatenate([head_of(keys, h, HEAD_QK) for h in range(HEADS)], axis=0), queries)
        for head in range(HEADS):
            rows = slice(head * across, (head + 1) * across)
            soft[rows, at] = jnp.exp2(scores[rows, :] * EXP2_SCALING - lse[head : head + 1, at]).astype(BF)

    for_blocks(across // BLOCK, block)


def masked(inside, row):
    return jnp.where(inside, row, jnp.zeros_like(row))


def conv_term(place, row, kernel, tap):
    return side(mm(row[:, :VAL], place.beside(kernel, tap)), CONV, 1)


def back_term(place, row, kernel, tap):
    return side(mm_t(row[:, VAL:], place.stacked(kernel, tap)), CONV, -1)


def store_middle(pre, back, out):
    sigma = 1.0 / (1.0 + jnp.exp(-pre))
    out[:, :CONV] = (pre * sigma).astype(BF)
    out[:, CONV:] = (back * (sigma * (1.0 + pre * (1.0 - sigma)))).astype(BF)


def inner_kernel(own, mate, mate1, first_kernel, second_kernel, mate_mid, near_part, own_part):
    place = Place()
    mate1 = masked(place.mate_inside, mate1[...])
    near_part[:, :CONV] = conv_term(place, own, first_kernel, 2)
    near_part[:, CONV:] = back_term(place, own, second_kernel, 0)
    own_part[:, :CONV] = conv_term(place, own, first_kernel, 1) + conv_term(place, mate, first_kernel, 2)
    own_part[:, CONV:] = back_term(place, own, second_kernel, 1) + back_term(place, mate, second_kernel, 0)
    rows = (own, mate, mate1)
    pre = sum(conv_term(place, row, first_kernel, a) for a, row in enumerate(rows))
    back = sum(back_term(place, row, second_kernel, 2 - a) for a, row in enumerate(rows))
    store_middle(pre, back, mate_mid)


def middle(place, far, near, near_part, own_part, first_kernel, second_kernel, near_mid, own_mid):
    pre = near_part[:, :CONV] + far[:, :CONV] + conv_term(place, near, first_kernel, 1)
    back = near_part[:, CONV:] + far[:, CONV:] + back_term(place, near, second_kernel, 1)
    store_middle(masked(place.near_inside, pre), masked(place.near_inside, back), near_mid)
    pre = own_part[:, :CONV] + conv_term(place, near, first_kernel, 0)
    back = own_part[:, CONV:] + back_term(place, near, second_kernel, 2)
    store_middle(pre, back, own_mid)


def conv_grads_kernel(near, own, mate, mate1, own_mid, mate_mid, keep, send):
    place = Place()
    slots = (masked(place.near_inside, near[...]), own[...], mate[...], masked(place.mate_inside, mate1[...]))
    mids = {1: own_mid, 2: mate_mid}

    def store(total, start, step, a):
        for b in range(3):
            at = pl.ds(pl.multiple_of(start + (place.taps[a] * 3 + b) * step, step), step)
            keep[at, :] = total[:step, b * CONV : (b + 1) * CONV]
            send[at, :] = total[step:, b * CONV : (b + 1) * CONV]

    pick = place.chosen(VAL, place.core)
    attended_t = [mm_t(pick, slot[:, :VAL]).astype(BF) for slot in slots]
    slope = {slot: spread(mid[:, CONV:].astype(F32)) for slot, mid in mids.items()}
    for a in range(3):
        total = sum(mm(attended_t[slot + a - 1], slope[slot]) for slot in mids).astype(BF)
        store(total, 0, VAL // PARTS, a)
    pick = place.chosen(CONV, place.core)
    hidden_t = {slot: mm_t(pick, mid[:, :CONV]).astype(BF) for slot, mid in mids.items()}
    cotangent = [spread(slot[:, VAL:].astype(F32)) for slot in slots]
    for a in range(3):
        total = sum(mm(hidden_t[slot], cotangent[slot + 1 - a]) for slot in mids).astype(BF)
        store(total, FIRST_ROWS, CONV // PARTS, a)


def backward_kernel(
    far,
    near,
    mate_mid,
    near_part,
    own_part,
    local,
    soft,
    keys_t,
    queries_t,
    attended_t,
    features_t,
    first_kernel,
    second_kernel,
    near_mid,
    own_mid,
    grad_own,
    proj_own,
    proj_mate,
    upstream_ref,
    grad_t,
):
    place = Place()
    across = near.shape[0]
    part_width = grad_own.shape[0]
    near = masked(place.near_inside, near[...])
    mids = (near_mid, own_mid, mate_mid)
    middle(place, far, near, near_part, own_part, first_kernel, second_kernel, near_mid, own_mid)
    upstream_ref[...] = side(
        sum(mm_t(mids[2 - a][:, CONV:], place.stacked(first_kernel, a)) for a in range(3)), VAL, -1
    ).astype(BF)
    values = local[:, 2 * QK : PACKED]
    blocks = across // BLOCK
    if blocks > 1:
        grad_t[...] = jnp.zeros_like(grad_t)

    def add_rows(start, count, terms):
        if blocks > 1:
            grad_t[start : start + count, :] += terms
        else:
            grad_t[start : start + count, :] = terms

    def block(index):
        at = block_at(index)
        upstream = upstream_ref[at, :]
        upstream_t = mm_t(identity(VAL), upstream)
        products = upstream_t * attended_t[:, at].astype(F32)
        upstream_t = upstream_t.astype(BF)
        slopes = mm_t(jnp.concatenate([head_of(values, h, HEAD_VAL) for h in range(HEADS)], axis=0), upstream)
        for head in range(HEADS):
            rows = slice(head * across, (head + 1) * across)
            qk_rows = slice(head * HEAD_QK, (head + 1) * HEAD_QK)
            val_rows = slice(head * HEAD_VAL, (head + 1) * HEAD_VAL)
            weights = soft[rows, at]
            inner = jnp.sum(products[val_rows, :], axis=0, keepdims=True)
            dscore = (weights.astype(F32) * (slopes[rows, :] - inner)).astype(BF)
            grad_t[qk_rows, at] = SCALING * mm(keys_t[qk_rows, :], dscore)
            add_rows(QK + head * HEAD_QK, HEAD_QK, SCALING * mm_t(queries_t[qk_rows, at], dscore))
            add_rows(2 * QK + head * HEAD_VAL, HEAD_VAL, mm_t(upstream_t[val_rows, :], weights))

    for_blocks(blocks, block)

    grad = grad_t[...].astype(BF)
    step = VAL // PARTS
    total = mm_t(features_t[...], grad).astype(BF)
    for which, target in enumerate((proj_own, proj_mate)):
        for j in range(PACKED // CONV):
            for part in range(2):
                begin = (2 * which + part) * step
                target[part, j * step : (j + 1) * step, :] = total[begin : begin + step, j * CONV : (j + 1) * CONV]
    own_pixels = one_hot((part_width, across), lambda rows: rows + place.col * part_width)
    grad_own[...] = mm_t(own_pixels, grad).astype(BF)


def outputs_kernel(near_mid, own_mid, mate_mid, grad_own, projection, second_kernel, output_map, input_grad, rows):
    place = Place()
    part_width = output_map.shape[0]
    mids = (near_mid, own_mid, mate_mid)
    rows[...] = side(sum(mm(mids[a][:, :CONV], place.beside(second_kernel, a)) for a in range(3)), CONV, 1)
    output_map[...] = rows[pl.ds(pl.multiple_of(place.col * part_width, part_width), part_width), :].astype(BF)
    input_grad[...] = mm_t(grad_own[...], projection[...]).astype(BF)


def unpack_kernel(factor, core_flip, *refs):
    pieces = refs[:4]
    outs = refs[-7:-4]
    blocks = refs[-4:-1]
    sem = refs[-1]
    projection_block, first_block, second_block = blocks
    row = lax.axis_index("rows")
    half = lax.rem(row + core_flip, 2)
    chip_bit = lax.rem(row // 2, 2)
    col_bit = lax.rem(lax.axis_index("cols"), 2)
    parts = [2 * lax.rem(col_bit + which // 2, 2) + lax.rem(chip_bit + which % 2, 2) for which in range(4)]
    copies = []

    def send(index, block, out):
        copies.append(pltpu.make_async_copy(block, out, sem.at[index]))
        copies[-1].start()

    def rows_of(which, step):
        return pl.ds(pl.multiple_of(parts[which] * step, step), step)

    def half_of(rows):
        return pl.ds(pl.multiple_of(half * rows, rows), rows)

    step = VAL // PARTS
    for a in range(3):
        for which, piece in enumerate(pieces):
            for b in range(3):
                begin = (3 * a + b) * step
                first_block[a, b, rows_of(which, step), :] = piece[begin : begin + step, :].astype(F32) * factor
        send(a, first_block.at[a], outs[1].at[a, :, half_of(VAL // 2), :])
    for which, piece in enumerate(pieces):
        for j in range(PACKED // CONV):
            begin = FIRST_ROWS + SECOND_ROWS + j * step
            projection_block[rows_of(which, step), j * CONV : (j + 1) * CONV] = (
                piece[begin : begin + step, :].astype(F32) * factor
            )
    send(3, projection_block, outs[0].at[half_of(VAL // 2), :])
    step = CONV // PARTS
    for which, piece in enumerate(pieces):
        for tap in range(9):
            begin = FIRST_ROWS + tap * step
            second_block[tap // 3, tap % 3, rows_of(which, step), :] = (
                piece[begin : begin + step, :].astype(F32) * factor
            )
    send(4, second_block, outs[2].at[:, :, half_of(CONV // 2), :])
    for copy in copies:
        copy.wait()


def unpack(factor, core_flip, pieces, into, **params):
    dims = ((2 * QK, PACKED), (3, 3, VAL, CONV), (3, 3, CONV, CONV))
    return pl.pallas_call(
        functools.partial(unpack_kernel, factor, core_flip),
        out_shape=tuple(shape(*size, dtype=F32) for size in dims),
        in_specs=[VMEM] * 4 + [HBM] * len(into),
        out_specs=[HBM] * 3,
        scratch_shapes=[pltpu.VMEM(size[:-2] + (size[-2] // 2, size[-1]), F32) for size in dims]
        + [pltpu.SemaphoreType.DMA((5,))],
        input_output_aliases={4 + i: i for i in range(len(into))},
        cost_estimate=pl.CostEstimate(flops=10**9, bytes_accessed=4 * 1024 * 1024, transcendentals=0),
        name="unpack_sums",
        **params,
    )(*pieces, *into)


def shape(*dims, dtype=BF):
    return jax.ShapeDtypeStruct(dims, dtype)


def granted(across):
    return dict(compiler_params=pltpu.CompilerParams(vmem_limit_bytes=across * 64 * 1024))


VMEM = pl.BlockSpec(memory_space=pltpu.VMEM)
HBM = pl.BlockSpec(memory_space=pltpu.HBM)


def body(features, projection, first_kernel, second_kernel, cotangent):
    height, part_width, channels = features.shape
    rows_size = lax.axis_size("rows")
    cols_size = lax.axis_size("cols")
    across = part_width * cols_size

    def rows_flip(values, bit):
        return lax.ppermute(values, "rows", [(i, i ^ bit) for i in range(rows_size)])

    def cols_flip(values):
        return lax.ppermute(values, "cols", [(i, i ^ 1) for i in range(cols_size)])

    def wide(values):
        return values.astype(F32)

    def added(one, two):
        return (one + two).astype(BF)

    def call(kernel, out_shape, operands, scratch=(), name=None, flops=10**9):
        return pl.pallas_call(
            kernel,
            out_shape=out_shape,
            in_specs=[VMEM] * len(operands),
            out_specs=[VMEM] * len(out_shape),
            scratch_shapes=scratch,
            cost_estimate=pl.CostEstimate(flops=flops, bytes_accessed=flops // 250, transcendentals=0),
            name=name,
            **granted(across),
        )(*operands)

    given = (features, cotangent)
    projection, features, cotangent = fetch((projection, features[0], cotangent[0]))
    if cols_size == 2:
        pieces = (features, cols_flip(given[0][0]), cotangent, cols_flip(given[1][0]))
    else:
        pieces = tuple(lax.all_gather(array[0], "cols", axis=0, tiled=True) for array in given)
    own, local, lse = call(
        functools.partial(forward_kernel, cols_size != 2),
        (
            shape(across, VAL + CONV),
            shape(across, PACKED + channels),
            shape(HEADS, across, dtype=F32),
        ),
        (*pieces, projection),
        (pltpu.VMEM((VAL, across), BF),),
        name="attention_forward",
    )

    given_first = first_kernel
    first_kernel, second_kernel = fetch((first_kernel, second_kernel), (lse,), 10**5)
    last = rows_size - 1
    out = [(i, i + 2) for i in range(0, last - 1, 2)] + [(i, i - 2) for i in range(3, rows_size, 2)]
    out += [(last - 1, last), (1, 0)]
    back = [(j, i) for i, j in out]
    (term,) = call(far_term_kernel, (shape(across, 2 * CONV),), (own, given_first), name="far_term")
    own, term = lax.optimization_barrier((own, term))
    mate1 = lax.ppermute(own, "rows", back)
    far = lax.ppermute(term, "rows", out)
    (far,) = call(
        far_back_kernel, (shape(across, 2 * CONV, dtype=F32),), (far, second_kernel), name="far_back", flops=4 * 10**9
    )
    mate = rows_flip(own, 1)
    near = rows_flip(mate1, 1)
    soft, keys_t, queries_t, attended_t, features_t = call(
        prepare_kernel,
        (
            shape(HEADS * across, across),
            shape(QK, across),
            shape(QK, across),
            shape(VAL, across),
            shape(VAL // 2, across),
        ),
        (own, local, lse),
        name="prepare",
        flops=10**7,
    )
    mate_mid, near_part, own_part = call(
        inner_kernel,
        (shape(across, 2 * CONV), shape(across, 2 * CONV, dtype=F32), shape(across, 2 * CONV, dtype=F32)),
        (own, mate, mate1, first_kernel, second_kernel),
        name="inner",
    )
    near_mid, own_mid, grad_own, proj_own, proj_mate = call(
        backward_kernel,
        (
            shape(across, 2 * CONV),
            shape(across, 2 * CONV),
            shape(part_width, PACKED),
            shape(2, PROJ_ROWS, CONV),
            shape(2, PROJ_ROWS, CONV),
        ),
        (
            far,
            near,
            mate_mid,
            near_part,
            own_part,
            local,
            soft,
            keys_t,
            queries_t,
            attended_t,
            features_t,
            first_kernel,
            second_kernel,
        ),
        (pltpu.VMEM((across, VAL), BF), pltpu.VMEM((PACKED, across), F32)),
        name="block_backward",
    )
    keep, send = call(
        conv_grads_kernel,
        (shape(FIRST_ROWS + SECOND_ROWS, CONV),) * 2,
        (near, own, mate, mate1, own_mid, mate_mid),
        name="conv_grads",
    )
    output_map, input_grad = call(
        outputs_kernel,
        (shape(part_width, CONV), shape(part_width, channels)),
        (near_mid, own_mid, mate_mid, grad_own, projection, second_kernel),
        (pltpu.VMEM((across, CONV), F32),),
        name="outputs",
    )
    proj_sum = added(wide(proj_own), wide(rows_flip(proj_mate, 1)))
    sent = jnp.concatenate([send, proj_sum[1]], axis=0)
    kept = jnp.concatenate([keep, proj_sum[0]], axis=0)
    if rows_size > 4:
        total = added(wide(kept) + wide(rows_flip(kept, 4)), wide(rows_flip(sent, 2)) + wide(rows_flip(sent, 6)))
    else:
        total = added(wide(kept), wide(rows_flip(sent, 2)))
    bit = 8
    while bit < rows_size:
        total = added(wide(total), wide(rows_flip(total, bit)))
        bit *= 2
    total, output_map, input_grad = lax.optimization_barrier((total, output_map, input_grad))
    chip = rows_flip(total, 2)
    side = cols_flip(total)
    corner = lax.ppermute(
        total,
        ("rows", "cols"),
        [(i * cols_size + j, (i ^ 2) * cols_size + (j ^ 1)) for i in range(rows_size) for j in range(cols_size)],
    )
    four = (total, chip, side, corner)
    factor = 1.0 / math.sqrt(height * across * rows_size)
    halves = unpack(factor, 0, four, (), **granted(across))
    projection_grad, first_grad, second_grad = unpack(
        factor, 1, [rows_flip(piece, 1) for piece in four], halves, **granted(across)
    )
    return (output_map[None], input_grad[None], projection_grad, first_grad, second_grad)


def solution(mesh):
    placed = (P("rows", "cols", None), P(), P(), P(), P("rows", "cols", None))
    return jax.shard_map(
        body,
        mesh=mesh,
        in_specs=placed,
        out_specs=(P("rows", "cols", None), P("rows", "cols", None), P(), P(), P()),
        check_vma=False,
    )
```

```python
import functools
import math

import jax
import jax.numpy as jnp
from jax import lax
from jax.experimental import pallas as pl
from jax.experimental.pallas import tpu as pltpu
from jax.sharding import PartitionSpec as P

QK = 128
VAL = 256
HEADS = 8
CONV = 128
HEAD_QK = QK // HEADS
HEAD_VAL = VAL // HEADS
PACKED = 2 * QK + VAL
BLOCK = 256
BF = jnp.bfloat16
F32 = jnp.float32
SCALING = HEAD_QK ** (-0.5)
EXP2_SCALING = SCALING * math.log2(math.e)

PARTS = 8
FIRST_ROWS = 9 * VAL // PARTS
SECOND_ROWS = 9 * CONV // PARTS
CONV_ROWS = FIRST_ROWS + SECOND_ROWS
PROJ_ROWS = PACKED // CONV * (VAL // PARTS)


def mm(a, b):
    return lax.dot_general(a, b, (((1,), (0,)), ((), ())), preferred_element_type=F32)


def mm_t(a, b):
    return lax.dot_general(a, b, (((1,), (1,)), ((), ())), preferred_element_type=F32)


def one_hot(shape, wanted):
    rows = lax.broadcasted_iota(jnp.int32, shape, 0)
    columns = lax.broadcasted_iota(jnp.int32, shape, 1)
    return jnp.where(columns == wanted(rows), 1.0, 0.0).astype(BF)


def identity(size):
    return one_hot((size, size), lambda rows: rows)


def head_of(values, head, width):
    lanes = lax.broadcasted_iota(jnp.int32, values.shape, 1)
    return jnp.where(lanes // width == head, values, jnp.zeros_like(values))


def moved(values, step):
    count = values.shape[0]
    turned = pltpu.roll(values, (-step) % count, 0)
    at = lax.broadcasted_iota(jnp.int32, values.shape, 0)
    return jnp.where(at == (count - 1 if step > 0 else 0), 0.0, turned)


def for_blocks(count, run):
    if count == 1:
        run(0)
    else:
        lax.fori_loop(0, count, lambda i, carry: (run(i), carry)[1], 0)


def block_at(index):
    return pl.ds(index if isinstance(index, int) else pl.multiple_of(index * BLOCK, BLOCK), BLOCK)


def fetch_kernel(count, *refs):
    targets = refs[-1 - count : -1]
    copies = [pltpu.make_async_copy(refs[i], targets[i], refs[-1].at[i]) for i in range(count)]
    for copy in copies:
        copy.start()
    for copy in copies:
        copy.wait()


def fetch(arrays, after=(), nbytes=4 * 1024 * 1024):
    return pl.pallas_call(
        functools.partial(fetch_kernel, len(arrays)),
        out_shape=tuple(shape(*array.shape) for array in arrays),
        in_specs=[HBM] * (len(arrays) + len(after)),
        out_specs=[VMEM] * len(arrays),
        scratch_shapes=[pltpu.SemaphoreType.DMA((len(arrays),))],
        cost_estimate=pl.CostEstimate(flops=0, bytes_accessed=nbytes, transcendentals=0),
        name="fetch",
        **granted(32),
    )(*arrays, *after)


def lay_out(pieces, target, lanes):
    for which, piece in enumerate(pieces):
        width = piece.shape[0]
        if len(pieces) == 1:
            at = slice(None)
        else:
            place = lax.rem(lax.axis_index("cols") + which, 2)
            at = pl.ds(pl.multiple_of(place * width, width), width)
        target[at, lanes] = piece[...]


def forward_kernel(count, *refs):
    projection, attended, local, lse, values_t = refs[count:]
    across = attended.shape[0]
    lay_out(refs[:count], local, slice(PACKED, None))
    packed = mm(local[:, PACKED:], projection[...]).astype(BF)
    local[:, :PACKED] = packed
    keys = packed[:, QK : 2 * QK]
    values_t[...] = mm_t(identity(VAL), packed[:, 2 * QK :]).astype(BF)

    def block(index):
        at = block_at(index)
        queries = local[at, :QK]
        rows = []
        all_scores = mm_t(jnp.concatenate([head_of(keys, h, HEAD_QK) for h in range(HEADS)], axis=0), queries)
        for head in range(HEADS):
            scores = all_scores[head * across : (head + 1) * across, :]
            maxima = jnp.max(scores, axis=0, keepdims=True)
            exponent = jnp.exp2((scores - maxima) * EXP2_SCALING)
            totals = jnp.sum(exponent, axis=0, keepdims=True)
            weighted = mm(values_t[head * HEAD_VAL : (head + 1) * HEAD_VAL, :], exponent.astype(BF))
            rows.append((weighted * (1.0 / totals)).astype(BF))
            lse[head : head + 1, at] = maxima * EXP2_SCALING + jnp.log2(totals)
        attended[at, :] = mm_t(identity(BLOCK), jnp.concatenate(rows, axis=0)).astype(BF)

    for_blocks(across // BLOCK, block)


class Place:
    def __init__(self):
        row = lax.axis_index("rows")
        self.col = lax.axis_index("cols")
        self.core = lax.rem(row, 2)
        self.chip_bit = lax.rem(row // 2, 2)
        self.col_bit = lax.rem(self.col, 2)
        self.near_inside = jnp.where(self.core == 0, row > 0, row < lax.axis_size("rows") - 1)
        self.mate_inside = jnp.where(self.core == 0, row < lax.axis_size("rows") - 2, row > 1)
        self.taps = [tap + self.core * (2 - 2 * tap) for tap in range(3)]

    def chosen(self, total, half):
        size = total // 4
        middle = size // 2

        def wanted(rows):
            swapped = jnp.where(rows < middle, rows + middle, rows - middle)
            return (2 * half + self.col_bit) * size + jnp.where(self.chip_bit == 0, rows, swapped)

        return one_hot((size, total), wanted)

    def beside(self, weights, tap):
        return jnp.concatenate([weights[self.taps[tap], b] for b in range(3)], axis=1)

    def stacked(self, weights, tap):
        return jnp.concatenate([weights[self.taps[tap], b] for b in range(3)], axis=0)


def side(total, width, sign):
    left = moved(total[:, :width], -sign)
    right = moved(total[:, 2 * width :], sign)
    return left + total[:, width : 2 * width] + right


def spread(values):
    return jnp.concatenate(
        [moved(values, 1).astype(BF), values.astype(BF), moved(values, -1).astype(BF)], axis=1
    )


def rows_kernel(count, *refs):
    attended, first_kernel, row, term = refs[count:]
    lay_out(refs[:count], row, slice(VAL, None))
    lay_out(refs[:count], term, slice(CONV, None))
    row[:, :VAL] = attended[...]
    term[:, :CONV] = side(mm(attended[...], Place().beside(first_kernel, 0)), CONV, 1).astype(BF)


def far_back_kernel(far, second_kernel, out):
    back = side(mm_t(far[:, CONV:], Place().stacked(second_kernel, 2)), CONV, -1)
    out[:, :CONV] = far[:, :CONV].astype(F32)
    out[:, CONV:] = back


def prepare_kernel(own, local, lse, soft, keys_t, queries_t, attended_t, features_t, values):
    place = Place()
    across = own.shape[0]
    keys = local[:, QK : 2 * QK]
    keys_t[...] = mm_t(identity(QK), keys).astype(BF)
    pick = jnp.concatenate([place.chosen(VAL, place.core), place.chosen(VAL, 1 - place.core)], axis=0)
    features_t[...] = mm_t(pick, local[:, PACKED:]).astype(BF)
    for head in range(HEADS):
        values[head * across : (head + 1) * across, :] = head_of(local[:, 2 * QK : PACKED], head, HEAD_VAL)

    def block(index):
        at = block_at(index)
        queries = local[at, :QK]
        queries_t[:, at] = mm_t(identity(QK), queries).astype(BF)
        attended_t[:, at] = mm_t(identity(VAL), own[at, :VAL]).astype(BF)
        scores = mm_t(jnp.concatenate([head_of(keys, h, HEAD_QK) for h in range(HEADS)], axis=0), queries)
        for head in range(HEADS):
            rows = slice(head * across, (head + 1) * across)
            soft[rows, at] = jnp.exp2(scores[rows, :] * EXP2_SCALING - lse[head : head + 1, at]).astype(BF)

    for_blocks(across // BLOCK, block)


def masked(inside, row):
    return jnp.where(inside, row, jnp.zeros_like(row))


def conv_term(place, row, kernel, tap):
    return side(mm(row[:, :VAL], place.beside(kernel, tap)), CONV, 1)


def back_term(place, row, kernel, tap):
    return side(mm_t(row[:, VAL:], place.stacked(kernel, tap)), CONV, -1)


def store_middle(pre, back, out):
    sigma = 1.0 / (1.0 + jnp.exp(-pre))
    out[:, :CONV] = (pre * sigma).astype(BF)
    out[:, CONV:] = (back * (sigma * (1.0 + pre * (1.0 - sigma)))).astype(BF)


def inner_kernel(own, mate, mate1, first_kernel, second_kernel, mate_mid, near_part, own_part):
    place = Place()
    mate1 = masked(place.mate_inside, mate1[...])
    near_part[:, :CONV] = conv_term(place, own, first_kernel, 2)
    near_part[:, CONV:] = back_term(place, own, second_kernel, 0)
    own_part[:, :CONV] = conv_term(place, own, first_kernel, 1) + conv_term(place, mate, first_kernel, 2)
    own_part[:, CONV:] = back_term(place, own, second_kernel, 1) + back_term(place, mate, second_kernel, 0)
    rows = (own, mate, mate1)
    pre = sum(conv_term(place, row, first_kernel, a) for a, row in enumerate(rows))
    back = sum(back_term(place, row, second_kernel, 2 - a) for a, row in enumerate(rows))
    store_middle(pre, back, mate_mid)


def middle(place, far, near, near_part, own_part, first_kernel, second_kernel, near_mid, own_mid):
    pre = near_part[:, :CONV] + far[:, :CONV] + conv_term(place, near, first_kernel, 1)
    back = near_part[:, CONV:] + far[:, CONV:] + back_term(place, near, second_kernel, 1)
    store_middle(masked(place.near_inside, pre), masked(place.near_inside, back), near_mid)
    pre = own_part[:, :CONV] + conv_term(place, near, first_kernel, 0)
    back = own_part[:, CONV:] + back_term(place, near, second_kernel, 2)
    store_middle(pre, back, own_mid)


def conv_grads_kernel(near, own, mate, mate1, own_mid, mate_mid, keep, send):
    place = Place()
    slots = (masked(place.near_inside, near[...]), own[...], mate[...], masked(place.mate_inside, mate1[...]))
    mids = {1: own_mid, 2: mate_mid}

    def store(total, start, step, a):
        for b in range(3):
            at = pl.ds(pl.multiple_of(start + (place.taps[a] * 3 + b) * step, step), step)
            keep[at, :] = total[:step, b * CONV : (b + 1) * CONV]
            send[at, :] = total[step:, b * CONV : (b + 1) * CONV]

    pick = place.chosen(VAL, place.core)
    attended_t = [mm_t(pick, slot[:, :VAL]).astype(BF) for slot in slots]
    slope = {slot: spread(mid[:, CONV:].astype(F32)) for slot, mid in mids.items()}
    for a in range(3):
        total = sum(mm(attended_t[slot + a - 1], slope[slot]) for slot in mids).astype(BF)
        store(total, 0, VAL // PARTS, a)
    pick = place.chosen(CONV, place.core)
    hidden_t = {slot: mm_t(pick, mid[:, :CONV]).astype(BF) for slot, mid in mids.items()}
    cotangent = [spread(slot[:, VAL:].astype(F32)) for slot in slots]
    for a in range(3):
        total = sum(mm(hidden_t[slot], cotangent[slot + 1 - a]) for slot in mids).astype(BF)
        store(total, FIRST_ROWS, CONV // PARTS, a)


def backward_kernel(
    far,
    near,
    mate_mid,
    near_part,
    own_part,
    values,
    soft,
    keys_t,
    queries_t,
    attended_t,
    features_t,
    first_kernel,
    second_kernel,
    near_mid,
    own_mid,
    grad_out,
    proj_own,
    proj_mate,
    upstream_ref,
    grad_t,
):
    place = Place()
    across = near.shape[0]
    near = masked(place.near_inside, near[...])
    mids = (near_mid, own_mid, mate_mid)
    middle(place, far, near, near_part, own_part, first_kernel, second_kernel, near_mid, own_mid)
    upstream_ref[...] = side(
        sum(mm_t(mids[2 - a][:, CONV:], place.stacked(first_kernel, a)) for a in range(3)), VAL, -1
    ).astype(BF)
    blocks = across // BLOCK
    if blocks > 1:
        grad_t[...] = jnp.zeros_like(grad_t)

    def add_rows(start, count, terms):
        if blocks > 1:
            grad_t[start : start + count, :] += terms
        else:
            grad_t[start : start + count, :] = terms

    def block(index):
        at = block_at(index)
        upstream = upstream_ref[at, :]
        upstream_t = mm_t(identity(VAL), upstream)
        products = upstream_t * attended_t[:, at].astype(F32)
        upstream_t = upstream_t.astype(BF)
        slopes = mm_t(values[...], upstream)
        for head in range(HEADS):
            rows = slice(head * across, (head + 1) * across)
            qk_rows = slice(head * HEAD_QK, (head + 1) * HEAD_QK)
            val_rows = slice(head * HEAD_VAL, (head + 1) * HEAD_VAL)
            weights = soft[rows, at]
            inner = jnp.sum(products[val_rows, :], axis=0, keepdims=True)
            dscore = (weights.astype(F32) * (slopes[rows, :] - inner)).astype(BF)
            grad_t[qk_rows, at] = SCALING * mm(keys_t[qk_rows, :], dscore)
            add_rows(QK + head * HEAD_QK, HEAD_QK, SCALING * mm_t(queries_t[qk_rows, at], dscore))
            add_rows(2 * QK + head * HEAD_VAL, HEAD_VAL, mm_t(upstream_t[val_rows, :], weights))

    for_blocks(blocks, block)

    grad = grad_t[...].astype(BF)
    grad_out[...] = grad
    step = VAL // PARTS
    total = mm_t(features_t[...], grad).astype(BF)
    for which, target in enumerate((proj_own, proj_mate)):
        for j in range(PACKED // CONV):
            for part in range(2):
                begin = (2 * which + part) * step
                target[part, j * step : (j + 1) * step, :] = total[begin : begin + step, j * CONV : (j + 1) * CONV]


def outputs_kernel(near_mid, own_mid, mate_mid, grad, projection, second_kernel, output_map, input_grad, rows):
    place = Place()
    part_width = output_map.shape[0]
    mids = (near_mid, own_mid, mate_mid)
    rows[...] = side(sum(mm(mids[a][:, :CONV], place.beside(second_kernel, a)) for a in range(3)), CONV, 1)
    output_map[...] = rows[pl.ds(pl.multiple_of(place.col * part_width, part_width), part_width), :].astype(BF)
    own_pixels = one_hot((part_width, rows.shape[0]), lambda pixels: pixels + place.col * part_width)
    input_grad[...] = mm_t(mm_t(own_pixels, grad[...]).astype(BF), projection[...]).astype(BF)


def unpack_kernel(factor, core_flip, *refs):
    pieces = refs[:4]
    outs = refs[-7:-4]
    blocks = refs[-4:-1]
    sem = refs[-1]
    projection_block, first_block, second_block = blocks
    row = lax.axis_index("rows")
    half = lax.rem(row + core_flip, 2)
    chip_bit = lax.rem(row // 2, 2)
    col_bit = lax.rem(lax.axis_index("cols"), 2)
    parts = [2 * lax.rem(col_bit + which // 2, 2) + lax.rem(chip_bit + which % 2, 2) for which in range(4)]
    copies = []

    def send(index, block, out):
        copies.append(pltpu.make_async_copy(block, out, sem.at[index]))
        copies[-1].start()

    def rows_of(which, step):
        return pl.ds(pl.multiple_of(parts[which] * step, step), step)

    def half_of(rows):
        return pl.ds(pl.multiple_of(half * rows, rows), rows)

    step = VAL // PARTS
    for a in range(3):
        for which, piece in enumerate(pieces):
            for b in range(3):
                begin = (3 * a + b) * step
                first_block[a, b, rows_of(which, step), :] = piece[begin : begin + step, :].astype(F32) * factor
        send(a, first_block.at[a], outs[1].at[a, :, half_of(VAL // 2), :])
    for which, piece in enumerate(pieces):
        for j in range(PACKED // CONV):
            begin = FIRST_ROWS + SECOND_ROWS + j * step
            projection_block[rows_of(which, step), j * CONV : (j + 1) * CONV] = (
                piece[begin : begin + step, :].astype(F32) * factor
            )
    send(3, projection_block, outs[0].at[half_of(VAL // 2), :])
    step = CONV // PARTS
    for which, piece in enumerate(pieces):
        for tap in range(9):
            begin = FIRST_ROWS + tap * step
            second_block[tap // 3, tap % 3, rows_of(which, step), :] = (
                piece[begin : begin + step, :].astype(F32) * factor
            )
    send(4, second_block, outs[2].at[:, :, half_of(CONV // 2), :])
    for copy in copies:
        copy.wait()


def unpack(factor, core_flip, pieces, into, **params):
    dims = ((2 * QK, PACKED), (3, 3, VAL, CONV), (3, 3, CONV, CONV))
    return pl.pallas_call(
        functools.partial(unpack_kernel, factor, core_flip),
        out_shape=tuple(shape(*size, dtype=F32) for size in dims),
        in_specs=[VMEM] * 4 + [HBM] * len(into),
        out_specs=[HBM] * 3,
        scratch_shapes=[pltpu.VMEM(size[:-2] + (size[-2] // 2, size[-1]), F32) for size in dims]
        + [pltpu.SemaphoreType.DMA((5,))],
        input_output_aliases={4 + i: i for i in range(len(into))},
        cost_estimate=pl.CostEstimate(flops=10**9, bytes_accessed=4 * 1024 * 1024, transcendentals=0),
        name="unpack_sums",
        **params,
    )(*pieces, *into)


def shape(*dims, dtype=BF):
    return jax.ShapeDtypeStruct(dims, dtype)


def granted(across):
    return dict(compiler_params=pltpu.CompilerParams(vmem_limit_bytes=across * 64 * 1024))


VMEM = pl.BlockSpec(memory_space=pltpu.VMEM)
HBM = pl.BlockSpec(memory_space=pltpu.HBM)


def body(features, projection, first_kernel, second_kernel, cotangent):
    height, part_width, channels = features.shape
    rows_size = lax.axis_size("rows")
    cols_size = lax.axis_size("cols")
    across = part_width * cols_size

    def rows_flip(values, bit):
        return lax.ppermute(values, "rows", [(i, i ^ bit) for i in range(rows_size)])

    def cols_flip(values):
        return lax.ppermute(values, "cols", [(i, i ^ 1) for i in range(cols_size)])

    def wide(values):
        return values.astype(F32)

    def added(one, two):
        return (one + two).astype(BF)

    def call(kernel, out_shape, operands, scratch=(), name=None, flops=10**9):
        return pl.pallas_call(
            kernel,
            out_shape=out_shape,
            in_specs=[VMEM] * len(operands),
            out_specs=[VMEM] * len(out_shape),
            scratch_shapes=scratch,
            cost_estimate=pl.CostEstimate(flops=flops, bytes_accessed=flops // 250, transcendentals=0),
            name=name,
            **granted(across),
        )(*operands)

    features, cotangent = (features[0], cotangent[0])
    if cols_size == 2:
        swapped = cols_flip(features)
        cotangent = (cotangent, cols_flip(cotangent))
        projection, features = fetch((projection, features))
        features = (features, swapped)
    else:
        features, cotangent = (
            (lax.all_gather(array, "cols", axis=0, tiled=True),) for array in (features, cotangent)
        )
    attended, local, lse = call(
        functools.partial(forward_kernel, len(features)),
        (shape(across, VAL), shape(across, PACKED + channels), shape(HEADS, across, dtype=F32)),
        (*features, projection),
        (pltpu.VMEM((VAL, across), BF),),
        name="attention_forward",
    )
    own, term = call(
        functools.partial(rows_kernel, len(cotangent)),
        (shape(across, VAL + CONV), shape(across, 2 * CONV)),
        (*cotangent, attended, first_kernel),
        name="rows",
    )
    first_kernel, second_kernel = fetch((first_kernel, second_kernel), (lse,), 10**5)
    last = rows_size - 1
    out = [(i, i + 2) for i in range(0, last - 1, 2)] + [(i, i - 2) for i in range(3, rows_size, 2)]
    out += [(last - 1, last), (1, 0)]
    back = [(j, i) for i, j in out]
    mate1 = lax.ppermute(own, "rows", back)
    far = lax.ppermute(term, "rows", out)
    (far,) = call(
        far_back_kernel, (shape(across, 2 * CONV, dtype=F32),), (far, second_kernel), name="far_back", flops=4 * 10**9
    )
    mate = rows_flip(own, 1)
    near = rows_flip(mate1, 1)
    soft, keys_t, queries_t, attended_t, features_t, values = call(
        prepare_kernel,
        (
            shape(HEADS * across, across),
            shape(QK, across),
            shape(QK, across),
            shape(VAL, across),
            shape(VAL // 2, across),
            shape(HEADS * across, VAL),
        ),
        (own, local, lse),
        name="prepare",
        flops=10**7,
    )
    mate_mid, near_part, own_part = call(
        inner_kernel,
        (shape(across, 2 * CONV), shape(across, 2 * CONV, dtype=F32), shape(across, 2 * CONV, dtype=F32)),
        (own, mate, mate1, first_kernel, second_kernel),
        name="inner",
    )
    near_mid, own_mid, grad, proj_own, proj_mate = call(
        backward_kernel,
        (
            shape(across, 2 * CONV),
            shape(across, 2 * CONV),
            shape(PACKED, across),
            shape(2, PROJ_ROWS, CONV),
            shape(2, PROJ_ROWS, CONV),
        ),
        (
            far,
            near,
            mate_mid,
            near_part,
            own_part,
            values,
            soft,
            keys_t,
            queries_t,
            attended_t,
            features_t,
            first_kernel,
            second_kernel,
        ),
        (pltpu.VMEM((across, VAL), BF), pltpu.VMEM((PACKED, across), F32)),
        name="block_backward",
    )
    keep, send = call(
        conv_grads_kernel,
        (shape(FIRST_ROWS + SECOND_ROWS, CONV),) * 2,
        (near, own, mate, mate1, own_mid, mate_mid),
        name="conv_grads",
    )
    output_map, input_grad = call(
        outputs_kernel,
        (shape(part_width, CONV), shape(part_width, channels)),
        (near_mid, own_mid, mate_mid, grad, projection, second_kernel),
        (pltpu.VMEM((across, CONV), F32),),
        name="outputs",
    )
    proj_sum = added(wide(proj_own), wide(rows_flip(proj_mate, 1)))
    sent = jnp.concatenate([send, proj_sum[1]], axis=0)
    kept = jnp.concatenate([keep, proj_sum[0]], axis=0)
    if rows_size > 4:
        total = added(wide(kept) + wide(rows_flip(kept, 4)), wide(rows_flip(sent, 2)) + wide(rows_flip(sent, 6)))
    else:
        total = added(wide(kept), wide(rows_flip(sent, 2)))
    bit = 8
    while bit < rows_size:
        total = added(wide(total), wide(rows_flip(total, bit)))
        bit *= 2
    total, output_map, input_grad = lax.optimization_barrier((total, output_map, input_grad))
    chip = rows_flip(total, 2)
    side = cols_flip(total)
    corner = lax.ppermute(
        total,
        ("rows", "cols"),
        [(i * cols_size + j, (i ^ 2) * cols_size + (j ^ 1)) for i in range(rows_size) for j in range(cols_size)],
    )
    four = (total, chip, side, corner)
    factor = 1.0 / math.sqrt(height * across * rows_size)
    halves = unpack(factor, 0, four, (), **granted(across))
    projection_grad, first_grad, second_grad = unpack(
        factor, 1, [rows_flip(piece, 1) for piece in four], halves, **granted(across)
    )
    return (output_map[None], input_grad[None], projection_grad, first_grad, second_grad)


def solution(mesh):
    placed = (P("rows", "cols", None), P(), P(), P(), P("rows", "cols", None))
    return jax.shard_map(
        body,
        mesh=mesh,
        in_specs=placed,
        out_specs=(P("rows", "cols", None), P("rows", "cols", None), P(), P(), P()),
        check_vma=False,
    )
```

```python
import functools
import math

import jax
import jax.numpy as jnp
from jax import lax
from jax.experimental import pallas as pl
from jax.experimental.pallas import tpu as pltpu
from jax.sharding import PartitionSpec as P

QK = 128
VAL = 256
HEADS = 8
CONV = 128
HEAD_QK = QK // HEADS
HEAD_VAL = VAL // HEADS
PACKED = 2 * QK + VAL
BLOCK = 256
BF = jnp.bfloat16
F32 = jnp.float32
SCALING = HEAD_QK ** (-0.5)
EXP2_SCALING = SCALING * math.log2(math.e)

PARTS = 8
FIRST_ROWS = 9 * VAL // PARTS
SECOND_ROWS = 9 * CONV // PARTS
CONV_ROWS = FIRST_ROWS + SECOND_ROWS
PROJ_ROWS = PACKED // CONV * (VAL // PARTS)


def mm(a, b):
    return lax.dot_general(a, b, (((1,), (0,)), ((), ())), preferred_element_type=F32)


def mm_t(a, b):
    return lax.dot_general(a, b, (((1,), (1,)), ((), ())), preferred_element_type=F32)


def one_hot(shape, wanted):
    rows = lax.broadcasted_iota(jnp.int32, shape, 0)
    columns = lax.broadcasted_iota(jnp.int32, shape, 1)
    return jnp.where(columns == wanted(rows), 1.0, 0.0).astype(BF)


def identity(size):
    return one_hot((size, size), lambda rows: rows)


def head_of(values, head, width):
    lanes = lax.broadcasted_iota(jnp.int32, values.shape, 1)
    return jnp.where(lanes // width == head, values, jnp.zeros_like(values))


def moved(values, step):
    count = values.shape[0]
    turned = pltpu.roll(values, (-step) % count, 0)
    at = lax.broadcasted_iota(jnp.int32, values.shape, 0)
    return jnp.where(at == (count - 1 if step > 0 else 0), 0.0, turned)


def for_blocks(count, run):
    if count == 1:
        run(0)
    else:
        lax.fori_loop(0, count, lambda i, carry: (run(i), carry)[1], 0)


def block_at(index):
    return pl.ds(index if isinstance(index, int) else pl.multiple_of(index * BLOCK, BLOCK), BLOCK)


def fetch_kernel(count, *refs):
    targets = refs[-1 - count : -1]
    copies = [pltpu.make_async_copy(refs[i], targets[i], refs[-1].at[i]) for i in range(count)]
    for copy in copies:
        copy.start()
    for copy in copies:
        copy.wait()


def fetch(arrays, after=(), nbytes=4 * 1024 * 1024):
    return pl.pallas_call(
        functools.partial(fetch_kernel, len(arrays)),
        out_shape=tuple(shape(*array.shape) for array in arrays),
        in_specs=[HBM] * (len(arrays) + len(after)),
        out_specs=[VMEM] * len(arrays),
        scratch_shapes=[pltpu.SemaphoreType.DMA((len(arrays),))],
        cost_estimate=pl.CostEstimate(flops=0, bytes_accessed=nbytes, transcendentals=0),
        name="fetch",
        **granted(32),
    )(*arrays, *after)


def lay_out(pieces, target, lanes):
    for which, piece in enumerate(pieces):
        width = piece.shape[0]
        if len(pieces) == 1:
            at = slice(None)
        else:
            place = lax.rem(lax.axis_index("cols") + which, 2)
            at = pl.ds(pl.multiple_of(place * width, width), width)
        target[at, lanes] = piece[...]


def forward_kernel(count, *refs):
    projection, attended, local, lse, values_t = refs[count:]
    across = attended.shape[0]
    lay_out(refs[:count], local, slice(PACKED, None))
    packed = mm(local[:, PACKED:], projection[...]).astype(BF)
    local[:, :PACKED] = packed
    keys = packed[:, QK : 2 * QK]
    values_t[...] = mm_t(identity(VAL), packed[:, 2 * QK :]).astype(BF)

    def block(index):
        at = block_at(index)
        queries = local[at, :QK]
        rows = []
        all_scores = mm_t(jnp.concatenate([head_of(keys, h, HEAD_QK) for h in range(HEADS)], axis=0), queries)
        for head in range(HEADS):
            scores = all_scores[head * across : (head + 1) * across, :]
            maxima = jnp.max(scores, axis=0, keepdims=True)
            exponent = jnp.exp2((scores - maxima) * EXP2_SCALING)
            totals = jnp.sum(exponent, axis=0, keepdims=True)
            weighted = mm(values_t[head * HEAD_VAL : (head + 1) * HEAD_VAL, :], exponent.astype(BF))
            rows.append((weighted * (1.0 / totals)).astype(BF))
            lse[head : head + 1, at] = maxima * EXP2_SCALING + jnp.log2(totals)
        attended[at, :] = mm_t(identity(BLOCK), jnp.concatenate(rows, axis=0)).astype(BF)

    for_blocks(across // BLOCK, block)


class Place:
    def __init__(self):
        row = lax.axis_index("rows")
        self.col = lax.axis_index("cols")
        self.core = lax.rem(row, 2)
        self.chip_bit = lax.rem(row // 2, 2)
        self.col_bit = lax.rem(self.col, 2)
        self.near_inside = jnp.where(self.core == 0, row > 0, row < lax.axis_size("rows") - 1)
        self.mate_inside = jnp.where(self.core == 0, row < lax.axis_size("rows") - 2, row > 1)
        self.taps = [tap + self.core * (2 - 2 * tap) for tap in range(3)]

    def chosen(self, total, half):
        size = total // 4
        middle = size // 2

        def wanted(rows):
            swapped = jnp.where(rows < middle, rows + middle, rows - middle)
            return (2 * half + self.col_bit) * size + jnp.where(self.chip_bit == 0, rows, swapped)

        return one_hot((size, total), wanted)

    def beside(self, weights, tap):
        return jnp.concatenate([weights[self.taps[tap], b] for b in range(3)], axis=1)

    def stacked(self, weights, tap):
        return jnp.concatenate([weights[self.taps[tap], b] for b in range(3)], axis=0)


def side(total, width, sign):
    left = moved(total[:, :width], -sign)
    right = moved(total[:, 2 * width :], sign)
    return left + total[:, width : 2 * width] + right


def spread(values):
    return jnp.concatenate(
        [moved(values, 1).astype(BF), values.astype(BF), moved(values, -1).astype(BF)], axis=1
    )


def rows_kernel(count, *refs):
    attended, first_kernel, row, term = refs[count:]
    lay_out(refs[:count], row, slice(VAL, None))
    lay_out(refs[:count], term, slice(CONV, None))
    row[:, :VAL] = attended[...]
    term[:, :CONV] = side(mm(attended[...], Place().beside(first_kernel, 0)), CONV, 1).astype(BF)


def far_back_kernel(far, second_t, out):
    back = side(mm(far[:, CONV:], second_t[2]), CONV, -1)
    out[:, :CONV] = far[:, :CONV].astype(F32)
    out[:, CONV:] = back


def turn_kernel(first_kernel, second_kernel, first_t, second_t):
    place = Place()
    eye = identity(CONV)
    for a in range(3):
        first_t[a * CONV : (a + 1) * CONV, :] = mm_t(eye, place.stacked(first_kernel, a)).astype(BF)
        second_t[a] = mm_t(eye, place.stacked(second_kernel, a)).astype(BF)


def prepare_kernel(own, local, lse, soft, keys_t, queries_t, attended_t, features_t, values):
    place = Place()
    across = own.shape[0]
    keys = local[:, QK : 2 * QK]
    keys_t[...] = mm_t(identity(QK), keys).astype(BF)
    pick = jnp.concatenate([place.chosen(VAL, place.core), place.chosen(VAL, 1 - place.core)], axis=0)
    features_t[...] = mm_t(pick, local[:, PACKED:]).astype(BF)
    for head in range(HEADS):
        values[head * across : (head + 1) * across, :] = head_of(local[:, 2 * QK : PACKED], head, HEAD_VAL)

    def block(index):
        at = block_at(index)
        queries = local[at, :QK]
        queries_t[:, at] = mm_t(identity(QK), queries).astype(BF)
        attended_t[:, at] = mm_t(identity(VAL), own[at, :VAL]).astype(BF)
        scores = mm_t(jnp.concatenate([head_of(keys, h, HEAD_QK) for h in range(HEADS)], axis=0), queries)
        for head in range(HEADS):
            rows = slice(head * across, (head + 1) * across)
            soft[rows, at] = jnp.exp2(scores[rows, :] * EXP2_SCALING - lse[head : head + 1, at]).astype(BF)

    for_blocks(across // BLOCK, block)


def masked(inside, row):
    return jnp.where(inside, row, jnp.zeros_like(row))


def conv_term(place, row, kernel, tap):
    return side(mm(row[:, :VAL], place.beside(kernel, tap)), CONV, 1)


def back_term(row, second_t, tap):
    return side(mm(row[:, VAL:], second_t[tap]), CONV, -1)


def store_middle(pre, back, out):
    sigma = 1.0 / (1.0 + jnp.exp(-pre))
    out[:, :CONV] = (pre * sigma).astype(BF)
    out[:, CONV:] = (back * (sigma * (1.0 + pre * (1.0 - sigma)))).astype(BF)


def inner_kernel(own, mate, mate1, first_kernel, second_t, mate_mid, near_part, own_part):
    place = Place()
    mate1 = masked(place.mate_inside, mate1[...])
    near_part[:, :CONV] = conv_term(place, own, first_kernel, 2)
    near_part[:, CONV:] = back_term(own, second_t, 0)
    own_part[:, :CONV] = conv_term(place, own, first_kernel, 1) + conv_term(place, mate, first_kernel, 2)
    own_part[:, CONV:] = back_term(own, second_t, 1) + back_term(mate, second_t, 0)
    rows = (own, mate, mate1)
    pre = sum(conv_term(place, row, first_kernel, a) for a, row in enumerate(rows))
    back = sum(back_term(row, second_t, 2 - a) for a, row in enumerate(rows))
    store_middle(pre, back, mate_mid)


def middle(place, far, near, near_part, own_part, first_kernel, second_t, near_mid, own_mid):
    pre = near_part[:, :CONV] + far[:, :CONV] + conv_term(place, near, first_kernel, 1)
    back = near_part[:, CONV:] + far[:, CONV:] + back_term(near, second_t, 1)
    store_middle(masked(place.near_inside, pre), masked(place.near_inside, back), near_mid)
    pre = own_part[:, :CONV] + conv_term(place, near, first_kernel, 0)
    back = own_part[:, CONV:] + back_term(near, second_t, 2)
    store_middle(pre, back, own_mid)


def conv_grads_kernel(near, own, mate, mate1, own_mid, mate_mid, keep, send):
    place = Place()
    slots = (masked(place.near_inside, near[...]), own[...], mate[...], masked(place.mate_inside, mate1[...]))
    mids = {1: own_mid, 2: mate_mid}

    def store(total, start, step, a):
        for b in range(3):
            at = pl.ds(pl.multiple_of(start + (place.taps[a] * 3 + b) * step, step), step)
            keep[at, :] = total[:step, b * CONV : (b + 1) * CONV]
            send[at, :] = total[step:, b * CONV : (b + 1) * CONV]

    pick = place.chosen(VAL, place.core)
    attended_t = [mm_t(pick, slot[:, :VAL]).astype(BF) for slot in slots]
    slope = {slot: spread(mid[:, CONV:].astype(F32)) for slot, mid in mids.items()}
    for a in range(3):
        total = sum(mm(attended_t[slot + a - 1], slope[slot]) for slot in mids).astype(BF)
        store(total, 0, VAL // PARTS, a)
    pick = place.chosen(CONV, place.core)
    hidden_t = {slot: mm_t(pick, mid[:, :CONV]).astype(BF) for slot, mid in mids.items()}
    cotangent = [spread(slot[:, VAL:].astype(F32)) for slot in slots]
    for a in range(3):
        total = sum(mm(hidden_t[slot], cotangent[slot + 1 - a]) for slot in mids).astype(BF)
        store(total, FIRST_ROWS, CONV // PARTS, a)


def backward_kernel(
    far,
    near,
    mate_mid,
    near_part,
    own_part,
    values,
    soft,
    keys_t,
    queries_t,
    attended_t,
    features_t,
    first_kernel,
    first_t,
    second_t,
    near_mid,
    own_mid,
    grad_out,
    proj_own,
    proj_mate,
    upstream_ref,
    grad_t,
):
    place = Place()
    across = near.shape[0]
    near = masked(place.near_inside, near[...])
    mids = (near_mid, own_mid, mate_mid)
    middle(place, far, near, near_part, own_part, first_kernel, second_t, near_mid, own_mid)
    slopes_beside = jnp.concatenate([mids[2 - a][:, CONV:] for a in range(3)], axis=1)
    upstream_ref[...] = side(mm(slopes_beside, first_t[...]), VAL, -1).astype(BF)
    blocks = across // BLOCK
    if blocks > 1:
        grad_t[...] = jnp.zeros_like(grad_t)

    def add_rows(start, count, terms):
        if blocks > 1:
            grad_t[start : start + count, :] += terms
        else:
            grad_t[start : start + count, :] = terms

    def block(index):
        at = block_at(index)
        upstream = upstream_ref[at, :]
        upstream_t = mm_t(identity(VAL), upstream)
        products = upstream_t * attended_t[:, at].astype(F32)
        upstream_t = upstream_t.astype(BF)
        slopes = mm_t(values[...], upstream)
        for head in range(HEADS):
            rows = slice(head * across, (head + 1) * across)
            qk_rows = slice(head * HEAD_QK, (head + 1) * HEAD_QK)
            val_rows = slice(head * HEAD_VAL, (head + 1) * HEAD_VAL)
            weights = soft[rows, at]
            inner = jnp.sum(products[val_rows, :], axis=0, keepdims=True)
            dscore = (weights.astype(F32) * (slopes[rows, :] - inner)).astype(BF)
            grad_t[qk_rows, at] = SCALING * mm(keys_t[qk_rows, :], dscore)
            add_rows(QK + head * HEAD_QK, HEAD_QK, SCALING * mm_t(queries_t[qk_rows, at], dscore))
            add_rows(2 * QK + head * HEAD_VAL, HEAD_VAL, mm_t(upstream_t[val_rows, :], weights))

    for_blocks(blocks, block)

    grad = grad_t[...].astype(BF)
    grad_out[...] = grad
    step = VAL // PARTS
    total = mm_t(features_t[...], grad).astype(BF)
    for which, target in enumerate((proj_own, proj_mate)):
        for j in range(PACKED // CONV):
            for part in range(2):
                begin = (2 * which + part) * step
                target[part, j * step : (j + 1) * step, :] = total[begin : begin + step, j * CONV : (j + 1) * CONV]


def outputs_kernel(near_mid, own_mid, mate_mid, grad, projection, second_kernel, output_map, input_grad, rows):
    place = Place()
    part_width = output_map.shape[0]
    mids = (near_mid, own_mid, mate_mid)
    rows[...] = side(sum(mm(mids[a][:, :CONV], place.beside(second_kernel, a)) for a in range(3)), CONV, 1)
    output_map[...] = rows[pl.ds(pl.multiple_of(place.col * part_width, part_width), part_width), :].astype(BF)
    own_pixels = one_hot((part_width, rows.shape[0]), lambda pixels: pixels + place.col * part_width)
    input_grad[...] = mm_t(mm_t(own_pixels, grad[...]).astype(BF), projection[...]).astype(BF)


def unpack_kernel(factor, core_flip, *refs):
    pieces = refs[:4]
    outs = refs[-7:-4]
    blocks = refs[-4:-1]
    sem = refs[-1]
    projection_block, first_block, second_block = blocks
    row = lax.axis_index("rows")
    half = lax.rem(row + core_flip, 2)
    chip_bit = lax.rem(row // 2, 2)
    col_bit = lax.rem(lax.axis_index("cols"), 2)
    parts = [2 * lax.rem(col_bit + which // 2, 2) + lax.rem(chip_bit + which % 2, 2) for which in range(4)]
    copies = []

    def send(index, block, out):
        copies.append(pltpu.make_async_copy(block, out, sem.at[index]))
        copies[-1].start()

    def rows_of(which, step):
        return pl.ds(pl.multiple_of(parts[which] * step, step), step)

    def half_of(rows):
        return pl.ds(pl.multiple_of(half * rows, rows), rows)

    step = VAL // PARTS
    for a in range(3):
        for which, piece in enumerate(pieces):
            for b in range(3):
                begin = (3 * a + b) * step
                first_block[a, b, rows_of(which, step), :] = piece[begin : begin + step, :].astype(F32) * factor
        send(a, first_block.at[a], outs[1].at[a, :, half_of(VAL // 2), :])
    for which, piece in enumerate(pieces):
        for j in range(PACKED // CONV):
            begin = FIRST_ROWS + SECOND_ROWS + j * step
            projection_block[rows_of(which, step), j * CONV : (j + 1) * CONV] = (
                piece[begin : begin + step, :].astype(F32) * factor
            )
    send(3, projection_block, outs[0].at[half_of(VAL // 2), :])
    step = CONV // PARTS
    for which, piece in enumerate(pieces):
        for tap in range(9):
            begin = FIRST_ROWS + tap * step
            second_block[tap // 3, tap % 3, rows_of(which, step), :] = (
                piece[begin : begin + step, :].astype(F32) * factor
            )
    send(4, second_block, outs[2].at[:, :, half_of(CONV // 2), :])
    for copy in copies:
        copy.wait()


def unpack(factor, core_flip, pieces, into, **params):
    dims = ((2 * QK, PACKED), (3, 3, VAL, CONV), (3, 3, CONV, CONV))
    return pl.pallas_call(
        functools.partial(unpack_kernel, factor, core_flip),
        out_shape=tuple(shape(*size, dtype=F32) for size in dims),
        in_specs=[VMEM] * 4 + [HBM] * len(into),
        out_specs=[HBM] * 3,
        scratch_shapes=[pltpu.VMEM(size[:-2] + (size[-2] // 2, size[-1]), F32) for size in dims]
        + [pltpu.SemaphoreType.DMA((5,))],
        input_output_aliases={4 + i: i for i in range(len(into))},
        cost_estimate=pl.CostEstimate(flops=10**9, bytes_accessed=4 * 1024 * 1024, transcendentals=0),
        name="unpack_sums",
        **params,
    )(*pieces, *into)


def shape(*dims, dtype=BF):
    return jax.ShapeDtypeStruct(dims, dtype)


def granted(across):
    return dict(compiler_params=pltpu.CompilerParams(vmem_limit_bytes=across * 64 * 1024))


VMEM = pl.BlockSpec(memory_space=pltpu.VMEM)
HBM = pl.BlockSpec(memory_space=pltpu.HBM)


def body(features, projection, first_kernel, second_kernel, cotangent):
    height, part_width, channels = features.shape
    rows_size = lax.axis_size("rows")
    cols_size = lax.axis_size("cols")
    across = part_width * cols_size

    def rows_flip(values, bit):
        return lax.ppermute(values, "rows", [(i, i ^ bit) for i in range(rows_size)])

    def cols_flip(values):
        return lax.ppermute(values, "cols", [(i, i ^ 1) for i in range(cols_size)])

    def wide(values):
        return values.astype(F32)

    def added(one, two):
        return (one + two).astype(BF)

    def call(kernel, out_shape, operands, scratch=(), name=None, flops=10**9):
        return pl.pallas_call(
            kernel,
            out_shape=out_shape,
            in_specs=[VMEM] * len(operands),
            out_specs=[VMEM] * len(out_shape),
            scratch_shapes=scratch,
            cost_estimate=pl.CostEstimate(flops=flops, bytes_accessed=flops // 250, transcendentals=0),
            name=name,
            **granted(across),
        )(*operands)

    features, cotangent = (features[0], cotangent[0])
    if cols_size == 2:
        swapped = cols_flip(features)
        cotangent = (cotangent, cols_flip(cotangent))
        projection, features = fetch((projection, features))
        features = (features, swapped)
    else:
        features, cotangent = (
            (lax.all_gather(array, "cols", axis=0, tiled=True),) for array in (features, cotangent)
        )
    attended, local, lse = call(
        functools.partial(forward_kernel, len(features)),
        (shape(across, VAL), shape(across, PACKED + channels), shape(HEADS, across, dtype=F32)),
        (*features, projection),
        (pltpu.VMEM((VAL, across), BF),),
        name="attention_forward",
    )
    own, term = call(
        functools.partial(rows_kernel, len(cotangent)),
        (shape(across, VAL + CONV), shape(across, 2 * CONV)),
        (*cotangent, attended, first_kernel),
        name="rows",
    )
    first_kernel, second_kernel = fetch((first_kernel, second_kernel), (lse,), 10**5)
    last = rows_size - 1
    out = [(i, i + 2) for i in range(0, last - 1, 2)] + [(i, i - 2) for i in range(3, rows_size, 2)]
    out += [(last - 1, last), (1, 0)]
    back = [(j, i) for i, j in out]
    first_t, second_t = call(
        turn_kernel,
        (shape(3 * CONV, 3 * VAL), shape(3, CONV, 3 * CONV)),
        (first_kernel, second_kernel),
        name="turn",
        flops=10**7,
    )
    mate1 = lax.ppermute(own, "rows", back)
    far = lax.ppermute(term, "rows", out)
    (far,) = call(
        far_back_kernel, (shape(across, 2 * CONV, dtype=F32),), (far, second_t), name="far_back", flops=4 * 10**9
    )
    mate = rows_flip(own, 1)
    near = rows_flip(mate1, 1)
    soft, keys_t, queries_t, attended_t, features_t, values = call(
        prepare_kernel,
        (
            shape(HEADS * across, across),
            shape(QK, across),
            shape(QK, across),
            shape(VAL, across),
            shape(VAL // 2, across),
            shape(HEADS * across, VAL),
        ),
        (own, local, lse),
        name="prepare",
        flops=10**7,
    )
    mate_mid, near_part, own_part = call(
        inner_kernel,
        (shape(across, 2 * CONV), shape(across, 2 * CONV, dtype=F32), shape(across, 2 * CONV, dtype=F32)),
        (own, mate, mate1, first_kernel, second_t),
        name="inner",
    )
    near_mid, own_mid, grad, proj_own, proj_mate = call(
        backward_kernel,
        (
            shape(across, 2 * CONV),
            shape(across, 2 * CONV),
            shape(PACKED, across),
            shape(2, PROJ_ROWS, CONV),
            shape(2, PROJ_ROWS, CONV),
        ),
        (
            far,
            near,
            mate_mid,
            near_part,
            own_part,
            values,
            soft,
            keys_t,
            queries_t,
            attended_t,
            features_t,
            first_kernel,
            first_t,
            second_t,
        ),
        (pltpu.VMEM((across, VAL), BF), pltpu.VMEM((PACKED, across), F32)),
        name="block_backward",
    )
    keep, send = call(
        conv_grads_kernel,
        (shape(FIRST_ROWS + SECOND_ROWS, CONV),) * 2,
        (near, own, mate, mate1, own_mid, mate_mid),
        name="conv_grads",
    )
    output_map, input_grad = call(
        outputs_kernel,
        (shape(part_width, CONV), shape(part_width, channels)),
        (near_mid, own_mid, mate_mid, grad, projection, second_kernel),
        (pltpu.VMEM((across, CONV), F32),),
        name="outputs",
    )
    proj_sum = added(wide(proj_own), wide(rows_flip(proj_mate, 1)))
    sent = jnp.concatenate([send, proj_sum[1]], axis=0)
    kept = jnp.concatenate([keep, proj_sum[0]], axis=0)
    if rows_size > 4:
        total = added(wide(kept) + wide(rows_flip(kept, 4)), wide(rows_flip(sent, 2)) + wide(rows_flip(sent, 6)))
    else:
        total = added(wide(kept), wide(rows_flip(sent, 2)))
    bit = 8
    while bit < rows_size:
        total = added(wide(total), wide(rows_flip(total, bit)))
        bit *= 2
    total, output_map, input_grad = lax.optimization_barrier((total, output_map, input_grad))
    chip = rows_flip(total, 2)
    side = cols_flip(total)
    corner = lax.ppermute(
        total,
        ("rows", "cols"),
        [(i * cols_size + j, (i ^ 2) * cols_size + (j ^ 1)) for i in range(rows_size) for j in range(cols_size)],
    )
    four = (total, chip, side, corner)
    factor = 1.0 / math.sqrt(height * across * rows_size)
    halves = unpack(factor, 0, four, (), **granted(across))
    projection_grad, first_grad, second_grad = unpack(
        factor, 1, [rows_flip(piece, 1) for piece in four], halves, **granted(across)
    )
    return (output_map[None], input_grad[None], projection_grad, first_grad, second_grad)


def solution(mesh):
    placed = (P("rows", "cols", None), P(), P(), P(), P("rows", "cols", None))
    return jax.shard_map(
        body,
        mesh=mesh,
        in_specs=placed,
        out_specs=(P("rows", "cols", None), P("rows", "cols", None), P(), P(), P()),
        check_vma=False,
    )
```

```python
import functools
import math

import jax
import jax.numpy as jnp
from jax import lax
from jax.experimental import pallas as pl
from jax.experimental.pallas import tpu as pltpu
from jax.sharding import PartitionSpec as P

QK = 128
VAL = 256
HEADS = 8
CONV = 128
HEAD_QK = QK // HEADS
HEAD_VAL = VAL // HEADS
PACKED = 2 * QK + VAL
BLOCK = 256
BF = jnp.bfloat16
F32 = jnp.float32
SCALING = HEAD_QK ** (-0.5)
EXP2_SCALING = SCALING * math.log2(math.e)

PARTS = 8
FIRST_ROWS = 9 * VAL // PARTS
SECOND_ROWS = 9 * CONV // PARTS
CONV_ROWS = FIRST_ROWS + SECOND_ROWS
PROJ_ROWS = PACKED // CONV * (VAL // PARTS)


def mm(a, b):
    return lax.dot_general(a, b, (((1,), (0,)), ((), ())), preferred_element_type=F32)


def mm_t(a, b):
    return lax.dot_general(a, b, (((1,), (1,)), ((), ())), preferred_element_type=F32)


def one_hot(shape, wanted):
    rows = lax.broadcasted_iota(jnp.int32, shape, 0)
    columns = lax.broadcasted_iota(jnp.int32, shape, 1)
    return jnp.where(columns == wanted(rows), 1.0, 0.0).astype(BF)


def identity(size):
    return one_hot((size, size), lambda rows: rows)


def head_of(values, head, width):
    lanes = lax.broadcasted_iota(jnp.int32, values.shape, 1)
    return jnp.where(lanes // width == head, values, jnp.zeros_like(values))


def moved(values, step):
    count = values.shape[0]
    turned = pltpu.roll(values, (-step) % count, 0)
    at = lax.broadcasted_iota(jnp.int32, values.shape, 0)
    return jnp.where(at == (count - 1 if step > 0 else 0), 0.0, turned)


def for_blocks(count, run):
    if count == 1:
        run(0)
    else:
        lax.fori_loop(0, count, lambda i, carry: (run(i), carry)[1], 0)


def block_at(index):
    return pl.ds(index if isinstance(index, int) else pl.multiple_of(index * BLOCK, BLOCK), BLOCK)


def fetch_kernel(count, *refs):
    targets = refs[-1 - count : -1]
    copies = [pltpu.make_async_copy(refs[i], targets[i], refs[-1].at[i]) for i in range(count)]
    for copy in copies:
        copy.start()
    for copy in copies:
        copy.wait()


def fetch(arrays, after=(), nbytes=4 * 1024 * 1024):
    return pl.pallas_call(
        functools.partial(fetch_kernel, len(arrays)),
        out_shape=tuple(shape(*array.shape) for array in arrays),
        in_specs=[HBM] * (len(arrays) + len(after)),
        out_specs=[VMEM] * len(arrays),
        scratch_shapes=[pltpu.SemaphoreType.DMA((len(arrays),))],
        cost_estimate=pl.CostEstimate(flops=0, bytes_accessed=nbytes, transcendentals=0),
        name="fetch",
        **granted(32),
    )(*arrays, *after)


def lay_out(pieces, target, lanes):
    for which, piece in enumerate(pieces):
        width = piece.shape[0]
        if len(pieces) == 1:
            at = slice(None)
        else:
            place = lax.rem(lax.axis_index("cols") + which, 2)
            at = pl.ds(pl.multiple_of(place * width, width), width)
        target[at, lanes] = piece[...]


def forward_kernel(count, *refs):
    projection, attended, local, lse, values_t = refs[count:]
    across = attended.shape[0]
    lay_out(refs[:count], local, slice(PACKED, None))
    packed = mm(local[:, PACKED:], projection[...]).astype(BF)
    local[:, :PACKED] = packed
    keys = packed[:, QK : 2 * QK]
    values_t[...] = mm_t(identity(VAL), packed[:, 2 * QK :]).astype(BF)

    def block(index):
        at = block_at(index)
        queries = local[at, :QK]
        rows = []
        all_scores = mm_t(jnp.concatenate([head_of(keys, h, HEAD_QK) for h in range(HEADS)], axis=0), queries)
        for head in range(HEADS):
            scores = all_scores[head * across : (head + 1) * across, :]
            maxima = jnp.max(scores, axis=0, keepdims=True)
            exponent = jnp.exp2((scores - maxima) * EXP2_SCALING)
            totals = jnp.sum(exponent, axis=0, keepdims=True)
            weighted = mm(values_t[head * HEAD_VAL : (head + 1) * HEAD_VAL, :], exponent.astype(BF))
            rows.append((weighted * (1.0 / totals)).astype(BF))
            lse[head : head + 1, at] = maxima * EXP2_SCALING + jnp.log2(totals)
        attended[at, :] = mm_t(identity(BLOCK), jnp.concatenate(rows, axis=0)).astype(BF)

    for_blocks(across // BLOCK, block)


class Place:
    def __init__(self):
        row = lax.axis_index("rows")
        self.col = lax.axis_index("cols")
        self.core = lax.rem(row, 2)
        self.chip_bit = lax.rem(row // 2, 2)
        self.col_bit = lax.rem(self.col, 2)
        self.near_inside = jnp.where(self.core == 0, row > 0, row < lax.axis_size("rows") - 1)
        self.mate_inside = jnp.where(self.core == 0, row < lax.axis_size("rows") - 2, row > 1)
        self.taps = [tap + self.core * (2 - 2 * tap) for tap in range(3)]

    def chosen(self, total, half):
        size = total // 4
        middle = size // 2

        def wanted(rows):
            swapped = jnp.where(rows < middle, rows + middle, rows - middle)
            return (2 * half + self.col_bit) * size + jnp.where(self.chip_bit == 0, rows, swapped)

        return one_hot((size, total), wanted)

    def beside(self, weights, tap):
        return jnp.concatenate([weights[self.taps[tap], b] for b in range(3)], axis=1)

    def stacked(self, weights, tap):
        return jnp.concatenate([weights[self.taps[tap], b] for b in range(3)], axis=0)


def side(total, width, sign):
    left = moved(total[:, :width], -sign)
    right = moved(total[:, 2 * width :], sign)
    return left + total[:, width : 2 * width] + right


def spread(values):
    return jnp.concatenate(
        [moved(values, 1).astype(BF), values.astype(BF), moved(values, -1).astype(BF)], axis=1
    )


def rows_kernel(attended, first_kernel, far_cot, cotangent, mate1_cot, term, bundle):
    term[...] = side(mm(attended[...], Place().beside(first_kernel, 0)), CONV, 1).astype(BF)
    for row, half in enumerate((far_cot, cotangent, mate1_cot)):
        bundle[row] = half[...]


def assemble_kernel(count, *refs):
    far, pair = refs[count:]
    for row, target in enumerate((far, pair.at[0], pair.at[1])):
        lay_out([piece.at[row] for piece in refs[:count]], target, slice(None))


def turn_kernel(first_kernel, second_kernel, first_t, second_t):
    place = Place()
    eye = identity(CONV)
    for a in range(3):
        first_t[a * CONV : (a + 1) * CONV, :] = mm_t(eye, place.stacked(first_kernel, a)).astype(BF)
        second_t[a] = mm_t(eye, place.stacked(second_kernel, a)).astype(BF)


def prepare_kernel(own, local, lse, soft, keys_t, queries_t, attended_t, features_t, values):
    place = Place()
    across = own.shape[0]
    keys = local[:, QK : 2 * QK]
    keys_t[...] = mm_t(identity(QK), keys).astype(BF)
    pick = jnp.concatenate([place.chosen(VAL, place.core), place.chosen(VAL, 1 - place.core)], axis=0)
    features_t[...] = mm_t(pick, local[:, PACKED:]).astype(BF)
    for head in range(HEADS):
        values[head * across : (head + 1) * across, :] = head_of(local[:, 2 * QK : PACKED], head, HEAD_VAL)

    def block(index):
        at = block_at(index)
        queries = local[at, :QK]
        queries_t[:, at] = mm_t(identity(QK), queries).astype(BF)
        attended_t[:, at] = mm_t(identity(VAL), own[at, :]).astype(BF)
        scores = mm_t(jnp.concatenate([head_of(keys, h, HEAD_QK) for h in range(HEADS)], axis=0), queries)
        for head in range(HEADS):
            rows = slice(head * across, (head + 1) * across)
            soft[rows, at] = jnp.exp2(scores[rows, :] * EXP2_SCALING - lse[head : head + 1, at]).astype(BF)

    for_blocks(across // BLOCK, block)


def masked(inside, row):
    return jnp.where(inside, row, jnp.zeros_like(row))


def conv_term(place, row, kernel, tap):
    return side(mm(row[...], place.beside(kernel, tap)), CONV, 1)


def back_term(row, second_t, tap):
    return side(mm(row[...], second_t[tap]), CONV, -1)


def cotangent_terms_kernel(far_cot, pair_cot, second_t, near_back, own_back, mate_back):
    place = Place()
    own = pair_cot[0]
    near_back[...] = back_term(far_cot, second_t, 2) + back_term(own, second_t, 0)
    own_back[...] = back_term(own, second_t, 1)
    mate1 = masked(place.mate_inside, pair_cot[1])
    mate_back[...] = back_term(own, second_t, 2) + back_term(mate1, second_t, 0)


def attended_terms_kernel(own, mate, first_kernel, near_pre, own_pre, mate_pre):
    place = Place()
    near_pre[...] = conv_term(place, own, first_kernel, 2)
    own_pre[...] = conv_term(place, own, first_kernel, 1) + conv_term(place, mate, first_kernel, 2)
    mate_pre[...] = conv_term(place, own, first_kernel, 0) + conv_term(place, mate, first_kernel, 1)


def store_middle(pre, back, out):
    sigma = 1.0 / (1.0 + jnp.exp(-pre))
    out[:, :CONV] = (pre * sigma).astype(BF)
    out[:, CONV:] = (back * (sigma * (1.0 + pre * (1.0 - sigma)))).astype(BF)


def near_terms_kernel(far_term, near_pre, near_terms):
    near_terms[...] = near_pre[...] + far_term[...].astype(F32)


def mate_middle_kernel(
    mate1, mate_cot, mate_pre, mate_back, own_back, first_kernel, second_t, mate_mid, own_terms
):
    place = Place()
    own_terms[...] = own_back[...] + back_term(mate_cot[0], second_t, 0)
    pre = mate_pre[...] + conv_term(place, masked(place.mate_inside, mate1[...]), first_kernel, 2)
    store_middle(pre, mate_back[...] + back_term(mate_cot[0], second_t, 1), mate_mid)


def conv_grads_kernel(near, own, mate, mate1, pair_cot, mate_cot, own_mid, mate_mid, keep, send):
    place = Place()
    slots = (masked(place.near_inside, near[...]), own[...], mate[...], masked(place.mate_inside, mate1[...]))
    cots = (
        masked(place.near_inside, mate_cot[1]),
        pair_cot[0],
        mate_cot[0],
        masked(place.mate_inside, pair_cot[1]),
    )
    mids = {1: own_mid, 2: mate_mid}

    def store(total, start, step, a):
        for b in range(3):
            at = pl.ds(pl.multiple_of(start + (place.taps[a] * 3 + b) * step, step), step)
            keep[at, :] = total[:step, b * CONV : (b + 1) * CONV]
            send[at, :] = total[step:, b * CONV : (b + 1) * CONV]

    pick = place.chosen(VAL, place.core)
    attended_t = [mm_t(pick, slot).astype(BF) for slot in slots]
    slope = {slot: spread(mid[:, CONV:].astype(F32)) for slot, mid in mids.items()}
    for a in range(3):
        total = sum(mm(attended_t[slot + a - 1], slope[slot]) for slot in mids).astype(BF)
        store(total, 0, VAL // PARTS, a)
    pick = place.chosen(CONV, place.core)
    hidden_t = {slot: mm_t(pick, mid[:, :CONV]).astype(BF) for slot, mid in mids.items()}
    cotangent = [spread(cot.astype(F32)) for cot in cots]
    for a in range(3):
        total = sum(mm(hidden_t[slot], cotangent[slot + 1 - a]) for slot in mids).astype(BF)
        store(total, FIRST_ROWS, CONV // PARTS, a)


def backward_kernel(
    near,
    mate_cot,
    mate_mid,
    near_pre,
    near_back,
    own_pre,
    own_back,
    values,
    soft,
    keys_t,
    queries_t,
    attended_t,
    features_t,
    first_kernel,
    first_t,
    second_t,
    near_mid,
    own_mid,
    grad_out,
    proj_own,
    proj_mate,
    upstream_ref,
    grad_t,
):
    place = Place()
    across = near.shape[0]
    near = masked(place.near_inside, near[...])
    mids = (near_mid, own_mid, mate_mid)
    pre = near_pre[...] + conv_term(place, near, first_kernel, 1)
    near_cot = masked(place.near_inside, mate_cot[1])
    back = near_back[...] + back_term(near_cot, second_t, 1)
    store_middle(masked(place.near_inside, pre), masked(place.near_inside, back), near_mid)
    pre = own_pre[...] + conv_term(place, near, first_kernel, 0)
    store_middle(pre, own_back[...] + back_term(near_cot, second_t, 2), own_mid)
    slopes_beside = jnp.concatenate([mids[2 - a][:, CONV:] for a in range(3)], axis=1)
    upstream_ref[...] = side(mm(slopes_beside, first_t[...]), VAL, -1).astype(BF)
    blocks = across // BLOCK
    if blocks > 1:
        grad_t[...] = jnp.zeros_like(grad_t)

    def add_rows(start, count, terms):
        if blocks > 1:
            grad_t[start : start + count, :] += terms
        else:
            grad_t[start : start + count, :] = terms

    def block(index):
        at = block_at(index)
        upstream = upstream_ref[at, :]
        upstream_t = mm_t(identity(VAL), upstream)
        products = upstream_t * attended_t[:, at].astype(F32)
        upstream_t = upstream_t.astype(BF)
        slopes = mm_t(values[...], upstream)
        for head in range(HEADS):
            rows = slice(head * across, (head + 1) * across)
            qk_rows = slice(head * HEAD_QK, (head + 1) * HEAD_QK)
            val_rows = slice(head * HEAD_VAL, (head + 1) * HEAD_VAL)
            weights = soft[rows, at]
            inner = jnp.sum(products[val_rows, :], axis=0, keepdims=True)
            dscore = (weights.astype(F32) * (slopes[rows, :] - inner)).astype(BF)
            grad_t[qk_rows, at] = SCALING * mm(keys_t[qk_rows, :], dscore)
            add_rows(QK + head * HEAD_QK, HEAD_QK, SCALING * mm_t(queries_t[qk_rows, at], dscore))
            add_rows(2 * QK + head * HEAD_VAL, HEAD_VAL, mm_t(upstream_t[val_rows, :], weights))

    for_blocks(blocks, block)

    grad = grad_t[...].astype(BF)
    grad_out[...] = grad
    step = VAL // PARTS
    total = mm_t(features_t[...], grad).astype(BF)
    for which, target in enumerate((proj_own, proj_mate)):
        for j in range(PACKED // CONV):
            for part in range(2):
                begin = (2 * which + part) * step
                target[part, j * step : (j + 1) * step, :] = total[begin : begin + step, j * CONV : (j + 1) * CONV]


def outputs_kernel(near_mid, own_mid, mate_mid, grad, projection, second_kernel, output_map, input_grad, rows):
    place = Place()
    part_width = output_map.shape[0]
    mids = (near_mid, own_mid, mate_mid)
    rows[...] = side(sum(mm(mids[a][:, :CONV], place.beside(second_kernel, a)) for a in range(3)), CONV, 1)
    output_map[...] = rows[pl.ds(pl.multiple_of(place.col * part_width, part_width), part_width), :].astype(BF)
    own_pixels = one_hot((part_width, rows.shape[0]), lambda pixels: pixels + place.col * part_width)
    input_grad[...] = mm_t(mm_t(own_pixels, grad[...]).astype(BF), projection[...]).astype(BF)


def unpack_kernel(factor, core_flip, *refs):
    pieces = refs[:4]
    outs = refs[-7:-4]
    blocks = refs[-4:-1]
    sem = refs[-1]
    projection_block, first_block, second_block = blocks
    row = lax.axis_index("rows")
    half = lax.rem(row + core_flip, 2)
    chip_bit = lax.rem(row // 2, 2)
    col_bit = lax.rem(lax.axis_index("cols"), 2)
    parts = [2 * lax.rem(col_bit + which // 2, 2) + lax.rem(chip_bit + which % 2, 2) for which in range(4)]
    copies = []

    def send(index, block, out):
        copies.append(pltpu.make_async_copy(block, out, sem.at[index]))
        copies[-1].start()

    def rows_of(which, step):
        return pl.ds(pl.multiple_of(parts[which] * step, step), step)

    def half_of(rows):
        return pl.ds(pl.multiple_of(half * rows, rows), rows)

    step = VAL // PARTS
    for a in range(3):
        for which, piece in enumerate(pieces):
            for b in range(3):
                begin = (3 * a + b) * step
                first_block[a, b, rows_of(which, step), :] = piece[begin : begin + step, :].astype(F32) * factor
        send(a, first_block.at[a], outs[1].at[a, :, half_of(VAL // 2), :])
    for which, piece in enumerate(pieces):
        for j in range(PACKED // CONV):
            begin = FIRST_ROWS + SECOND_ROWS + j * step
            projection_block[rows_of(which, step), j * CONV : (j + 1) * CONV] = (
                piece[begin : begin + step, :].astype(F32) * factor
            )
    send(3, projection_block, outs[0].at[half_of(VAL // 2), :])
    step = CONV // PARTS
    for which, piece in enumerate(pieces):
        for tap in range(9):
            begin = FIRST_ROWS + tap * step
            second_block[tap // 3, tap % 3, rows_of(which, step), :] = (
                piece[begin : begin + step, :].astype(F32) * factor
            )
    send(4, second_block, outs[2].at[:, :, half_of(CONV // 2), :])
    for copy in copies:
        copy.wait()


def unpack(factor, core_flip, pieces, into, **params):
    dims = ((2 * QK, PACKED), (3, 3, VAL, CONV), (3, 3, CONV, CONV))
    return pl.pallas_call(
        functools.partial(unpack_kernel, factor, core_flip),
        out_shape=tuple(shape(*size, dtype=F32) for size in dims),
        in_specs=[VMEM] * 4 + [HBM] * len(into),
        out_specs=[HBM] * 3,
        scratch_shapes=[pltpu.VMEM(size[:-2] + (size[-2] // 2, size[-1]), F32) for size in dims]
        + [pltpu.SemaphoreType.DMA((5,))],
        input_output_aliases={4 + i: i for i in range(len(into))},
        cost_estimate=pl.CostEstimate(flops=10**9, bytes_accessed=4 * 1024 * 1024, transcendentals=0),
        name="unpack_sums",
        **params,
    )(*pieces, *into)


def shape(*dims, dtype=BF):
    return jax.ShapeDtypeStruct(dims, dtype)


def granted(across):
    return dict(compiler_params=pltpu.CompilerParams(vmem_limit_bytes=across * 64 * 1024))


VMEM = pl.BlockSpec(memory_space=pltpu.VMEM)
HBM = pl.BlockSpec(memory_space=pltpu.HBM)


def body(features, projection, first_kernel, second_kernel, cotangent):
    height, part_width, channels = features.shape
    rows_size = lax.axis_size("rows")
    cols_size = lax.axis_size("cols")
    across = part_width * cols_size

    def rows_flip(values, bit):
        return lax.ppermute(values, "rows", [(i, i ^ bit) for i in range(rows_size)])

    def cols_flip(values):
        return lax.ppermute(values, "cols", [(i, i ^ 1) for i in range(cols_size)])

    def wide(values):
        return values.astype(F32)

    def added(one, two):
        return (one + two).astype(BF)

    def call(kernel, out_shape, operands, scratch=(), name=None, flops=10**9):
        return pl.pallas_call(
            kernel,
            out_shape=out_shape,
            in_specs=[VMEM] * len(operands),
            out_specs=[VMEM] * len(out_shape),
            scratch_shapes=scratch,
            cost_estimate=pl.CostEstimate(flops=flops, bytes_accessed=flops // 250, transcendentals=0),
            name=name,
            **granted(across),
        )(*operands)

    features, cotangent = (features[0], cotangent[0])
    last = rows_size - 1
    out = [(i, i + 2) for i in range(0, last - 1, 2)] + [(i, i - 2) for i in range(3, rows_size, 2)]
    out += [(last - 1, last), (1, 0)]
    back = [(j, i) for i, j in out]
    if cols_size == 2:
        swapped = cols_flip(features)
        out_cot = lax.ppermute(cotangent, "rows", out)
        back_cot = lax.ppermute(cotangent, "rows", back)
        projection, features = fetch((projection, features))
        features = (features, swapped)
    else:
        out_cot = lax.ppermute(cotangent, "rows", out)
        back_cot = lax.ppermute(cotangent, "rows", back)
        features = (lax.all_gather(features, "cols", axis=0, tiled=True),)
    own, local, lse = call(
        functools.partial(forward_kernel, len(features)),
        (shape(across, VAL), shape(across, PACKED + channels), shape(HEADS, across, dtype=F32)),
        (*features, projection),
        (pltpu.VMEM((VAL, across), BF),),
        name="attention_forward",
    )
    term, bundle = call(
        rows_kernel,
        (shape(across, CONV), shape(3, part_width, CONV)),
        (own, first_kernel, out_cot, cotangent, back_cot),
        name="rows",
    )
    first_kernel, second_kernel = fetch((first_kernel, second_kernel), (lse,), 10**4)
    first_t, second_t = call(
        turn_kernel,
        (shape(3 * CONV, 3 * VAL), shape(3, CONV, 3 * CONV)),
        (first_kernel, second_kernel),
        name="turn",
        flops=10**6,
    )
    mate1 = lax.ppermute(own, "rows", back)
    if cols_size == 2:
        bundles = (bundle, cols_flip(bundle))
    else:
        bundles = (lax.all_gather(bundle, "cols", axis=1, tiled=True),)
    far = lax.ppermute(term, "rows", out)
    mate = rows_flip(own, 1)
    terms = (shape(across, CONV, dtype=F32),) * 3
    near_pre, own_pre, mate_pre = call(
        attended_terms_kernel, terms, (own, mate, first_kernel), name="attended_terms", flops=10**6
    )
    bundles, near_pre = lax.optimization_barrier((bundles, near_pre))
    far_cot, pair_cot = call(
        functools.partial(assemble_kernel, len(bundles)),
        (shape(across, CONV), shape(2, across, CONV)),
        bundles,
        name="assemble",
        flops=10**6,
    )
    mate_cot = rows_flip(pair_cot, 1)
    near = rows_flip(mate1, 1)
    soft, keys_t, queries_t, attended_t, features_t, values = call(
        prepare_kernel,
        (
            shape(HEADS * across, across),
            shape(QK, across),
            shape(QK, across),
            shape(VAL, across),
            shape(VAL // 2, across),
            shape(HEADS * across, VAL),
        ),
        (own, local, lse),
        name="prepare",
        flops=10**6,
    )
    near_back, own_back, mate_back = call(
        cotangent_terms_kernel, terms, (far_cot, pair_cot, second_t), name="cotangent_terms", flops=10**6
    )
    (near_pre,) = call(near_terms_kernel, terms[:1], (far, near_pre), name="near_terms", flops=4 * 10**9)
    mate_mid, own_back = call(
        mate_middle_kernel,
        (shape(across, 2 * CONV), terms[0]),
        (mate1, mate_cot, mate_pre, mate_back, own_back, first_kernel, second_t),
        name="mate_middle",
    )
    near_mid, own_mid, grad, proj_own, proj_mate = call(
        backward_kernel,
        (
            shape(across, 2 * CONV),
            shape(across, 2 * CONV),
            shape(PACKED, across),
            shape(2, PROJ_ROWS, CONV),
            shape(2, PROJ_ROWS, CONV),
        ),
        (
            near,
            mate_cot,
            mate_mid,
            near_pre,
            near_back,
            own_pre,
            own_back,
            values,
            soft,
            keys_t,
            queries_t,
            attended_t,
            features_t,
            first_kernel,
            first_t,
            second_t,
        ),
        (pltpu.VMEM((across, VAL), BF), pltpu.VMEM((PACKED, across), F32)),
        name="block_backward",
    )
    keep, send = call(
        conv_grads_kernel,
        (shape(FIRST_ROWS + SECOND_ROWS, CONV),) * 2,
        (near, own, mate, mate1, pair_cot, mate_cot, own_mid, mate_mid),
        name="conv_grads",
    )
    output_map, input_grad = call(
        outputs_kernel,
        (shape(part_width, CONV), shape(part_width, channels)),
        (near_mid, own_mid, mate_mid, grad, projection, second_kernel),
        (pltpu.VMEM((across, CONV), F32),),
        name="outputs",
    )
    proj_sum = added(wide(proj_own), wide(rows_flip(proj_mate, 1)))
    sent = jnp.concatenate([send, proj_sum[1]], axis=0)
    kept = jnp.concatenate([keep, proj_sum[0]], axis=0)
    if rows_size > 4:
        total = added(wide(kept) + wide(rows_flip(kept, 4)), wide(rows_flip(sent, 2)) + wide(rows_flip(sent, 6)))
    else:
        total = added(wide(kept), wide(rows_flip(sent, 2)))
    bit = 8
    while bit < rows_size:
        total = added(wide(total), wide(rows_flip(total, bit)))
        bit *= 2
    total, output_map, input_grad = lax.optimization_barrier((total, output_map, input_grad))
    chip = rows_flip(total, 2)
    side = cols_flip(total)
    corner = lax.ppermute(
        total,
        ("rows", "cols"),
        [(i * cols_size + j, (i ^ 2) * cols_size + (j ^ 1)) for i in range(rows_size) for j in range(cols_size)],
    )
    four = (total, chip, side, corner)
    factor = 1.0 / math.sqrt(height * across * rows_size)
    halves = unpack(factor, 0, four, (), **granted(across))
    projection_grad, first_grad, second_grad = unpack(
        factor, 1, [rows_flip(piece, 1) for piece in four], halves, **granted(across)
    )
    return (output_map[None], input_grad[None], projection_grad, first_grad, second_grad)


def solution(mesh):
    placed = (P("rows", "cols", None), P(), P(), P(), P("rows", "cols", None))
    return jax.shard_map(
        body,
        mesh=mesh,
        in_specs=placed,
        out_specs=(P("rows", "cols", None), P("rows", "cols", None), P(), P(), P()),
        check_vma=False,
    )
```

```python
import functools
import math

import jax
import jax.numpy as jnp
from jax import lax
from jax.experimental import pallas as pl
from jax.experimental.pallas import tpu as pltpu
from jax.sharding import PartitionSpec as P

QK = 128
VAL = 256
HEADS = 8
CONV = 128
HEAD_QK = QK // HEADS
HEAD_VAL = VAL // HEADS
PACKED = 2 * QK + VAL
BLOCK = 256
BF = jnp.bfloat16
F32 = jnp.float32
SCALING = HEAD_QK ** (-0.5)
EXP2_SCALING = SCALING * math.log2(math.e)

PARTS = 8
FIRST_ROWS = 9 * VAL // PARTS
SECOND_ROWS = 9 * CONV // PARTS
CONV_ROWS = FIRST_ROWS + SECOND_ROWS
PROJ_ROWS = PACKED // CONV * (VAL // PARTS)


def mm(a, b):
    return lax.dot_general(a, b, (((1,), (0,)), ((), ())), preferred_element_type=F32)


def mm_t(a, b):
    return lax.dot_general(a, b, (((1,), (1,)), ((), ())), preferred_element_type=F32)


def one_hot(shape, wanted):
    rows = lax.broadcasted_iota(jnp.int32, shape, 0)
    columns = lax.broadcasted_iota(jnp.int32, shape, 1)
    return jnp.where(columns == wanted(rows), 1.0, 0.0).astype(BF)


def identity(size):
    return one_hot((size, size), lambda rows: rows)


def head_of(values, head, width):
    lanes = lax.broadcasted_iota(jnp.int32, values.shape, 1)
    return jnp.where(lanes // width == head, values, jnp.zeros_like(values))


def moved(values, step):
    count = values.shape[0]
    turned = pltpu.roll(values, (-step) % count, 0)
    at = lax.broadcasted_iota(jnp.int32, values.shape, 0)
    return jnp.where(at == (count - 1 if step > 0 else 0), 0.0, turned)


def for_blocks(count, run):
    if count == 1:
        run(0)
    else:
        lax.fori_loop(0, count, lambda i, carry: (run(i), carry)[1], 0)


def block_at(index):
    return pl.ds(index if isinstance(index, int) else pl.multiple_of(index * BLOCK, BLOCK), BLOCK)


def fetch_kernel(count, *refs):
    targets = refs[-1 - count : -1]
    copies = [pltpu.make_async_copy(refs[i], targets[i], refs[-1].at[i]) for i in range(count)]
    for copy in copies:
        copy.start()
    for copy in copies:
        copy.wait()


def fetch(arrays, after=(), nbytes=4 * 1024 * 1024):
    return pl.pallas_call(
        functools.partial(fetch_kernel, len(arrays)),
        out_shape=tuple(shape(*array.shape) for array in arrays),
        in_specs=[HBM] * (len(arrays) + len(after)),
        out_specs=[VMEM] * len(arrays),
        scratch_shapes=[pltpu.SemaphoreType.DMA((len(arrays),))],
        cost_estimate=pl.CostEstimate(flops=0, bytes_accessed=nbytes, transcendentals=0),
        name="fetch",
        **granted(32),
    )(*arrays, *after)


def lay_out(pieces, target, lanes):
    for which, piece in enumerate(pieces):
        width = piece.shape[0]
        if len(pieces) == 1:
            at = slice(None)
        else:
            place = lax.rem(lax.axis_index("cols") + which, 2)
            at = pl.ds(pl.multiple_of(place * width, width), width)
        target[at, lanes] = piece[...]


def forward_kernel(count, *refs):
    projection, attended, local, stats, values_t = refs[count:]
    across = attended.shape[0]
    lay_out(refs[:count], local, slice(PACKED, None))
    packed = mm(local[:, PACKED:], projection[...]).astype(BF)
    local[:, :PACKED] = packed
    keys = packed[:, QK : 2 * QK]
    values_t[...] = mm_t(identity(VAL), packed[:, 2 * QK :]).astype(BF)

    def block(index):
        at = block_at(index)
        queries = local[at, :QK]
        rows = []
        all_scores = mm_t(jnp.concatenate([head_of(keys, h, HEAD_QK) for h in range(HEADS)], axis=0), queries)
        for head in range(HEADS):
            scores = all_scores[head * across : (head + 1) * across, :]
            maxima = jnp.max(scores, axis=0, keepdims=True)
            exponent = jnp.exp2((scores - maxima) * EXP2_SCALING)
            totals = jnp.sum(exponent, axis=0, keepdims=True)
            weighted = mm(values_t[head * HEAD_VAL : (head + 1) * HEAD_VAL, :], exponent.astype(BF))
            rows.append((weighted * (1.0 / totals)).astype(BF))
            stats[head : head + 1, at] = maxima
            stats[HEADS + head : HEADS + head + 1, at] = jnp.log2(totals)
        attended[at, :] = mm_t(identity(BLOCK), jnp.concatenate(rows, axis=0)).astype(BF)

    for_blocks(across // BLOCK, block)


class Place:
    def __init__(self):
        row = lax.axis_index("rows")
        self.col = lax.axis_index("cols")
        self.core = lax.rem(row, 2)
        self.chip_bit = lax.rem(row // 2, 2)
        self.col_bit = lax.rem(self.col, 2)
        self.near_inside = jnp.where(self.core == 0, row > 0, row < lax.axis_size("rows") - 1)
        self.mate_inside = jnp.where(self.core == 0, row < lax.axis_size("rows") - 2, row > 1)
        self.taps = [tap + self.core * (2 - 2 * tap) for tap in range(3)]

    def chosen(self, total, half):
        size = total // 4
        middle = size // 2

        def wanted(rows):
            swapped = jnp.where(rows < middle, rows + middle, rows - middle)
            return (2 * half + self.col_bit) * size + jnp.where(self.chip_bit == 0, rows, swapped)

        return one_hot((size, total), wanted)

    def beside(self, weights, tap):
        return jnp.concatenate([weights[self.taps[tap], b] for b in range(3)], axis=1)

    def stacked(self, weights, tap):
        return jnp.concatenate([weights[self.taps[tap], b] for b in range(3)], axis=0)


def side(total, width, sign):
    left = moved(total[:, :width], -sign)
    right = moved(total[:, 2 * width :], sign)
    return left + total[:, width : 2 * width] + right


def spread(values):
    return jnp.concatenate(
        [moved(values, 1).astype(BF), values.astype(BF), moved(values, -1).astype(BF)], axis=1
    )


def rows_kernel(attended, first_kernel, far_cot, cotangent, mate1_cot, term, bundle):
    term[...] = side(mm(attended[...], Place().beside(first_kernel, 0)), CONV, 1).astype(BF)
    for row, half in enumerate((far_cot, cotangent, mate1_cot)):
        bundle[row] = half[...]


def assemble_kernel(count, *refs):
    far, pair = refs[count:]
    for row, target in enumerate((far, pair.at[0], pair.at[1])):
        lay_out([piece.at[row] for piece in refs[:count]], target, slice(None))


def turn_kernel(first_kernel, second_kernel, first_t, second_t):
    place = Place()
    eye = identity(CONV)
    for a in range(3):
        first_t[a * CONV : (a + 1) * CONV, :] = mm_t(eye, place.stacked(first_kernel, a)).astype(BF)
        second_t[a] = mm_t(eye, place.stacked(second_kernel, a)).astype(BF)


def prepare_kernel(own, local, stats, soft, keys_t, queries_t, attended_t, features_t, values):
    place = Place()
    across = own.shape[0]
    keys = local[:, QK : 2 * QK]
    keys_t[...] = mm_t(identity(QK), keys).astype(BF)
    pick = jnp.concatenate([place.chosen(VAL, place.core), place.chosen(VAL, 1 - place.core)], axis=0)
    features_t[...] = mm_t(pick, local[:, PACKED:]).astype(BF)
    for head in range(HEADS):
        values[head * across : (head + 1) * across, :] = head_of(local[:, 2 * QK : PACKED], head, HEAD_VAL)

    def block(index):
        at = block_at(index)
        queries = local[at, :QK]
        queries_t[:, at] = mm_t(identity(QK), queries).astype(BF)
        attended_t[:, at] = mm_t(identity(VAL), own[at, :]).astype(BF)
        scores = mm_t(jnp.concatenate([head_of(keys, h, HEAD_QK) for h in range(HEADS)], axis=0), queries)
        for head in range(HEADS):
            rows = slice(head * across, (head + 1) * across)
            below = (scores[rows, :] - stats[head : head + 1, at]) * EXP2_SCALING
            soft[rows, at] = jnp.exp2(below - stats[HEADS + head : HEADS + head + 1, at]).astype(BF)

    for_blocks(across // BLOCK, block)


def masked(inside, row):
    return jnp.where(inside, row, jnp.zeros_like(row))


def conv_term(place, row, kernel, tap):
    return side(mm(row[...], place.beside(kernel, tap)), CONV, 1)


def back_term(row, second_t, tap):
    return side(mm(row[...], second_t[tap]), CONV, -1)


def cotangent_terms_kernel(far_cot, pair_cot, second_t, near_back, own_back, mate_back):
    place = Place()
    own = pair_cot[0]
    near_back[...] = back_term(far_cot, second_t, 2) + back_term(own, second_t, 0)
    own_back[...] = back_term(own, second_t, 1)
    mate1 = masked(place.mate_inside, pair_cot[1])
    mate_back[...] = back_term(own, second_t, 2) + back_term(mate1, second_t, 0)


def attended_terms_kernel(own, mate, first_kernel, near_pre, own_pre, mate_pre):
    place = Place()
    near_pre[...] = conv_term(place, own, first_kernel, 2)
    own_pre[...] = conv_term(place, own, first_kernel, 1) + conv_term(place, mate, first_kernel, 2)
    mate_pre[...] = conv_term(place, own, first_kernel, 0) + conv_term(place, mate, first_kernel, 1)


def store_middle(pre, back, out):
    sigma = 1.0 / (1.0 + jnp.exp(-pre))
    out[:, :CONV] = (pre * sigma).astype(BF)
    out[:, CONV:] = (back * (sigma * (1.0 + pre * (1.0 - sigma)))).astype(BF)


def near_terms_kernel(far_term, near_pre, near_terms):
    near_terms[...] = near_pre[...] + far_term[...].astype(F32)


def mate_middle_kernel(
    mate1, mate_cot, mate_pre, mate_back, own_back, first_kernel, second_t, mate_mid, own_terms
):
    place = Place()
    own_terms[...] = own_back[...] + back_term(mate_cot[0], second_t, 0)
    pre = mate_pre[...] + conv_term(place, masked(place.mate_inside, mate1[...]), first_kernel, 2)
    store_middle(pre, mate_back[...] + back_term(mate_cot[0], second_t, 1), mate_mid)


def conv_grads_kernel(near, own, mate, mate1, pair_cot, mate_cot, own_mid, mate_mid, keep, send):
    place = Place()
    slots = (masked(place.near_inside, near[...]), own[...], mate[...], masked(place.mate_inside, mate1[...]))
    cots = (
        masked(place.near_inside, mate_cot[1]),
        pair_cot[0],
        mate_cot[0],
        masked(place.mate_inside, pair_cot[1]),
    )
    mids = {1: own_mid, 2: mate_mid}

    def store(total, start, step, a):
        for b in range(3):
            at = pl.ds(pl.multiple_of(start + (place.taps[a] * 3 + b) * step, step), step)
            keep[at, :] = total[:step, b * CONV : (b + 1) * CONV]
            send[at, :] = total[step:, b * CONV : (b + 1) * CONV]

    pick = place.chosen(VAL, place.core)
    attended_t = [mm_t(pick, slot).astype(BF) for slot in slots]
    slope = {slot: spread(mid[:, CONV:].astype(F32)) for slot, mid in mids.items()}
    for a in range(3):
        total = sum(mm(attended_t[slot + a - 1], slope[slot]) for slot in mids).astype(BF)
        store(total, 0, VAL // PARTS, a)
    pick = place.chosen(CONV, place.core)
    hidden_t = {slot: mm_t(pick, mid[:, :CONV]).astype(BF) for slot, mid in mids.items()}
    cotangent = [spread(cot.astype(F32)) for cot in cots]
    for a in range(3):
        total = sum(mm(hidden_t[slot], cotangent[slot + 1 - a]) for slot in mids).astype(BF)
        store(total, FIRST_ROWS, CONV // PARTS, a)


def backward_kernel(
    near,
    mate_cot,
    mate_mid,
    near_pre,
    near_back,
    own_pre,
    own_back,
    values,
    soft,
    keys_t,
    queries_t,
    attended_t,
    features_t,
    first_kernel,
    first_t,
    second_t,
    near_mid,
    own_mid,
    grad_out,
    proj_own,
    proj_mate,
    upstream_ref,
    grad_t,
):
    place = Place()
    across = near.shape[0]
    near = masked(place.near_inside, near[...])
    mids = (near_mid, own_mid, mate_mid)
    pre = near_pre[...] + conv_term(place, near, first_kernel, 1)
    near_cot = masked(place.near_inside, mate_cot[1])
    back = near_back[...] + back_term(near_cot, second_t, 1)
    store_middle(masked(place.near_inside, pre), masked(place.near_inside, back), near_mid)
    pre = own_pre[...] + conv_term(place, near, first_kernel, 0)
    store_middle(pre, own_back[...] + back_term(near_cot, second_t, 2), own_mid)
    slopes_beside = jnp.concatenate([mids[2 - a][:, CONV:] for a in range(3)], axis=1)
    upstream_ref[...] = side(mm(slopes_beside, first_t[...]), VAL, -1).astype(BF)
    blocks = across // BLOCK
    if blocks > 1:
        grad_t[...] = jnp.zeros_like(grad_t)

    def add_rows(start, count, terms):
        if blocks > 1:
            grad_t[start : start + count, :] += terms
        else:
            grad_t[start : start + count, :] = terms

    def block(index):
        at = block_at(index)
        upstream = upstream_ref[at, :]
        upstream_t = mm_t(identity(VAL), upstream)
        products = upstream_t * attended_t[:, at].astype(F32)
        upstream_t = upstream_t.astype(BF)
        slopes = mm_t(values[...], upstream)
        for head in range(HEADS):
            rows = slice(head * across, (head + 1) * across)
            qk_rows = slice(head * HEAD_QK, (head + 1) * HEAD_QK)
            val_rows = slice(head * HEAD_VAL, (head + 1) * HEAD_VAL)
            weights = soft[rows, at]
            inner = jnp.sum(products[val_rows, :], axis=0, keepdims=True)
            dscore = (weights.astype(F32) * (slopes[rows, :] - inner)).astype(BF)
            grad_t[qk_rows, at] = SCALING * mm(keys_t[qk_rows, :], dscore)
            add_rows(QK + head * HEAD_QK, HEAD_QK, SCALING * mm_t(queries_t[qk_rows, at], dscore))
            add_rows(2 * QK + head * HEAD_VAL, HEAD_VAL, mm_t(upstream_t[val_rows, :], weights))

    for_blocks(blocks, block)

    grad = grad_t[...].astype(BF)
    grad_out[...] = grad
    step = VAL // PARTS
    total = mm_t(features_t[...], grad).astype(BF)
    for which, target in enumerate((proj_own, proj_mate)):
        for j in range(PACKED // CONV):
            for part in range(2):
                begin = (2 * which + part) * step
                target[part, j * step : (j + 1) * step, :] = total[begin : begin + step, j * CONV : (j + 1) * CONV]


def outputs_kernel(near_mid, own_mid, mate_mid, grad, projection, second_kernel, output_map, input_grad, rows):
    place = Place()
    part_width = output_map.shape[0]
    mids = (near_mid, own_mid, mate_mid)
    rows[...] = side(sum(mm(mids[a][:, :CONV], place.beside(second_kernel, a)) for a in range(3)), CONV, 1)
    output_map[...] = rows[pl.ds(pl.multiple_of(place.col * part_width, part_width), part_width), :].astype(BF)
    own_pixels = one_hot((part_width, rows.shape[0]), lambda pixels: pixels + place.col * part_width)
    input_grad[...] = mm_t(mm_t(own_pixels, grad[...]).astype(BF), projection[...]).astype(BF)


def unpack_kernel(factor, core_flip, *refs):
    pieces = refs[:4]
    outs = refs[-7:-4]
    blocks = refs[-4:-1]
    sem = refs[-1]
    projection_block, first_block, second_block = blocks
    row = lax.axis_index("rows")
    half = lax.rem(row + core_flip, 2)
    chip_bit = lax.rem(row // 2, 2)
    col_bit = lax.rem(lax.axis_index("cols"), 2)
    parts = [2 * lax.rem(col_bit + which // 2, 2) + lax.rem(chip_bit + which % 2, 2) for which in range(4)]
    copies = []

    def send(index, block, out):
        copies.append(pltpu.make_async_copy(block, out, sem.at[index]))
        copies[-1].start()

    def rows_of(which, step):
        return pl.ds(pl.multiple_of(parts[which] * step, step), step)

    def half_of(rows):
        return pl.ds(pl.multiple_of(half * rows, rows), rows)

    step = VAL // PARTS
    for a in range(3):
        for which, piece in enumerate(pieces):
            for b in range(3):
                begin = (3 * a + b) * step
                first_block[a, b, rows_of(which, step), :] = piece[begin : begin + step, :].astype(F32) * factor
        send(a, first_block.at[a], outs[1].at[a, :, half_of(VAL // 2), :])
    for which, piece in enumerate(pieces):
        for j in range(PACKED // CONV):
            begin = FIRST_ROWS + SECOND_ROWS + j * step
            projection_block[rows_of(which, step), j * CONV : (j + 1) * CONV] = (
                piece[begin : begin + step, :].astype(F32) * factor
            )
    send(3, projection_block, outs[0].at[half_of(VAL // 2), :])
    step = CONV // PARTS
    for which, piece in enumerate(pieces):
        for tap in range(9):
            begin = FIRST_ROWS + tap * step
            second_block[tap // 3, tap % 3, rows_of(which, step), :] = (
                piece[begin : begin + step, :].astype(F32) * factor
            )
    send(4, second_block, outs[2].at[:, :, half_of(CONV // 2), :])
    for copy in copies:
        copy.wait()


def unpack(factor, core_flip, pieces, into, **params):
    dims = ((2 * QK, PACKED), (3, 3, VAL, CONV), (3, 3, CONV, CONV))
    return pl.pallas_call(
        functools.partial(unpack_kernel, factor, core_flip),
        out_shape=tuple(shape(*size, dtype=F32) for size in dims),
        in_specs=[VMEM] * 4 + [HBM] * len(into),
        out_specs=[HBM] * 3,
        scratch_shapes=[pltpu.VMEM(size[:-2] + (size[-2] // 2, size[-1]), F32) for size in dims]
        + [pltpu.SemaphoreType.DMA((5,))],
        input_output_aliases={4 + i: i for i in range(len(into))},
        cost_estimate=pl.CostEstimate(flops=10**9, bytes_accessed=4 * 1024 * 1024, transcendentals=0),
        name="unpack_sums",
        **params,
    )(*pieces, *into)


def shape(*dims, dtype=BF):
    return jax.ShapeDtypeStruct(dims, dtype)


def granted(across):
    return dict(compiler_params=pltpu.CompilerParams(vmem_limit_bytes=across * 64 * 1024))


VMEM = pl.BlockSpec(memory_space=pltpu.VMEM)
HBM = pl.BlockSpec(memory_space=pltpu.HBM)


def body(features, projection, first_kernel, second_kernel, cotangent):
    height, part_width, channels = features.shape
    rows_size = lax.axis_size("rows")
    cols_size = lax.axis_size("cols")
    across = part_width * cols_size

    def rows_flip(values, bit):
        return lax.ppermute(values, "rows", [(i, i ^ bit) for i in range(rows_size)])

    def cols_flip(values):
        return lax.ppermute(values, "cols", [(i, i ^ 1) for i in range(cols_size)])

    def wide(values):
        return values.astype(F32)

    def added(one, two):
        return (one + two).astype(BF)

    def call(kernel, out_shape, operands, scratch=(), name=None, flops=10**9):
        return pl.pallas_call(
            kernel,
            out_shape=out_shape,
            in_specs=[VMEM] * len(operands),
            out_specs=[VMEM] * len(out_shape),
            scratch_shapes=scratch,
            cost_estimate=pl.CostEstimate(flops=flops, bytes_accessed=flops // 250, transcendentals=0),
            name=name,
            **granted(across),
        )(*operands)

    features, cotangent = (features[0], cotangent[0])
    last = rows_size - 1
    out = [(i, i + 2) for i in range(0, last - 1, 2)] + [(i, i - 2) for i in range(3, rows_size, 2)]
    out += [(last - 1, last), (1, 0)]
    back = [(j, i) for i, j in out]
    if cols_size == 2:
        swapped = cols_flip(features)
        out_cot = lax.ppermute(cotangent, "rows", out)
        back_cot = lax.ppermute(cotangent, "rows", back)
        projection, features = fetch((projection, features))
        features = (features, swapped)
    else:
        out_cot = lax.ppermute(cotangent, "rows", out)
        back_cot = lax.ppermute(cotangent, "rows", back)
        features = (lax.all_gather(features, "cols", axis=0, tiled=True),)
    own, local, stats = call(
        functools.partial(forward_kernel, len(features)),
        (shape(across, VAL), shape(across, PACKED + channels), shape(2 * HEADS, across, dtype=F32)),
        (*features, projection),
        (pltpu.VMEM((VAL, across), BF),),
        name="attention_forward",
    )
    term, bundle = call(
        rows_kernel,
        (shape(across, CONV), shape(3, part_width, CONV)),
        (own, first_kernel, out_cot, cotangent, back_cot),
        name="rows",
    )
    first_kernel, second_kernel = fetch((first_kernel, second_kernel), (stats,), 10**4)
    first_t, second_t = call(
        turn_kernel,
        (shape(3 * CONV, 3 * VAL), shape(3, CONV, 3 * CONV)),
        (first_kernel, second_kernel),
        name="turn",
        flops=10**6,
    )
    mate1 = lax.ppermute(own, "rows", back)
    if cols_size == 2:
        bundles = (bundle, cols_flip(bundle))
    else:
        bundles = (lax.all_gather(bundle, "cols", axis=1, tiled=True),)
    far = lax.ppermute(term, "rows", out)
    mate = rows_flip(own, 1)
    terms = (shape(across, CONV, dtype=F32),) * 3
    near_pre, own_pre, mate_pre = call(
        attended_terms_kernel, terms, (own, mate, first_kernel), name="attended_terms", flops=10**6
    )
    bundles, near_pre = lax.optimization_barrier((bundles, near_pre))
    far_cot, pair_cot = call(
        functools.partial(assemble_kernel, len(bundles)),
        (shape(across, CONV), shape(2, across, CONV)),
        bundles,
        name="assemble",
        flops=10**6,
    )
    mate_cot = rows_flip(pair_cot, 1)
    near = rows_flip(mate1, 1)
    soft, keys_t, queries_t, attended_t, features_t, values = call(
        prepare_kernel,
        (
            shape(HEADS * across, across),
            shape(QK, across),
            shape(QK, across),
            shape(VAL, across),
            shape(VAL // 2, across),
            shape(HEADS * across, VAL),
        ),
        (own, local, stats),
        name="prepare",
        flops=10**6,
    )
    near_back, own_back, mate_back = call(
        cotangent_terms_kernel, terms, (far_cot, pair_cot, second_t), name="cotangent_terms", flops=10**6
    )
    (near_pre,) = call(near_terms_kernel, terms[:1], (far, near_pre), name="near_terms", flops=4 * 10**9)
    mate_mid, own_back = call(
        mate_middle_kernel,
        (shape(across, 2 * CONV), terms[0]),
        (mate1, mate_cot, mate_pre, mate_back, own_back, first_kernel, second_t),
        name="mate_middle",
    )
    near_mid, own_mid, grad, proj_own, proj_mate = call(
        backward_kernel,
        (
            shape(across, 2 * CONV),
            shape(across, 2 * CONV),
            shape(PACKED, across),
            shape(2, PROJ_ROWS, CONV),
            shape(2, PROJ_ROWS, CONV),
        ),
        (
            near,
            mate_cot,
            mate_mid,
            near_pre,
            near_back,
            own_pre,
            own_back,
            values,
            soft,
            keys_t,
            queries_t,
            attended_t,
            features_t,
            first_kernel,
            first_t,
            second_t,
        ),
        (pltpu.VMEM((across, VAL), BF), pltpu.VMEM((PACKED, across), F32)),
        name="block_backward",
    )
    keep, send = call(
        conv_grads_kernel,
        (shape(FIRST_ROWS + SECOND_ROWS, CONV),) * 2,
        (near, own, mate, mate1, pair_cot, mate_cot, own_mid, mate_mid),
        name="conv_grads",
    )
    output_map, input_grad = call(
        outputs_kernel,
        (shape(part_width, CONV), shape(part_width, channels)),
        (near_mid, own_mid, mate_mid, grad, projection, second_kernel),
        (pltpu.VMEM((across, CONV), F32),),
        name="outputs",
    )
    proj_sum = added(wide(proj_own), wide(rows_flip(proj_mate, 1)))
    sent = jnp.concatenate([send, proj_sum[1]], axis=0)
    kept = jnp.concatenate([keep, proj_sum[0]], axis=0)
    if rows_size > 4:
        total = added(wide(kept) + wide(rows_flip(kept, 4)), wide(rows_flip(sent, 2)) + wide(rows_flip(sent, 6)))
    else:
        total = added(wide(kept), wide(rows_flip(sent, 2)))
    bit = 8
    while bit < rows_size:
        total = added(wide(total), wide(rows_flip(total, bit)))
        bit *= 2
    total, output_map, input_grad = lax.optimization_barrier((total, output_map, input_grad))
    chip = rows_flip(total, 2)
    side = cols_flip(total)
    corner = lax.ppermute(
        total,
        ("rows", "cols"),
        [(i * cols_size + j, (i ^ 2) * cols_size + (j ^ 1)) for i in range(rows_size) for j in range(cols_size)],
    )
    four = (total, chip, side, corner)
    factor = 1.0 / math.sqrt(height * across * rows_size)
    halves = unpack(factor, 0, four, (), **granted(across))
    projection_grad, first_grad, second_grad = unpack(
        factor, 1, [rows_flip(piece, 1) for piece in four], halves, **granted(across)
    )
    return (output_map[None], input_grad[None], projection_grad, first_grad, second_grad)


def solution(mesh):
    placed = (P("rows", "cols", None), P(), P(), P(), P("rows", "cols", None))
    return jax.shard_map(
        body,
        mesh=mesh,
        in_specs=placed,
        out_specs=(P("rows", "cols", None), P("rows", "cols", None), P(), P(), P()),
        check_vma=False,
    )
```

```python
import functools
import math

import jax
import jax.numpy as jnp
from jax import lax
from jax.experimental import pallas as pl
from jax.experimental.pallas import tpu as pltpu
from jax.sharding import PartitionSpec as P

QK = 128
VAL = 256
HEADS = 8
CONV = 128
HEAD_QK = QK // HEADS
HEAD_VAL = VAL // HEADS
PACKED = 2 * QK + VAL
BLOCK = 256
BF = jnp.bfloat16
F32 = jnp.float32
SCALING = HEAD_QK ** (-0.5)
EXP2_SCALING = SCALING * math.log2(math.e)

PARTS = 8
FIRST_ROWS = 9 * VAL // PARTS
SECOND_ROWS = 9 * CONV // PARTS
CONV_ROWS = FIRST_ROWS + SECOND_ROWS
PROJ_ROWS = PACKED // CONV * (VAL // PARTS)


def mm(a, b):
    return lax.dot_general(a, b, (((1,), (0,)), ((), ())), preferred_element_type=F32)


def mm_t(a, b):
    return lax.dot_general(a, b, (((1,), (1,)), ((), ())), preferred_element_type=F32)


def one_hot(shape, wanted):
    rows = lax.broadcasted_iota(jnp.int32, shape, 0)
    columns = lax.broadcasted_iota(jnp.int32, shape, 1)
    return jnp.where(columns == wanted(rows), 1.0, 0.0).astype(BF)


def identity(size):
    return one_hot((size, size), lambda rows: rows)


def head_of(values, head, width):
    lanes = lax.broadcasted_iota(jnp.int32, values.shape, 1)
    return jnp.where(lanes // width == head, values, jnp.zeros_like(values))


def moved(values, step):
    count = values.shape[0]
    turned = pltpu.roll(values, (-step) % count, 0)
    at = lax.broadcasted_iota(jnp.int32, values.shape, 0)
    return jnp.where(at == (count - 1 if step > 0 else 0), 0.0, turned)


def for_blocks(count, run):
    if count == 1:
        run(0)
    else:
        lax.fori_loop(0, count, lambda i, carry: (run(i), carry)[1], 0)


def block_at(index):
    return pl.ds(index if isinstance(index, int) else pl.multiple_of(index * BLOCK, BLOCK), BLOCK)


def fetch_kernel(count, *refs):
    targets = refs[-1 - count : -1]
    copies = [pltpu.make_async_copy(refs[i], targets[i], refs[-1].at[i]) for i in range(count)]
    for copy in copies:
        copy.start()
    for copy in copies:
        copy.wait()


def fetch(arrays, after=(), nbytes=4 * 1024 * 1024):
    return pl.pallas_call(
        functools.partial(fetch_kernel, len(arrays)),
        out_shape=tuple(shape(*array.shape) for array in arrays),
        in_specs=[HBM] * (len(arrays) + len(after)),
        out_specs=[VMEM] * len(arrays),
        scratch_shapes=[pltpu.SemaphoreType.DMA((len(arrays),))],
        cost_estimate=pl.CostEstimate(flops=0, bytes_accessed=nbytes, transcendentals=0),
        name="fetch",
        **granted(32),
    )(*arrays, *after)


def lay_out(pieces, target, lanes):
    for which, piece in enumerate(pieces):
        width = piece.shape[0]
        if len(pieces) == 1:
            at = slice(None)
        else:
            place = lax.rem(lax.axis_index("cols") + which, 2)
            at = pl.ds(pl.multiple_of(place * width, width), width)
        target[at, lanes] = piece[...]


def forward_kernel(count, *refs):
    projection, attended, local, stats, values_t = refs[count:]
    across = attended.shape[0]
    lay_out(refs[:count], local, slice(PACKED, None))
    packed = mm(local[:, PACKED:], projection[...]).astype(BF)
    local[:, :PACKED] = packed
    keys = packed[:, QK : 2 * QK]
    values_t[...] = mm_t(identity(VAL), packed[:, 2 * QK :]).astype(BF)

    def block(index):
        at = block_at(index)
        queries = local[at, :QK]
        rows = []
        all_scores = mm_t(jnp.concatenate([head_of(keys, h, HEAD_QK) for h in range(HEADS)], axis=0), queries)
        for head in range(HEADS):
            scores = all_scores[head * across : (head + 1) * across, :]
            maxima = jnp.max(scores, axis=0, keepdims=True)
            exponent = jnp.exp2((scores - maxima) * EXP2_SCALING)
            totals = jnp.sum(exponent, axis=0, keepdims=True)
            weighted = mm(values_t[head * HEAD_VAL : (head + 1) * HEAD_VAL, :], exponent.astype(BF))
            rows.append((weighted * (1.0 / totals)).astype(BF))
            stats[head : head + 1, at] = maxima
            stats[HEADS + head : HEADS + head + 1, at] = jnp.log2(totals)
        attended[at, :] = mm_t(identity(BLOCK), jnp.concatenate(rows, axis=0)).astype(BF)

    for_blocks(across // BLOCK, block)


class Place:
    def __init__(self):
        row = lax.axis_index("rows")
        self.col = lax.axis_index("cols")
        self.core = lax.rem(row, 2)
        self.chip_bit = lax.rem(row // 2, 2)
        self.col_bit = lax.rem(self.col, 2)
        self.near_inside = jnp.where(self.core == 0, row > 0, row < lax.axis_size("rows") - 1)
        self.mate_inside = jnp.where(self.core == 0, row < lax.axis_size("rows") - 2, row > 1)
        self.taps = [tap + self.core * (2 - 2 * tap) for tap in range(3)]

    def chosen(self, total, half):
        size = total // 4
        middle = size // 2

        def wanted(rows):
            swapped = jnp.where(rows < middle, rows + middle, rows - middle)
            return (2 * half + self.col_bit) * size + jnp.where(self.chip_bit == 0, rows, swapped)

        return one_hot((size, total), wanted)

    def beside(self, weights, tap):
        return jnp.concatenate([weights[self.taps[tap], b] for b in range(3)], axis=1)

    def stacked(self, weights, tap):
        return jnp.concatenate([weights[self.taps[tap], b] for b in range(3)], axis=0)


def side(total, width, sign):
    left = moved(total[:, :width], -sign)
    right = moved(total[:, 2 * width :], sign)
    return left + total[:, width : 2 * width] + right


def spread(values):
    return jnp.concatenate(
        [moved(values, 1).astype(BF), values.astype(BF), moved(values, -1).astype(BF)], axis=1
    )


def rows_kernel(attended, first_kernel, far_cot, cotangent, mate1_cot, term, bundle):
    term[...] = side(mm(attended[...], Place().beside(first_kernel, 0)), CONV, 1).astype(BF)
    for row, half in enumerate((far_cot, cotangent, mate1_cot)):
        bundle[row] = half[...]


def assemble_kernel(count, *refs):
    far, pair = refs[count:]
    for row, target in enumerate((far, pair.at[0], pair.at[1])):
        lay_out([piece.at[row] for piece in refs[:count]], target, slice(None))


def turn_kernel(first_kernel, second_kernel, first_t, second_t):
    place = Place()
    eye = identity(CONV)
    for a in range(3):
        first_t[a * CONV : (a + 1) * CONV, :] = mm_t(eye, place.stacked(first_kernel, a)).astype(BF)
        second_t[a] = mm_t(eye, place.stacked(second_kernel, a)).astype(BF)


def prepare_kernel(own, local, stats, soft, keys_t, queries_t, attended_t, features_t, values):
    place = Place()
    across = own.shape[0]
    keys = local[:, QK : 2 * QK]
    keys_t[...] = mm_t(identity(QK), keys).astype(BF)
    pick = jnp.concatenate([place.chosen(VAL, place.core), place.chosen(VAL, 1 - place.core)], axis=0)
    features_t[...] = mm_t(pick, local[:, PACKED:]).astype(BF)
    for head in range(HEADS):
        values[head * across : (head + 1) * across, :] = head_of(local[:, 2 * QK : PACKED], head, HEAD_VAL)

    def block(index):
        at = block_at(index)
        queries = local[at, :QK]
        queries_t[:, at] = mm_t(identity(QK), queries).astype(BF)
        attended_t[:, at] = mm_t(identity(VAL), own[at, :]).astype(BF)
        scores = mm_t(jnp.concatenate([head_of(keys, h, HEAD_QK) for h in range(HEADS)], axis=0), queries)
        for head in range(HEADS):
            rows = slice(head * across, (head + 1) * across)
            below = (scores[rows, :] - stats[head : head + 1, at]) * EXP2_SCALING
            soft[rows, at] = jnp.exp2(below - stats[HEADS + head : HEADS + head + 1, at]).astype(BF)

    for_blocks(across // BLOCK, block)


def masked(inside, row):
    return jnp.where(inside, row, jnp.zeros_like(row))


def conv_term(place, row, kernel, tap):
    return side(mm(row[...], place.beside(kernel, tap)), CONV, 1)


def back_term(row, second_t, tap):
    return side(mm(row[...], second_t[tap]), CONV, -1)


def cotangent_terms_kernel(far_cot, pair_cot, second_t, near_back, own_back, mate_back):
    place = Place()
    own = pair_cot[0]
    near_back[...] = back_term(far_cot, second_t, 2) + back_term(own, second_t, 0)
    own_back[...] = back_term(own, second_t, 1)
    mate1 = masked(place.mate_inside, pair_cot[1])
    mate_back[...] = back_term(own, second_t, 2) + back_term(mate1, second_t, 0)


def attended_terms_kernel(own, mate, first_kernel, near_pre, own_pre, mate_pre):
    place = Place()
    near_pre[...] = conv_term(place, own, first_kernel, 2)
    own_pre[...] = conv_term(place, own, first_kernel, 1) + conv_term(place, mate, first_kernel, 2)
    mate_pre[...] = conv_term(place, own, first_kernel, 0) + conv_term(place, mate, first_kernel, 1)


def store_middle(pre, back, out):
    sigma = 1.0 / (1.0 + jnp.exp(-pre))
    out[:, :CONV] = (pre * sigma).astype(BF)
    out[:, CONV:] = (back * (sigma * (1.0 + pre * (1.0 - sigma)))).astype(BF)


def near_terms_kernel(far_term, near_pre, near_terms):
    near_terms[...] = near_pre[...] + far_term[...].astype(F32)


def mate_middle_kernel(
    mate1, mate_cot, mate_pre, mate_back, own_back, first_kernel, second_t, mate_mid, own_terms
):
    place = Place()
    own_terms[...] = own_back[...] + back_term(mate_cot[0], second_t, 0)
    pre = mate_pre[...] + conv_term(place, masked(place.mate_inside, mate1[...]), first_kernel, 2)
    store_middle(pre, mate_back[...] + back_term(mate_cot[0], second_t, 1), mate_mid)


def conv_grads_kernel(near, own, mate, mate1, pair_cot, mate_cot, own_mid, mate_mid, keep, send):
    place = Place()
    slots = (masked(place.near_inside, near[...]), own[...], mate[...], masked(place.mate_inside, mate1[...]))
    cots = (
        masked(place.near_inside, mate_cot[1]),
        pair_cot[0],
        mate_cot[0],
        masked(place.mate_inside, pair_cot[1]),
    )
    mids = {1: own_mid, 2: mate_mid}

    def store(total, start, step, a):
        for b in range(3):
            at = pl.ds(pl.multiple_of(start + (place.taps[a] * 3 + b) * step, step), step)
            keep[at, :] = total[:step, b * CONV : (b + 1) * CONV]
            send[at, :] = total[step:, b * CONV : (b + 1) * CONV]

    pick = place.chosen(VAL, place.core)
    attended_t = [mm_t(pick, slot).astype(BF) for slot in slots]
    slope = {slot: spread(mid[:, CONV:].astype(F32)) for slot, mid in mids.items()}
    for a in range(3):
        total = sum(mm(attended_t[slot + a - 1], slope[slot]) for slot in mids).astype(BF)
        store(total, 0, VAL // PARTS, a)
    pick = place.chosen(CONV, place.core)
    hidden_t = {slot: mm_t(pick, mid[:, :CONV]).astype(BF) for slot, mid in mids.items()}
    cotangent = [spread(cot.astype(F32)) for cot in cots]
    for a in range(3):
        total = sum(mm(hidden_t[slot], cotangent[slot + 1 - a]) for slot in mids).astype(BF)
        store(total, FIRST_ROWS, CONV // PARTS, a)


def backward_kernel(
    near,
    mate_cot,
    mate_mid,
    near_pre,
    near_back,
    own_pre,
    own_back,
    values,
    soft,
    keys_t,
    queries_t,
    attended_t,
    features_t,
    first_kernel,
    first_t,
    second_t,
    near_mid,
    own_mid,
    grad_out,
    proj_own,
    proj_mate,
    upstream_ref,
    grad_t,
):
    place = Place()
    across = near.shape[0]
    near = masked(place.near_inside, near[...])
    mids = (near_mid, own_mid, mate_mid)
    pre = near_pre[...] + conv_term(place, near, first_kernel, 1)
    near_cot = masked(place.near_inside, mate_cot[1])
    back = near_back[...] + back_term(near_cot, second_t, 1)
    store_middle(masked(place.near_inside, pre), masked(place.near_inside, back), near_mid)
    pre = own_pre[...] + conv_term(place, near, first_kernel, 0)
    store_middle(pre, own_back[...] + back_term(near_cot, second_t, 2), own_mid)
    slopes_beside = jnp.concatenate([mids[2 - a][:, CONV:] for a in range(3)], axis=1)
    upstream_ref[...] = side(mm(slopes_beside, first_t[...]), VAL, -1).astype(BF)
    blocks = across // BLOCK
    if blocks > 1:
        grad_t[...] = jnp.zeros_like(grad_t)

    def add_rows(start, count, terms):
        if blocks > 1:
            grad_t[start : start + count, :] += terms
        else:
            grad_t[start : start + count, :] = terms

    def block(index):
        at = block_at(index)
        upstream = upstream_ref[at, :]
        upstream_t = mm_t(identity(VAL), upstream)
        products = upstream_t * attended_t[:, at].astype(F32)
        upstream_t = upstream_t.astype(BF)
        slopes = mm_t(values[...], upstream)
        for head in range(HEADS):
            rows = slice(head * across, (head + 1) * across)
            qk_rows = slice(head * HEAD_QK, (head + 1) * HEAD_QK)
            val_rows = slice(head * HEAD_VAL, (head + 1) * HEAD_VAL)
            weights = soft[rows, at]
            inner = jnp.sum(products[val_rows, :], axis=0, keepdims=True)
            dscore = (weights.astype(F32) * (slopes[rows, :] - inner)).astype(BF)
            grad_t[qk_rows, at] = SCALING * mm(keys_t[qk_rows, :], dscore)
            add_rows(QK + head * HEAD_QK, HEAD_QK, SCALING * mm_t(queries_t[qk_rows, at], dscore))
            add_rows(2 * QK + head * HEAD_VAL, HEAD_VAL, mm_t(upstream_t[val_rows, :], weights))

    for_blocks(blocks, block)

    grad = grad_t[...].astype(BF)
    grad_out[...] = grad
    step = VAL // PARTS
    total = mm_t(features_t[...], grad).astype(BF)
    for which, target in enumerate((proj_own, proj_mate)):
        for j in range(PACKED // CONV):
            for part in range(2):
                begin = (2 * which + part) * step
                target[part, j * step : (j + 1) * step, :] = total[begin : begin + step, j * CONV : (j + 1) * CONV]


def outputs_kernel(near_mid, own_mid, mate_mid, grad, projection, second_kernel, output_map, input_grad, rows):
    place = Place()
    part_width = output_map.shape[0]
    mids = (near_mid, own_mid, mate_mid)
    rows[...] = side(sum(mm(mids[a][:, :CONV], place.beside(second_kernel, a)) for a in range(3)), CONV, 1)
    output_map[...] = rows[pl.ds(pl.multiple_of(place.col * part_width, part_width), part_width), :].astype(BF)
    own_pixels = one_hot((part_width, rows.shape[0]), lambda pixels: pixels + place.col * part_width)
    input_grad[...] = mm_t(mm_t(own_pixels, grad[...]).astype(BF), projection[...]).astype(BF)


def unpack_kernel(factor, core_flip, *refs):
    pieces = refs[:4]
    outs = refs[-7:-4]
    blocks = refs[-4:-1]
    sem = refs[-1]
    projection_block, first_block, second_block = blocks
    row = lax.axis_index("rows")
    half = lax.rem(row + core_flip, 2)
    chip_bit = lax.rem(row // 2, 2)
    col_bit = lax.rem(lax.axis_index("cols"), 2)
    parts = [2 * lax.rem(col_bit + which // 2, 2) + lax.rem(chip_bit + which % 2, 2) for which in range(4)]
    copies = []

    def send(index, block, out):
        copies.append(pltpu.make_async_copy(block, out, sem.at[index]))
        copies[-1].start()

    def rows_of(which, step):
        return pl.ds(pl.multiple_of(parts[which] * step, step), step)

    def half_of(rows):
        return pl.ds(pl.multiple_of(half * rows, rows), rows)

    step = VAL // PARTS
    for a in range(3):
        for which, piece in enumerate(pieces):
            for b in range(3):
                begin = (3 * a + b) * step
                first_block[a, b, rows_of(which, step), :] = piece[begin : begin + step, :].astype(F32) * factor
        send(a, first_block.at[a], outs[1].at[a, :, half_of(VAL // 2), :])
    for which, piece in enumerate(pieces):
        for j in range(PACKED // CONV):
            begin = FIRST_ROWS + SECOND_ROWS + j * step
            projection_block[rows_of(which, step), j * CONV : (j + 1) * CONV] = (
                piece[begin : begin + step, :].astype(F32) * factor
            )
    send(3, projection_block, outs[0].at[half_of(VAL // 2), :])
    step = CONV // PARTS
    for which, piece in enumerate(pieces):
        for tap in range(9):
            begin = FIRST_ROWS + tap * step
            second_block[tap // 3, tap % 3, rows_of(which, step), :] = (
                piece[begin : begin + step, :].astype(F32) * factor
            )
    send(4, second_block, outs[2].at[:, :, half_of(CONV // 2), :])
    for copy in copies:
        copy.wait()


def unpack(factor, core_flip, pieces, into, **params):
    dims = ((2 * QK, PACKED), (3, 3, VAL, CONV), (3, 3, CONV, CONV))
    return pl.pallas_call(
        functools.partial(unpack_kernel, factor, core_flip),
        out_shape=tuple(shape(*size, dtype=F32) for size in dims),
        in_specs=[VMEM] * 4 + [HBM] * len(into),
        out_specs=[HBM] * 3,
        scratch_shapes=[pltpu.VMEM(size[:-2] + (size[-2] // 2, size[-1]), F32) for size in dims]
        + [pltpu.SemaphoreType.DMA((5,))],
        input_output_aliases={4 + i: i for i in range(len(into))},
        cost_estimate=pl.CostEstimate(flops=10**9, bytes_accessed=4 * 1024 * 1024, transcendentals=0),
        name="unpack_sums",
        **params,
    )(*pieces, *into)


def shape(*dims, dtype=BF):
    return jax.ShapeDtypeStruct(dims, dtype)


def granted(across):
    return dict(compiler_params=pltpu.CompilerParams(vmem_limit_bytes=across * 64 * 1024))


VMEM = pl.BlockSpec(memory_space=pltpu.VMEM)
HBM = pl.BlockSpec(memory_space=pltpu.HBM)


def body(features, projection, first_kernel, second_kernel, cotangent):
    height, part_width, channels = features.shape
    rows_size = lax.axis_size("rows")
    cols_size = lax.axis_size("cols")
    across = part_width * cols_size

    def rows_flip(values, bit):
        return lax.ppermute(values, "rows", [(i, i ^ bit) for i in range(rows_size)])

    def cols_flip(values):
        return lax.ppermute(values, "cols", [(i, i ^ 1) for i in range(cols_size)])

    def wide(values):
        return values.astype(F32)

    def added(one, two):
        return (one + two).astype(BF)

    def call(kernel, out_shape, operands, scratch=(), name=None, flops=10**9):
        return pl.pallas_call(
            kernel,
            out_shape=out_shape,
            in_specs=[VMEM] * len(operands),
            out_specs=[VMEM] * len(out_shape),
            scratch_shapes=scratch,
            cost_estimate=pl.CostEstimate(flops=flops, bytes_accessed=flops // 250, transcendentals=0),
            name=name,
            **granted(across),
        )(*operands)

    features, cotangent = (features[0], cotangent[0])
    last = rows_size - 1
    out = [(i, i + 2) for i in range(0, last - 1, 2)] + [(i, i - 2) for i in range(3, rows_size, 2)]
    out += [(last - 1, last), (1, 0)]
    back = [(j, i) for i, j in out]
    if cols_size == 2:
        swapped = cols_flip(features)
        out_cot = lax.ppermute(cotangent, "rows", out)
        back_cot = lax.ppermute(cotangent, "rows", back)
        (projection,) = fetch((projection,))
        features = (features, swapped)
    else:
        out_cot = lax.ppermute(cotangent, "rows", out)
        back_cot = lax.ppermute(cotangent, "rows", back)
        features = (lax.all_gather(features, "cols", axis=0, tiled=True),)
    own, local, stats = call(
        functools.partial(forward_kernel, len(features)),
        (shape(across, VAL), shape(across, PACKED + channels), shape(2 * HEADS, across, dtype=F32)),
        (*features, projection),
        (pltpu.VMEM((VAL, across), BF),),
        name="attention_forward",
    )
    term, bundle = call(
        rows_kernel,
        (shape(across, CONV), shape(3, part_width, CONV)),
        (own, first_kernel, out_cot, cotangent, back_cot),
        name="rows",
    )
    first_kernel, second_kernel = fetch((first_kernel, second_kernel), (stats,), 10**4)
    first_t, second_t = call(
        turn_kernel,
        (shape(3 * CONV, 3 * VAL), shape(3, CONV, 3 * CONV)),
        (first_kernel, second_kernel),
        name="turn",
        flops=10**6,
    )
    mate1 = lax.ppermute(own, "rows", back)
    if cols_size == 2:
        bundles = (bundle, cols_flip(bundle))
    else:
        bundles = (lax.all_gather(bundle, "cols", axis=1, tiled=True),)
    far = lax.ppermute(term, "rows", out)
    mate = rows_flip(own, 1)
    terms = (shape(across, CONV, dtype=F32),) * 3
    near_pre, own_pre, mate_pre = call(
        attended_terms_kernel, terms, (own, mate, first_kernel), name="attended_terms", flops=10**6
    )
    bundles, near_pre = lax.optimization_barrier((bundles, near_pre))
    far_cot, pair_cot = call(
        functools.partial(assemble_kernel, len(bundles)),
        (shape(across, CONV), shape(2, across, CONV)),
        bundles,
        name="assemble",
        flops=10**6,
    )
    mate_cot = rows_flip(pair_cot, 1)
    near = rows_flip(mate1, 1)
    soft, keys_t, queries_t, attended_t, features_t, values = call(
        prepare_kernel,
        (
            shape(HEADS * across, across),
            shape(QK, across),
            shape(QK, across),
            shape(VAL, across),
            shape(VAL // 2, across),
            shape(HEADS * across, VAL),
        ),
        (own, local, stats),
        name="prepare",
        flops=10**6,
    )
    near_back, own_back, mate_back = call(
        cotangent_terms_kernel, terms, (far_cot, pair_cot, second_t), name="cotangent_terms", flops=10**6
    )
    (near_pre,) = call(near_terms_kernel, terms[:1], (far, near_pre), name="near_terms", flops=4 * 10**9)
    mate_mid, own_back = call(
        mate_middle_kernel,
        (shape(across, 2 * CONV), terms[0]),
        (mate1, mate_cot, mate_pre, mate_back, own_back, first_kernel, second_t),
        name="mate_middle",
    )
    near_mid, own_mid, grad, proj_own, proj_mate = call(
        backward_kernel,
        (
            shape(across, 2 * CONV),
            shape(across, 2 * CONV),
            shape(PACKED, across),
            shape(2, PROJ_ROWS, CONV),
            shape(2, PROJ_ROWS, CONV),
        ),
        (
            near,
            mate_cot,
            mate_mid,
            near_pre,
            near_back,
            own_pre,
            own_back,
            values,
            soft,
            keys_t,
            queries_t,
            attended_t,
            features_t,
            first_kernel,
            first_t,
            second_t,
        ),
        (pltpu.VMEM((across, VAL), BF), pltpu.VMEM((PACKED, across), F32)),
        name="block_backward",
    )
    keep, send = call(
        conv_grads_kernel,
        (shape(FIRST_ROWS + SECOND_ROWS, CONV),) * 2,
        (near, own, mate, mate1, pair_cot, mate_cot, own_mid, mate_mid),
        name="conv_grads",
    )
    output_map, input_grad = call(
        outputs_kernel,
        (shape(part_width, CONV), shape(part_width, channels)),
        (near_mid, own_mid, mate_mid, grad, projection, second_kernel),
        (pltpu.VMEM((across, CONV), F32),),
        name="outputs",
    )
    proj_sum = added(wide(proj_own), wide(rows_flip(proj_mate, 1)))
    sent = jnp.concatenate([send, proj_sum[1]], axis=0)
    kept = jnp.concatenate([keep, proj_sum[0]], axis=0)
    if rows_size > 4:
        total = added(wide(kept) + wide(rows_flip(kept, 4)), wide(rows_flip(sent, 2)) + wide(rows_flip(sent, 6)))
    else:
        total = added(wide(kept), wide(rows_flip(sent, 2)))
    bit = 8
    while bit < rows_size:
        total = added(wide(total), wide(rows_flip(total, bit)))
        bit *= 2
    total, output_map, input_grad = lax.optimization_barrier((total, output_map, input_grad))
    chip = rows_flip(total, 2)
    side = cols_flip(total)
    corner = lax.ppermute(
        total,
        ("rows", "cols"),
        [(i * cols_size + j, (i ^ 2) * cols_size + (j ^ 1)) for i in range(rows_size) for j in range(cols_size)],
    )
    four = (total, chip, side, corner)
    factor = 1.0 / math.sqrt(height * across * rows_size)
    halves = unpack(factor, 0, four, (), **granted(across))
    projection_grad, first_grad, second_grad = unpack(
        factor, 1, [rows_flip(piece, 1) for piece in four], halves, **granted(across)
    )
    return (output_map[None], input_grad[None], projection_grad, first_grad, second_grad)


def solution(mesh):
    placed = (P("rows", "cols", None), P(), P(), P(), P("rows", "cols", None))
    return jax.shard_map(
        body,
        mesh=mesh,
        in_specs=placed,
        out_specs=(P("rows", "cols", None), P("rows", "cols", None), P(), P(), P()),
        check_vma=False,
    )
```

```python
import functools
import math

import jax
import jax.numpy as jnp
from jax import lax
from jax.experimental import pallas as pl
from jax.experimental.pallas import tpu as pltpu
from jax.sharding import PartitionSpec as P

QK = 128
VAL = 256
HEADS = 8
CONV = 128
HEAD_QK = QK // HEADS
HEAD_VAL = VAL // HEADS
PACKED = 2 * QK + VAL
BLOCK = 256
BF = jnp.bfloat16
F32 = jnp.float32
SCALING = HEAD_QK ** (-0.5)
EXP2_SCALING = SCALING * math.log2(math.e)

PARTS = 8
FIRST_ROWS = 9 * VAL // PARTS
SECOND_ROWS = 9 * CONV // PARTS
CONV_ROWS = FIRST_ROWS + SECOND_ROWS
PROJ_ROWS = PACKED // CONV * (VAL // PARTS)


def mm(a, b):
    return lax.dot_general(a, b, (((1,), (0,)), ((), ())), preferred_element_type=F32)


def mm_t(a, b):
    return lax.dot_general(a, b, (((1,), (1,)), ((), ())), preferred_element_type=F32)


def one_hot(shape, wanted):
    rows = lax.broadcasted_iota(jnp.int32, shape, 0)
    columns = lax.broadcasted_iota(jnp.int32, shape, 1)
    return jnp.where(columns == wanted(rows), 1.0, 0.0).astype(BF)


def identity(size):
    return one_hot((size, size), lambda rows: rows)


def head_of(values, head, width):
    lanes = lax.broadcasted_iota(jnp.int32, values.shape, 1)
    return jnp.where(lanes // width == head, values, jnp.zeros_like(values))


def moved(values, step):
    count = values.shape[0]
    turned = pltpu.roll(values, (-step) % count, 0)
    at = lax.broadcasted_iota(jnp.int32, values.shape, 0)
    return jnp.where(at == (count - 1 if step > 0 else 0), 0.0, turned)


def for_blocks(count, run):
    if count == 1:
        run(0)
    else:
        lax.fori_loop(0, count, lambda i, carry: (run(i), carry)[1], 0)


def block_at(index):
    return pl.ds(index if isinstance(index, int) else pl.multiple_of(index * BLOCK, BLOCK), BLOCK)


def fetch_kernel(count, *refs):
    targets = refs[-1 - count : -1]
    copies = [pltpu.make_async_copy(refs[i], targets[i], refs[-1].at[i]) for i in range(count)]
    for copy in copies:
        copy.start()
    for copy in copies:
        copy.wait()


def fetch(arrays, after=(), nbytes=4 * 1024 * 1024):
    return pl.pallas_call(
        functools.partial(fetch_kernel, len(arrays)),
        out_shape=tuple(shape(*array.shape) for array in arrays),
        in_specs=[HBM] * (len(arrays) + len(after)),
        out_specs=[VMEM] * len(arrays),
        scratch_shapes=[pltpu.SemaphoreType.DMA((len(arrays),))],
        cost_estimate=pl.CostEstimate(flops=0, bytes_accessed=nbytes, transcendentals=0),
        name="fetch",
        **granted(32),
    )(*arrays, *after)


def lay_out(pieces, target, lanes):
    for which, piece in enumerate(pieces):
        width = piece.shape[0]
        if len(pieces) == 1:
            at = slice(None)
        else:
            place = lax.rem(lax.axis_index("cols") + which, 2)
            at = pl.ds(pl.multiple_of(place * width, width), width)
        target[at, lanes] = piece[...]


def forward_kernel(count, *refs):
    projection, attended, local, stats, values_t = refs[count:]
    across = attended.shape[0]
    lay_out(refs[:count], local, slice(PACKED, None))
    packed = mm(local[:, PACKED:], projection[...]).astype(BF)
    local[:, :PACKED] = packed
    keys = packed[:, QK : 2 * QK]
    values_t[...] = mm_t(identity(VAL), packed[:, 2 * QK :]).astype(BF)

    def block(index):
        at = block_at(index)
        queries = local[at, :QK]
        rows = []
        all_scores = mm_t(jnp.concatenate([head_of(keys, h, HEAD_QK) for h in range(HEADS)], axis=0), queries)
        for head in range(HEADS):
            scores = all_scores[head * across : (head + 1) * across, :]
            maxima = jnp.max(scores, axis=0, keepdims=True)
            exponent = jnp.exp2((scores - maxima) * EXP2_SCALING)
            totals = jnp.sum(exponent, axis=0, keepdims=True)
            weighted = mm(values_t[head * HEAD_VAL : (head + 1) * HEAD_VAL, :], exponent.astype(BF))
            rows.append((weighted * (1.0 / totals)).astype(BF))
            stats[head : head + 1, at] = maxima
            stats[HEADS + head : HEADS + head + 1, at] = jnp.log2(totals)
        attended[at, :] = mm_t(identity(BLOCK), jnp.concatenate(rows, axis=0)).astype(BF)

    for_blocks(across // BLOCK, block)


class Place:
    def __init__(self):
        row = lax.axis_index("rows")
        self.col = lax.axis_index("cols")
        self.core = lax.rem(row, 2)
        self.chip_bit = lax.rem(row // 2, 2)
        self.col_bit = lax.rem(self.col, 2)
        self.near_inside = jnp.where(self.core == 0, row > 0, row < lax.axis_size("rows") - 1)
        self.mate_inside = jnp.where(self.core == 0, row < lax.axis_size("rows") - 2, row > 1)
        self.taps = [tap + self.core * (2 - 2 * tap) for tap in range(3)]

    def chosen(self, total, half):
        size = total // 4
        middle = size // 2

        def wanted(rows):
            swapped = jnp.where(rows < middle, rows + middle, rows - middle)
            return (2 * half + self.col_bit) * size + jnp.where(self.chip_bit == 0, rows, swapped)

        return one_hot((size, total), wanted)

    def beside(self, weights, tap):
        return jnp.concatenate([weights[self.taps[tap], b] for b in range(3)], axis=1)

    def stacked(self, weights, tap):
        return jnp.concatenate([weights[self.taps[tap], b] for b in range(3)], axis=0)


def side(total, width, sign):
    left = moved(total[:, :width], -sign)
    right = moved(total[:, 2 * width :], sign)
    return left + total[:, width : 2 * width] + right


def spread(values):
    return jnp.concatenate(
        [moved(values, 1).astype(BF), values.astype(BF), moved(values, -1).astype(BF)], axis=1
    )


def rows_kernel(attended, first_kernel, far_cot, cotangent, mate1_cot, term, bundle):
    term[...] = side(mm(attended[...], Place().beside(first_kernel, 0)), CONV, 1).astype(BF)
    for row, half in enumerate((far_cot, cotangent, mate1_cot)):
        bundle[row] = half[...]


def assemble_kernel(count, *refs):
    far, pair = refs[count:]
    for row, target in enumerate((far, pair.at[0], pair.at[1])):
        lay_out([piece.at[row] for piece in refs[:count]], target, slice(None))


def turn_kernel(first_kernel, second_kernel, first_t, second_t):
    place = Place()
    eye = identity(CONV)
    for a in range(3):
        first_t[a * CONV : (a + 1) * CONV, :] = mm_t(eye, place.stacked(first_kernel, a)).astype(BF)
        second_t[a] = mm_t(eye, place.stacked(second_kernel, a)).astype(BF)


def prepare_kernel(own, local, stats, soft, keys_t, queries_t, attended_t, features_t, values):
    place = Place()
    across = own.shape[0]
    keys = local[:, QK : 2 * QK]
    keys_t[...] = mm_t(identity(QK), keys).astype(BF)
    pick = jnp.concatenate([place.chosen(VAL, place.core), place.chosen(VAL, 1 - place.core)], axis=0)
    features_t[...] = mm_t(pick, local[:, PACKED:]).astype(BF)
    for head in range(HEADS):
        values[head * across : (head + 1) * across, :] = head_of(local[:, 2 * QK : PACKED], head, HEAD_VAL)

    def block(index):
        at = block_at(index)
        queries = local[at, :QK]
        queries_t[:, at] = mm_t(identity(QK), queries).astype(BF)
        attended_t[:, at] = mm_t(identity(VAL), own[at, :]).astype(BF)
        scores = mm_t(jnp.concatenate([head_of(keys, h, HEAD_QK) for h in range(HEADS)], axis=0), queries)
        for head in range(HEADS):
            rows = slice(head * across, (head + 1) * across)
            below = (scores[rows, :] - stats[head : head + 1, at]) * EXP2_SCALING
            soft[rows, at] = jnp.exp2(below - stats[HEADS + head : HEADS + head + 1, at]).astype(BF)

    for_blocks(across // BLOCK, block)


def masked(inside, row):
    return jnp.where(inside, row, jnp.zeros_like(row))


def conv_term(place, row, kernel, tap):
    return side(mm(row[...], place.beside(kernel, tap)), CONV, 1)


def back_term(row, second_t, tap):
    return side(mm(row[...], second_t[tap]), CONV, -1)


def cotangent_terms_kernel(far_cot, pair_cot, second_t, near_back, own_back, mate_back):
    place = Place()
    own = pair_cot[0]
    near_back[...] = back_term(far_cot, second_t, 2) + back_term(own, second_t, 0)
    own_back[...] = back_term(own, second_t, 1)
    mate1 = masked(place.mate_inside, pair_cot[1])
    mate_back[...] = back_term(own, second_t, 2) + back_term(mate1, second_t, 0)


def attended_terms_kernel(own, mate, first_kernel, near_pre, own_pre, mate_pre):
    place = Place()
    near_pre[...] = conv_term(place, own, first_kernel, 2)
    own_pre[...] = conv_term(place, own, first_kernel, 1) + conv_term(place, mate, first_kernel, 2)
    mate_pre[...] = conv_term(place, own, first_kernel, 0) + conv_term(place, mate, first_kernel, 1)


def store_middle(pre, back, out):
    sigma = 1.0 / (1.0 + jnp.exp(-pre))
    out[:, :CONV] = (pre * sigma).astype(BF)
    out[:, CONV:] = (back * (sigma * (1.0 + pre * (1.0 - sigma)))).astype(BF)


def near_terms_kernel(far_term, near_pre, near_terms):
    near_terms[...] = near_pre[...] + far_term[...].astype(F32)


def mate_middle_kernel(
    mate1, mate_cot, mate_pre, mate_back, own_back, first_kernel, second_t, mate_mid, own_terms
):
    place = Place()
    own_terms[...] = own_back[...] + back_term(mate_cot[0], second_t, 0)
    pre = mate_pre[...] + conv_term(place, masked(place.mate_inside, mate1[...]), first_kernel, 2)
    store_middle(pre, mate_back[...] + back_term(mate_cot[0], second_t, 1), mate_mid)


def conv_grads_kernel(near, own, mate, mate1, pair_cot, mate_cot, own_mid, mate_mid, keep, send):
    place = Place()
    slots = (masked(place.near_inside, near[...]), own[...], mate[...], masked(place.mate_inside, mate1[...]))
    cots = (
        masked(place.near_inside, mate_cot[1]),
        pair_cot[0],
        mate_cot[0],
        masked(place.mate_inside, pair_cot[1]),
    )
    mids = {1: own_mid, 2: mate_mid}

    def store(total, start, step, a):
        for b in range(3):
            at = pl.ds(pl.multiple_of(start + (place.taps[a] * 3 + b) * step, step), step)
            keep[at, :] = total[:step, b * CONV : (b + 1) * CONV]
            send[at, :] = total[step:, b * CONV : (b + 1) * CONV]

    pick = place.chosen(VAL, place.core)
    attended_t = [mm_t(pick, slot).astype(BF) for slot in slots]
    slope = {slot: spread(mid[:, CONV:].astype(F32)) for slot, mid in mids.items()}
    for a in range(3):
        total = sum(mm(attended_t[slot + a - 1], slope[slot]) for slot in mids).astype(BF)
        store(total, 0, VAL // PARTS, a)
    pick = place.chosen(CONV, place.core)
    hidden_t = {slot: mm_t(pick, mid[:, :CONV]).astype(BF) for slot, mid in mids.items()}
    cotangent = [spread(cot.astype(F32)) for cot in cots]
    for a in range(3):
        total = sum(mm(hidden_t[slot], cotangent[slot + 1 - a]) for slot in mids).astype(BF)
        store(total, FIRST_ROWS, CONV // PARTS, a)


def backward_kernel(
    near,
    mate_cot,
    mate_mid,
    near_pre,
    near_back,
    own_pre,
    own_back,
    values,
    soft,
    keys_t,
    queries_t,
    attended_t,
    features_t,
    first_kernel,
    first_t,
    second_t,
    near_mid,
    own_mid,
    grad_out,
    proj_own,
    proj_mate,
    upstream_ref,
    grad_t,
):
    place = Place()
    across = near.shape[0]
    near = masked(place.near_inside, near[...])
    mids = (near_mid, own_mid, mate_mid)
    pre = near_pre[...] + conv_term(place, near, first_kernel, 1)
    near_cot = masked(place.near_inside, mate_cot[1])
    back = near_back[...] + back_term(near_cot, second_t, 1)
    store_middle(masked(place.near_inside, pre), masked(place.near_inside, back), near_mid)
    pre = own_pre[...] + conv_term(place, near, first_kernel, 0)
    store_middle(pre, own_back[...] + back_term(near_cot, second_t, 2), own_mid)
    slopes_beside = jnp.concatenate([mids[2 - a][:, CONV:] for a in range(3)], axis=1)
    upstream_ref[...] = side(mm(slopes_beside, first_t[...]), VAL, -1).astype(BF)
    blocks = across // BLOCK
    if blocks > 1:
        grad_t[...] = jnp.zeros_like(grad_t)

    def add_rows(start, count, terms):
        if blocks > 1:
            grad_t[start : start + count, :] += terms
        else:
            grad_t[start : start + count, :] = terms

    def block(index):
        at = block_at(index)
        upstream = upstream_ref[at, :]
        upstream_t = mm_t(identity(VAL), upstream)
        products = upstream_t * attended_t[:, at].astype(F32)
        upstream_t = upstream_t.astype(BF)
        slopes = mm_t(values[...], upstream)
        for head in range(HEADS):
            rows = slice(head * across, (head + 1) * across)
            qk_rows = slice(head * HEAD_QK, (head + 1) * HEAD_QK)
            val_rows = slice(head * HEAD_VAL, (head + 1) * HEAD_VAL)
            weights = soft[rows, at]
            inner = jnp.sum(products[val_rows, :], axis=0, keepdims=True)
            dscore = (weights.astype(F32) * (slopes[rows, :] - inner)).astype(BF)
            grad_t[qk_rows, at] = SCALING * mm(keys_t[qk_rows, :], dscore)
            add_rows(QK + head * HEAD_QK, HEAD_QK, SCALING * mm_t(queries_t[qk_rows, at], dscore))
            add_rows(2 * QK + head * HEAD_VAL, HEAD_VAL, mm_t(upstream_t[val_rows, :], weights))

    for_blocks(blocks, block)

    grad = grad_t[...].astype(BF)
    grad_out[...] = grad
    step = VAL // PARTS
    total = mm_t(features_t[...], grad).astype(BF)
    for which, target in enumerate((proj_own, proj_mate)):
        for j in range(PACKED // CONV):
            for part in range(2):
                begin = (2 * which + part) * step
                target[part, j * step : (j + 1) * step, :] = total[begin : begin + step, j * CONV : (j + 1) * CONV]


def outputs_kernel(near_mid, own_mid, mate_mid, grad, projection, second_kernel, output_map, input_grad, rows):
    place = Place()
    part_width = output_map.shape[0]
    mids = (near_mid, own_mid, mate_mid)
    rows[...] = side(sum(mm(mids[a][:, :CONV], place.beside(second_kernel, a)) for a in range(3)), CONV, 1)
    output_map[...] = rows[pl.ds(pl.multiple_of(place.col * part_width, part_width), part_width), :].astype(BF)
    own_pixels = one_hot((part_width, rows.shape[0]), lambda pixels: pixels + place.col * part_width)
    input_grad[...] = mm_t(mm_t(own_pixels, grad[...]).astype(BF), projection[...]).astype(BF)


def unpack_kernel(factor, core_flip, *refs):
    pieces = refs[:4]
    outs = refs[-7:-4]
    blocks = refs[-4:-1]
    sem = refs[-1]
    projection_block, first_block, second_block = blocks
    row = lax.axis_index("rows")
    half = lax.rem(row + core_flip, 2)
    chip_bit = lax.rem(row // 2, 2)
    col_bit = lax.rem(lax.axis_index("cols"), 2)
    parts = [2 * lax.rem(col_bit + which // 2, 2) + lax.rem(chip_bit + which % 2, 2) for which in range(4)]
    copies = []

    def send(index, block, out):
        copies.append(pltpu.make_async_copy(block, out, sem.at[index]))
        copies[-1].start()

    def rows_of(which, step):
        return pl.ds(pl.multiple_of(parts[which] * step, step), step)

    def half_of(rows):
        return pl.ds(pl.multiple_of(half * rows, rows), rows)

    step = VAL // PARTS
    for a in range(3):
        for which, piece in enumerate(pieces):
            for b in range(3):
                begin = (3 * a + b) * step
                first_block[a, b, rows_of(which, step), :] = piece[begin : begin + step, :].astype(F32) * factor
        send(a, first_block.at[a], outs[1].at[a, :, half_of(VAL // 2), :])
    for which, piece in enumerate(pieces):
        for j in range(PACKED // CONV):
            begin = FIRST_ROWS + SECOND_ROWS + j * step
            projection_block[rows_of(which, step), j * CONV : (j + 1) * CONV] = (
                piece[begin : begin + step, :].astype(F32) * factor
            )
    send(3, projection_block, outs[0].at[half_of(VAL // 2), :])
    step = CONV // PARTS
    for a in range(3):
        for which, piece in enumerate(pieces):
            for b in range(3):
                begin = FIRST_ROWS + (3 * a + b) * step
                second_block[a, b, rows_of(which, step), :] = piece[begin : begin + step, :].astype(F32) * factor
        send(4 + a, second_block.at[a], outs[2].at[a, :, half_of(CONV // 2), :])
    for copy in copies:
        copy.wait()


def unpack(factor, core_flip, pieces, into, **params):
    dims = ((2 * QK, PACKED), (3, 3, VAL, CONV), (3, 3, CONV, CONV))
    return pl.pallas_call(
        functools.partial(unpack_kernel, factor, core_flip),
        out_shape=tuple(shape(*size, dtype=F32) for size in dims),
        in_specs=[VMEM] * 4 + [HBM] * len(into),
        out_specs=[HBM] * 3,
        scratch_shapes=[pltpu.VMEM(size[:-2] + (size[-2] // 2, size[-1]), F32) for size in dims]
        + [pltpu.SemaphoreType.DMA((7,))],
        input_output_aliases={4 + i: i for i in range(len(into))},
        cost_estimate=pl.CostEstimate(flops=10**9, bytes_accessed=4 * 1024 * 1024, transcendentals=0),
        name="unpack_sums",
        **params,
    )(*pieces, *into)


def shape(*dims, dtype=BF):
    return jax.ShapeDtypeStruct(dims, dtype)


def granted(across):
    return dict(compiler_params=pltpu.CompilerParams(vmem_limit_bytes=across * 64 * 1024))


VMEM = pl.BlockSpec(memory_space=pltpu.VMEM)
HBM = pl.BlockSpec(memory_space=pltpu.HBM)


def body(features, projection, first_kernel, second_kernel, cotangent):
    height, part_width, channels = features.shape
    rows_size = lax.axis_size("rows")
    cols_size = lax.axis_size("cols")
    across = part_width * cols_size

    def rows_flip(values, bit):
        return lax.ppermute(values, "rows", [(i, i ^ bit) for i in range(rows_size)])

    def cols_flip(values):
        return lax.ppermute(values, "cols", [(i, i ^ 1) for i in range(cols_size)])

    def wide(values):
        return values.astype(F32)

    def added(one, two):
        return (one + two).astype(BF)

    def call(kernel, out_shape, operands, scratch=(), name=None, flops=10**9):
        return pl.pallas_call(
            kernel,
            out_shape=out_shape,
            in_specs=[VMEM] * len(operands),
            out_specs=[VMEM] * len(out_shape),
            scratch_shapes=scratch,
            cost_estimate=pl.CostEstimate(flops=flops, bytes_accessed=flops // 250, transcendentals=0),
            name=name,
            **granted(across),
        )(*operands)

    features, cotangent = (features[0], cotangent[0])
    last = rows_size - 1
    out = [(i, i + 2) for i in range(0, last - 1, 2)] + [(i, i - 2) for i in range(3, rows_size, 2)]
    out += [(last - 1, last), (1, 0)]
    back = [(j, i) for i, j in out]
    if cols_size == 2:
        swapped = cols_flip(features)
        out_cot = lax.ppermute(cotangent, "rows", out)
        back_cot = lax.ppermute(cotangent, "rows", back)
        (projection,) = fetch((projection,))
        features = (features, swapped)
    else:
        out_cot = lax.ppermute(cotangent, "rows", out)
        back_cot = lax.ppermute(cotangent, "rows", back)
        features = (lax.all_gather(features, "cols", axis=0, tiled=True),)
    own, local, stats = call(
        functools.partial(forward_kernel, len(features)),
        (shape(across, VAL), shape(across, PACKED + channels), shape(2 * HEADS, across, dtype=F32)),
        (*features, projection),
        (pltpu.VMEM((VAL, across), BF),),
        name="attention_forward",
    )
    term, bundle = call(
        rows_kernel,
        (shape(across, CONV), shape(3, part_width, CONV)),
        (own, first_kernel, out_cot, cotangent, back_cot),
        name="rows",
    )
    first_kernel, second_kernel = fetch((first_kernel, second_kernel), (stats,), 10**4)
    first_t, second_t = call(
        turn_kernel,
        (shape(3 * CONV, 3 * VAL), shape(3, CONV, 3 * CONV)),
        (first_kernel, second_kernel),
        name="turn",
        flops=10**6,
    )
    mate1 = lax.ppermute(own, "rows", back)
    if cols_size == 2:
        bundles = (bundle, cols_flip(bundle))
    else:
        bundles = (lax.all_gather(bundle, "cols", axis=1, tiled=True),)
    far = lax.ppermute(term, "rows", out)
    mate = rows_flip(own, 1)
    terms = (shape(across, CONV, dtype=F32),) * 3
    near_pre, own_pre, mate_pre = call(
        attended_terms_kernel, terms, (own, mate, first_kernel), name="attended_terms", flops=10**6
    )
    bundles, near_pre = lax.optimization_barrier((bundles, near_pre))
    far_cot, pair_cot = call(
        functools.partial(assemble_kernel, len(bundles)),
        (shape(across, CONV), shape(2, across, CONV)),
        bundles,
        name="assemble",
        flops=10**6,
    )
    mate_cot = rows_flip(pair_cot, 1)
    near = rows_flip(mate1, 1)
    soft, keys_t, queries_t, attended_t, features_t, values = call(
        prepare_kernel,
        (
            shape(HEADS * across, across),
            shape(QK, across),
            shape(QK, across),
            shape(VAL, across),
            shape(VAL // 2, across),
            shape(HEADS * across, VAL),
        ),
        (own, local, stats),
        name="prepare",
        flops=10**6,
    )
    near_back, own_back, mate_back = call(
        cotangent_terms_kernel, terms, (far_cot, pair_cot, second_t), name="cotangent_terms", flops=10**6
    )
    (near_pre,) = call(near_terms_kernel, terms[:1], (far, near_pre), name="near_terms", flops=4 * 10**9)
    mate_mid, own_back = call(
        mate_middle_kernel,
        (shape(across, 2 * CONV), terms[0]),
        (mate1, mate_cot, mate_pre, mate_back, own_back, first_kernel, second_t),
        name="mate_middle",
    )
    near_mid, own_mid, grad, proj_own, proj_mate = call(
        backward_kernel,
        (
            shape(across, 2 * CONV),
            shape(across, 2 * CONV),
            shape(PACKED, across),
            shape(2, PROJ_ROWS, CONV),
            shape(2, PROJ_ROWS, CONV),
        ),
        (
            near,
            mate_cot,
            mate_mid,
            near_pre,
            near_back,
            own_pre,
            own_back,
            values,
            soft,
            keys_t,
            queries_t,
            attended_t,
            features_t,
            first_kernel,
            first_t,
            second_t,
        ),
        (pltpu.VMEM((across, VAL), BF), pltpu.VMEM((PACKED, across), F32)),
        name="block_backward",
    )
    keep, send = call(
        conv_grads_kernel,
        (shape(FIRST_ROWS + SECOND_ROWS, CONV),) * 2,
        (near, own, mate, mate1, pair_cot, mate_cot, own_mid, mate_mid),
        name="conv_grads",
    )
    output_map, input_grad = call(
        outputs_kernel,
        (shape(part_width, CONV), shape(part_width, channels)),
        (near_mid, own_mid, mate_mid, grad, projection, second_kernel),
        (pltpu.VMEM((across, CONV), F32),),
        name="outputs",
    )
    proj_sum = added(wide(proj_own), wide(rows_flip(proj_mate, 1)))
    sent = jnp.concatenate([send, proj_sum[1]], axis=0)
    kept = jnp.concatenate([keep, proj_sum[0]], axis=0)
    if rows_size > 4:
        total = added(wide(kept) + wide(rows_flip(kept, 4)), wide(rows_flip(sent, 2)) + wide(rows_flip(sent, 6)))
    else:
        total = added(wide(kept), wide(rows_flip(sent, 2)))
    bit = 8
    while bit < rows_size:
        total = added(wide(total), wide(rows_flip(total, bit)))
        bit *= 2
    total, output_map, input_grad = lax.optimization_barrier((total, output_map, input_grad))
    chip = rows_flip(total, 2)
    side = cols_flip(total)
    corner = lax.ppermute(
        total,
        ("rows", "cols"),
        [(i * cols_size + j, (i ^ 2) * cols_size + (j ^ 1)) for i in range(rows_size) for j in range(cols_size)],
    )
    four = (total, chip, side, corner)
    factor = 1.0 / math.sqrt(height * across * rows_size)
    halves = unpack(factor, 0, four, (), **granted(across))
    projection_grad, first_grad, second_grad = unpack(
        factor, 1, [rows_flip(piece, 1) for piece in four], halves, **granted(across)
    )
    return (output_map[None], input_grad[None], projection_grad, first_grad, second_grad)


def solution(mesh):
    placed = (P("rows", "cols", None), P(), P(), P(), P("rows", "cols", None))
    return jax.shard_map(
        body,
        mesh=mesh,
        in_specs=placed,
        out_specs=(P("rows", "cols", None), P("rows", "cols", None), P(), P(), P()),
        check_vma=False,
    )
```
